32 devices in a mesh: dp: 8 (over z, x), section: 4 (over y, core).
Axes of the slice: x: 2, y: 2, z: 4, core: 2. Of those that a mesh axis runs over, the one named last changes fastest.
Arguments:
- memory: float32 [512, 32, 512], P(('dp', 'section')), may hold values from -6 to 6
- enc_lengths: int32 [512, 2], P(('dp', 'section')), may hold values from 1 to 24, 32 in all within a row
- frame_segment: int32 [512, 8], P(('dp', 'section')), may hold values from 0 to 1, never falling along the last dimension, each value on 1 to 6 neighbouring positions
- mel_target: float32 [512, 8, 80], P(('dp', 'section')), may hold values from -6 to 6
- prenet_keep: int32 [512, 8, 2, 256], P(('dp', 'section')), may hold values 0 or 1
- zone_keep: int32 [512, 8, 4, 1024], P(('dp', 'section')), may hold values 0 or 1
- pre_first: float32 [80, 256], replicated, may hold values from -0.625 to 0.625
- pre_second: float32 [256, 256], replicated, may hold values from -0.375 to 0.375
- att_weight: float32 [1792, 4096], P(None, ('dp', 'section')), may hold values from -0.125 to 0.125
- att_bias: float32 [4096], replicated, may hold values from -3 to 3
- query_weight: float32 [1024, 128], replicated, may hold values from -0.1875 to 0.1875
- memory_weight: float32 [512, 128], replicated, may hold values from -0.25 to 0.25
- loc_filters: float32 [32, 2, 31], replicated, may hold values from -3 to 3
- loc_dense: float32 [32, 128], replicated, may hold values from -1 to 1
- energy_v: float32 [128], replicated, may hold values from -1 to 1
- dec_weight: float32 [2560, 4096], P(None, ('dp', 'section')), may hold values from -0.125 to 0.125
- dec_bias: float32 [4096], replicated, may hold values from -3 to 3
- proj_weight: float32 [1536, 80], replicated, may hold values from -0.15625 to 0.15625
- proj_bias: float32 [80], replicated, may hold values from -3 to 3
- stop_weight: float32 [1536], replicated, may hold values from -0.15625 to 0.15625
- post_first: float32 [5, 80, 512], replicated, may hold values from -0.3125 to 0.3125
- post_mid: float32 [3, 5, 512, 512], P(None, None, None, 'section'), may hold values from -0.125 to 0.125
- post_last: float32 [5, 512, 80], replicated, may hold values from -0.125 to 0.125
- norm_gain: float32 [4, 512], replicated, may hold values from 0.5 to 1.5
- norm_shift: float32 [4, 512], replicated, may hold values from -2 to 2
- last_gain: float32 [80], replicated, may hold values from 0.5 to 1.5
- last_shift: float32 [80], replicated, may hold values from -2 to 2
- grad_after: float32 [512, 8, 80], P(('dp', 'section')), may hold values from -6 to 6
- grad_stop: float32 [512, 8], P(('dp', 'section')), may hold values from -6 to 6
Outputs:
- mel_after: float32 [512, 8, 80], P(('dp', 'section'))
- stop_logit: float32 [512, 8], P(('dp', 'section'))
- grad_memory: float32 [512, 32, 512], P(('dp', 'section'))
- g_pre_first: float32 [80, 256], replicated
- g_pre_second: float32 [256, 256], replicated
- g_att_weight: float32 [1792, 4096], P(None, ('dp', 'section'))
- g_att_bias: float32 [4096], replicated
- g_query_weight: float32 [1024, 128], replicated
- g_memory_weight: float32 [512, 128], replicated
- g_loc_filters: float32 [32, 2, 31], replicated
- g_loc_dense: float32 [32, 128], replicated
- g_energy_v: float32 [128], replicated
- g_dec_weight: float32 [2560, 4096], P(None, ('dp', 'section'))
- g_dec_bias: float32 [4096], replicated
- g_proj_weight: float32 [1536, 80], replicated
- g_proj_bias: float32 [80], replicated
- g_stop_weight: float32 [1536], replicated
- g_post_first: float32 [5, 80, 512], replicated
- g_post_mid: float32 [3, 5, 512, 512], P(None, None, None, 'section')
- g_post_last: float32 [5, 512, 80], replicated
- g_norm_gain: float32 [4, 512], replicated
- g_norm_shift: float32 [4, 512], replicated
- g_last_gain: float32 [80], replicated
- g_last_shift: float32 [80], replicated
The draws below stay inside these ranges and needn't reach their ends.
Inputs may be any that keep to these rules, and one draw needn't show every extreme that they name: `enc_lengths`: the two lengths of a row add up to 32. `frame_segment`: never falls along a row; both utterances occur in every row, each with at most 6 frames. `zone_keep`: 1 keeps the previous state.
All inputs are finite; a program needn't handle non-finite values. No bound on the sum of `prenet_keep` or of `zone_keep` on one device may be relied on, other than what follows from the above.
Results may differ from the reference program's by a relative error of at most 0.0003.
Values sent between devices are 32-bit elements; how exact they have to be, the bound alone decides.
No kernel may reach another device: no remote copies, remote signals or barrier semaphores. Data moves between devices by JAX's collectives and lax.ppermute only.
A program may use at most 448 MiB of HBM per device.

```python
import math
import jax
import jax.numpy as jnp
import numpy as np
from jax import lax

MEL = 80
PRENET = 256
RNN = 1024
ENC_DIM = 512
ATT = 128
LOC_FILT = 32
LOC_K = 31
POST = 512
POST_K = 5
FRAMES = 8
ENC = 32
ROWS = 512


def with_ends(array, rng, least, top_value):
    place = [jax.random.randint(jax.random.fold_in(rng, axis), (), 0, length) for axis, length in enumerate(array.shape)]
    longest = array.shape.index(max(array.shape))
    neighbour = place[:longest] + [(place[longest] + 1) % array.shape[longest]] + place[longest + 1:]
    return array.at[tuple(place)].set(least).at[tuple(neighbour)].set(top_value)


def steps_of(key, extent, shards, low, high):
    def one(dim, parts):
        heights = jax.random.uniform(jax.random.fold_in(jax.random.fold_in(key, 6), dim), (parts,), jnp.float32, low / len(shards), high / len(shards))
        return jnp.repeat(jnp.exp(heights), extent[dim] // parts).reshape((-1,) + (1,) * (len(extent) - dim - 1))

    gain = one(*shards[0])
    for cut in shards[1:]:
        gain = gain * one(*cut)
    return gain


def length_profile(amount, total, bound, lean):
    weights = [(1 << 20) // math.isqrt(rank ** lean) + 1 for rank in range(2, amount + 1)]
    surplus, counts = total - bound - (amount - 1), [1] * (amount - 1)
    while surplus > 0:
        movable = [i for i in range(amount - 1) if counts[i] < bound]
        mass, left = sum([weights[i] for i in movable]), surplus
        for i in movable:
            extra = min(bound - counts[i], max(1, left * weights[i] // mass), surplus)
            counts[i] = counts[i] + extra
            surplus = surplus - extra
    return np.array([bound] + counts)


def ragged_sizes(stream_key, count, total, reach, lean):
    if count == 2:
        one = jax.random.randint(stream_key, (), max(1, total - reach), min(reach, total - 1) + 1)
        return jnp.stack([one, total - one])
    sizes = jnp.asarray(length_profile(count, total, reach, lean), jnp.int32)
    pairs = (count - 1) // 2
    source_of, receiver = sizes[1:1 + 2 * pairs:2], sizes[2:2 + 2 * pairs:2]
    room = jnp.minimum(source_of - 1, reach - receiver)
    passed = jax.random.randint(jax.random.fold_in(stream_key, 1), (pairs,), 0, 1 << 20) % (room + 1)
    sizes = sizes.at[1:1 + 2 * pairs:2].set(source_of - passed).at[2:2 + 2 * pairs:2].set(receiver + passed)
    return sizes[jax.random.permutation(jax.random.fold_in(stream_key, 2), count)]


def noise(stream_key, extent, deviation, bound, cuts=(), kind=jnp.bfloat16):
    array = deviation * jax.random.normal(stream_key, extent, jnp.float32)
    if cuts:
        array = array * steps_of(stream_key, extent, cuts, -0.22, 0.18)
    return jnp.clip(array, -bound, bound).astype(kind)


def setup_inputs(seed: int = 0) -> dict:
    key_of = jax.random.split(jax.random.key(seed), 30)
    memory = noise(key_of[0], (ROWS, ENC, ENC_DIM), 1.0, 6.0, ((0, 32),), jnp.float32)
    enc_lengths = jax.vmap(lambda own: ragged_sizes(own, 2, ENC, ENC * 3 // 4, 0))(jax.random.split(key_of[1], ROWS)).reshape((ROWS, 2)).astype(jnp.int32)
    frame_segment = jax.vmap(lambda own: jnp.searchsorted(jnp.cumsum(ragged_sizes(own, 2, FRAMES, FRAMES - 2, 0)), jnp.arange(FRAMES), side="right"))(jax.random.split(key_of[2], ROWS)).reshape((ROWS, FRAMES)).astype(jnp.int32)
    mel_target = noise(key_of[3], (ROWS, FRAMES, MEL), 1.0, 6.0, ((0, 32),), jnp.float32)
    prenet_keep = with_ends((jax.random.randint(key_of[4], (ROWS, FRAMES, 2, PRENET), 0, 2) < 1).astype(jnp.int32), jax.random.fold_in(key_of[4], 1), 0, 1)
    zone_keep = with_ends((jax.random.randint(key_of[5], (ROWS, FRAMES, 4, RNN), 0, 10) < 1).astype(jnp.int32), jax.random.fold_in(key_of[5], 1), 0, 1)
    pre_first = noise(key_of[6], (MEL, PRENET), MEL ** -0.5, 0.625, (), jnp.float32)
    pre_second = noise(key_of[7], (PRENET, PRENET), PRENET ** -0.5, 0.375, (), jnp.float32)
    att_weight = noise(key_of[8], (PRENET + ENC_DIM + RNN, 4 * RNN), (PRENET + ENC_DIM + RNN) ** -0.5, 0.125, ((1, 32),), jnp.float32)
    att_bias = noise(key_of[9], (4 * RNN,), 0.5, 3.0, (), jnp.float32)
    query_weight = noise(key_of[10], (RNN, ATT), RNN ** -0.5, 0.1875, (), jnp.float32)
    memory_weight = noise(key_of[11], (ENC_DIM, ATT), ENC_DIM ** -0.5, 0.25, (), jnp.float32)
    loc_filters = noise(key_of[12], (LOC_FILT, 2, LOC_K), 4 ** -0.5, 3.0, (), jnp.float32)
    loc_dense = noise(key_of[13], (LOC_FILT, ATT), LOC_FILT ** -0.5, 1.0, (), jnp.float32)
    energy_v = noise(key_of[14], (ATT,), 32 ** -0.5, 1.0, (), jnp.float32)
    dec_weight = noise(key_of[15], (2 * RNN + ENC_DIM, 4 * RNN), (2 * RNN + ENC_DIM) ** -0.5, 0.125, ((1, 32),), jnp.float32)
    dec_bias = noise(key_of[16], (4 * RNN,), 0.5, 3.0, (), jnp.float32)
    proj_weight = noise(key_of[17], (RNN + ENC_DIM, MEL), (RNN + ENC_DIM) ** -0.5, 0.15625, (), jnp.float32)
    proj_bias = noise(key_of[18], (MEL,), 0.5, 3.0, (), jnp.float32)
    stop_weight = noise(key_of[19], (RNN + ENC_DIM,), (RNN + ENC_DIM) ** -0.5, 0.15625, (), jnp.float32)
    post_first = noise(key_of[20], (POST_K, MEL, POST), (POST_K * MEL) ** -0.5, 0.3125, (), jnp.float32)
    post_mid = noise(key_of[21], (3, POST_K, POST, POST), (POST_K * POST) ** -0.5, 0.125, ((3, 4),), jnp.float32)
    post_last = noise(key_of[22], (POST_K, POST, MEL), (POST_K * POST) ** -0.5, 0.125, (), jnp.float32)
    norm_gain = jnp.clip(1.0 + 0.1 * jax.random.normal(key_of[23], (4, POST), jnp.float32), 0.5, 1.5)
    norm_shift = noise(key_of[24], (4, POST), 0.3, 2.0, (), jnp.float32)
    last_gain = jnp.clip(1.0 + 0.1 * jax.random.normal(key_of[25], (MEL,), jnp.float32), 0.5, 1.5)
    last_shift = noise(key_of[26], (MEL,), 0.3, 2.0, (), jnp.float32)
    grad_after = noise(key_of[27], (ROWS, FRAMES, MEL), 1.0, 6.0, ((0, 32),), jnp.float32)
    grad_stop = noise(key_of[28], (ROWS, FRAMES), 1.0, 6.0, ((0, 32),), jnp.float32)
    return {"memory": memory, "enc_lengths": enc_lengths, "frame_segment": frame_segment, "mel_target": mel_target, "prenet_keep": prenet_keep, "zone_keep": zone_keep, "pre_first": pre_first, "pre_second": pre_second, "att_weight": att_weight, "att_bias": att_bias, "query_weight": query_weight, "memory_weight": memory_weight, "loc_filters": loc_filters, "loc_dense": loc_dense, "energy_v": energy_v, "dec_weight": dec_weight, "dec_bias": dec_bias, "proj_weight": proj_weight, "proj_bias": proj_bias, "stop_weight": stop_weight, "post_first": post_first, "post_mid": post_mid, "post_last": post_last, "norm_gain": norm_gain, "norm_shift": norm_shift, "last_gain": last_gain, "last_shift": last_shift, "grad_after": grad_after, "grad_stop": grad_stop}


highest = lax.Precision.HIGHEST
norm_eps = 1e-05

@jax.custom_vjp
def low(v):
    return lax.optimization_barrier(v.astype(jnp.bfloat16)).astype(jnp.float32)

@jax.custom_vjp
def low_back(v):
    return v

def low_keep(v):
    return (low(v), None)

def low_pass(kept, grad):
    return (grad,)

def back_keep(v):
    return (v, None)

def back_low(kept, grad):
    return (low(grad),)
low.defvjp(low_keep, low_pass)
low_back.defvjp(back_keep, back_low)

def matmul(left, right):
    return jnp.matmul(left, right, precision=highest)

def segment_starts(frame_segment):
    earlier = jnp.concatenate([frame_segment[:, :1] - 1, frame_segment[:, :-1]], axis=1)
    return (frame_segment != earlier).astype(jnp.float32)

def teacher_frames(mel_target, starts):
    shifted = jnp.concatenate([jnp.zeros_like(mel_target[:, :1]), mel_target[:, :-1]], axis=1)
    return shifted * (1.0 - starts)[:, :, None]

def encoder_segment(enc_lengths, positions):
    places = jnp.arange(positions, dtype=jnp.int32)
    return (places[None, :] >= enc_lengths[:, :1]).astype(jnp.int32)

def tap_mask(frame_segment, kernel):
    margin = kernel // 2
    frames = frame_segment.shape[1]
    padded = jnp.pad(frame_segment, ((0, 0), (margin, margin)), constant_values=-1)
    stacked = jnp.stack([padded[:, offset:offset + frames] == frame_segment for offset in range(kernel)], axis=2)
    return stacked.astype(jnp.float32)

def lstm_update(gate_sums, cell_state, hidden_state, zone_hidden, zone_cell):
    unit_count = cell_state.shape[-1]
    input_gate = jax.nn.sigmoid(gate_sums[:, :unit_count])
    forget = jax.nn.sigmoid(gate_sums[:, unit_count:2 * unit_count])
    update = jnp.tanh(gate_sums[:, 2 * unit_count:3 * unit_count])
    output_gate = jax.nn.sigmoid(gate_sums[:, 3 * unit_count:])
    new_cell = forget * cell_state + input_gate * update
    new_hidden = output_gate * jnp.tanh(new_cell)
    hidden_state = zone_hidden * hidden_state + (1.0 - zone_hidden) * new_hidden
    cell_state = zone_cell * cell_state + (1.0 - zone_cell) * new_cell
    return (hidden_state, cell_state)

def location_terms(attention_pair, loc_filters, loc_dense):
    kernel = loc_filters.shape[-1]
    positions = attention_pair.shape[-1]
    padded = jnp.pad(attention_pair, ((0, 0), (0, 0), (kernel // 2, kernel // 2)))
    windows = jnp.stack([padded[:, :, offset:offset + positions] for offset in range(kernel)], axis=2)
    filtered = jnp.einsum('rcke,fck->ref', windows, loc_filters, precision=highest)
    return jnp.einsum('ref,fa->rea', filtered, loc_dense, precision=highest)

def decode_rows(params, memory, encoder_ids, frame_segment, starts, frames_in, prenet_keep, zone_keep):
    pre_first, pre_second, att_weight, att_bias, query_weight, memory_weight, loc_filters, loc_dense, energy_v, dec_weight, dec_bias, proj_weight, proj_bias, stop_weight = params
    prenet_width = pre_first.shape[1]
    unit_count = dec_weight.shape[1] // 4
    row_count = memory.shape[0]
    positions = memory.shape[1]
    context_width = memory.shape[2]
    drop_scale = prenet_keep.astype(jnp.float32) * 2.0
    prenet_out = jax.nn.gelu(matmul(frames_in, pre_first)) * drop_scale[:, :, 0]
    prenet_out = jax.nn.gelu(matmul(prenet_out, pre_second)) * drop_scale[:, :, 1]
    att_input = matmul(prenet_out, att_weight[:prenet_width]) + att_bias
    att_rest = att_weight[prenet_width:]
    processed = matmul(memory, memory_weight)
    zone_float = zone_keep.astype(jnp.float32)

    def advance(state_in, inputs):
        att_hidden, att_cell, dec_hidden, dec_cell, context, weights_now, weights_sum = state_in
        step_input, step_start, step_segment, step_zone = inputs
        resume = (1.0 - step_start)[:, None]
        att_hidden = att_hidden * resume
        att_cell = att_cell * resume
        dec_hidden = dec_hidden * resume
        dec_cell = dec_cell * resume
        context = context * resume
        weights_now = weights_now * resume
        weights_sum = weights_sum * resume
        gate_sums = step_input + matmul(jnp.concatenate([context, att_hidden], axis=1), att_rest)
        att_hidden, att_cell = lstm_update(gate_sums, att_cell, att_hidden, step_zone[:, 0], step_zone[:, 1])
        query_vec = matmul(att_hidden, query_weight)
        located = location_terms(jnp.stack([weights_now, weights_sum], axis=1), loc_filters, loc_dense)
        energy = matmul(jnp.tanh(query_vec[:, None, :] + processed + located), energy_v)
        allowed = encoder_ids == step_segment[:, None]
        masked = jnp.where(allowed, energy, -1000000000.0)
        shifted = masked - lax.optimization_barrier(jnp.max(masked, axis=1, keepdims=True))
        exponent = jnp.exp(shifted)
        weights_now = exponent / lax.optimization_barrier(jnp.sum(exponent, axis=1, keepdims=True))
        weights_sum = weights_sum + weights_now
        context = jnp.einsum('re,rec->rc', weights_now, memory, precision=highest)
        gate_sums = matmul(jnp.concatenate([att_hidden, context, dec_hidden], axis=1), dec_weight) + dec_bias
        dec_hidden, dec_cell = lstm_update(gate_sums, dec_cell, dec_hidden, step_zone[:, 2], step_zone[:, 3])
        state_out = (att_hidden, att_cell, dec_hidden, dec_cell, context, weights_now, weights_sum)
        return (state_out, jnp.concatenate([dec_hidden, context], axis=1))
    hidden_zero = jnp.zeros((row_count, unit_count), jnp.float32)
    initial = (hidden_zero, hidden_zero, hidden_zero, hidden_zero, jnp.zeros((row_count, context_width), jnp.float32), jnp.zeros((row_count, positions), jnp.float32), jnp.zeros((row_count, positions), jnp.float32))
    inputs = (jnp.swapaxes(att_input, 0, 1), jnp.swapaxes(starts, 0, 1), jnp.swapaxes(frame_segment, 0, 1), jnp.swapaxes(zone_float, 0, 1))
    final_state, outputs = lax.scan(advance, initial, inputs)
    outputs = jnp.swapaxes(outputs, 0, 1)
    mel_before = matmul(outputs, proj_weight) + proj_bias
    stop_logit = matmul(outputs, stop_weight)
    return (mel_before, stop_logit)

def shift_taps(values, same_segment):
    kernel = same_segment.shape[2]
    margin = kernel // 2
    frames = values.shape[1]
    padded = jnp.pad(values, ((0, 0), (margin, margin), (0, 0)))
    tapped = jnp.stack([padded[:, offset:offset + frames] for offset in range(kernel)], axis=2)
    return tapped * same_segment[:, :, :, None]

def conv_piece(values, weight, same_segment):
    tapped = shift_taps(values, same_segment)
    return jnp.einsum('rfkc,kco->rfo', tapped, weight, precision=highest)

def postnet(mel_before, same_segment, post_params):
    post_first, post_mid, post_last, norm_gain, norm_shift, last_gain, last_shift = post_params
    weights_list = [post_first, post_mid[0], post_mid[1], post_mid[2], post_last]
    gains = [norm_gain[0], norm_gain[1], norm_gain[2], norm_gain[3], last_gain]
    shifts = [norm_shift[0], norm_shift[1], norm_shift[2], norm_shift[3], last_shift]
    layer_in = mel_before
    for layer_index in range(5):
        conv_out = conv_piece(layer_in, weights_list[layer_index], same_segment)
        average = lax.optimization_barrier(jnp.mean(conv_out, axis=(0, 1)))
        spread = lax.optimization_barrier(jnp.mean(conv_out * conv_out, axis=(0, 1))) - average * average
        scaled = (conv_out - average) * lax.rsqrt(spread + norm_eps)
        normed = scaled * gains[layer_index] + shifts[layer_index]
        layer_in = jnp.tanh(normed) if layer_index < 4 else normed
    return mel_before + layer_in

def reference(memory, enc_lengths, frame_segment, mel_target, prenet_keep, zone_keep, pre_first, pre_second, att_weight, att_bias, query_weight, memory_weight, loc_filters, loc_dense, energy_v, dec_weight, dec_bias, proj_weight, proj_bias, stop_weight, post_first, post_mid, post_last, norm_gain, norm_shift, last_gain, last_shift, grad_after, grad_stop):
    starts = segment_starts(frame_segment)
    frames_in = teacher_frames(mel_target, starts)
    encoder_ids = encoder_segment(enc_lengths, memory.shape[1])
    same_segment = tap_mask(frame_segment, post_first.shape[0])
    decoder_params = (pre_first, pre_second, att_weight, att_bias, query_weight, memory_weight, loc_filters, loc_dense, energy_v, dec_weight, dec_bias, proj_weight, proj_bias, stop_weight)
    post_params = (post_first, post_mid, post_last, norm_gain, norm_shift, last_gain, last_shift)
    total_rows = memory.shape[0]
    group_size = math.gcd(total_rows, 512)
    group_count = total_rows // group_size

    def regroup(tensor):
        return tensor.reshape((group_count, group_size) + tensor.shape[1:])

    def forward(memory_rows, dec_params, net_params):

        def decode_group(pieces):
            return decode_rows(dec_params, *pieces)
        one_group = jax.checkpoint(decode_group)
        pieces = tuple((regroup(tensor) for tensor in (memory_rows, encoder_ids, frame_segment, starts, frames_in, prenet_keep, zone_keep)))
        mel_groups, stop_groups = lax.map(one_group, pieces)
        mel_before = mel_groups.reshape((total_rows,) + mel_groups.shape[2:])
        stop_logit = stop_groups.reshape((total_rows,) + stop_groups.shape[2:])
        return (postnet(mel_before, same_segment, net_params), stop_logit)
    (mel_after, stop_logit), pullback = jax.vjp(forward, memory, decoder_params, post_params)
    grad_memory, dec_grads, post_grads = pullback((grad_after, grad_stop))
    return (mel_after, stop_logit, grad_memory, dec_grads[0], dec_grads[1], dec_grads[2], dec_grads[3], dec_grads[4], dec_grads[5], dec_grads[6], dec_grads[7], dec_grads[8], dec_grads[9], dec_grads[10], dec_grads[11], dec_grads[12], dec_grads[13], post_grads[0], post_grads[1], post_grads[2], post_grads[3], post_grads[4], post_grads[5], post_grads[6])
```

```python
import functools

import jax
import jax.numpy as jnp
from jax import lax
from jax.experimental import pallas as pl
from jax.experimental.pallas import tpu as pltpu
from jax.sharding import PartitionSpec as P

high = lax.Precision.HIGH
norm_eps = 1e-05
f32 = jnp.float32
bf16 = jnp.bfloat16
both = ("dp", "section")
lanes = 128
vmem_limit = 62 * 1024 * 1024

span = 6
shard_block = 4


def split(values):
    upper = values.astype(bf16)
    lower = (values - upper.astype(f32)).astype(bf16)
    return upper, lower


def product(left, upper, lower, transposed=False):
    rows = left.shape[0]
    left_upper, left_lower = split(left)
    stacked = jnp.concatenate([left_upper, left_lower], axis=0)
    dims = (((1,), (1,)), ((), ())) if transposed else (((1,), (0,)), ((), ()))
    first = lax.dot_general(stacked, upper, dims, preferred_element_type=f32)
    second = lax.dot_general(left_upper, lower, dims, preferred_element_type=f32)
    return first[:rows] + first[rows:] + second


def sigmoid(values):
    return 0.5 * jnp.tanh(0.5 * values) + 0.5


def lane_index(shape):
    return lax.broadcasted_iota(jnp.int32, shape, 1)


def fold_lanes(values, positions):
    copies = values
    shift = positions
    while shift < lanes:
        copies = copies + pltpu.roll(copies, shift, 1)
        shift *= 2
    return copies


def diagonal_mask(rows, positions):
    shape = (2 * rows, rows * positions)
    row = lax.broadcasted_iota(jnp.int32, shape, 0)
    group = lax.broadcasted_iota(jnp.int32, shape, 1) // positions
    return group == jnp.where(row >= rows, row - rows, row)


def spread(weights, rows, positions):
    copies = fold_lanes(weights, positions)
    wide = jnp.concatenate([copies] * (rows * positions // lanes), axis=1)
    return jnp.where(diagonal_mask(rows, positions), wide, 0.0)


def collect(wide, rows, positions):
    kept = jnp.where(diagonal_mask(rows, positions), wide, 0.0)
    total = kept[:, :lanes]
    for start in range(lanes, rows * positions, lanes):
        total = total + kept[:, start : start + lanes]
    shift = positions
    while shift < lanes:
        total = total + pltpu.roll(total, shift, 1)
        shift *= 2
    return jnp.where(lane_index(total.shape) < positions, total, 0.0)


def store_parts(block_ref, first, last, upper_ref, lower_ref, index):
    for place in range(shard_block):
        upper, lower = split(block_ref[place, first:last, :])
        upper_ref[index, :, place * lanes : (place + 1) * lanes] = upper
        lower_ref[index, :, place * lanes : (place + 1) * lanes] = lower


def gate_forward(gate_sums, cell, hidden, zone_hidden, zone_cell):
    units = cell.shape[1]
    gate_in = sigmoid(gate_sums[:, :units])
    gate_keep = sigmoid(gate_sums[:, units : 2 * units])
    update = jnp.tanh(gate_sums[:, 2 * units : 3 * units])
    gate_out = sigmoid(gate_sums[:, 3 * units :])
    new_cell = gate_keep * cell + gate_in * update
    new_hidden = gate_out * jnp.tanh(new_cell)
    hidden = zone_hidden * hidden + (1.0 - zone_hidden) * new_hidden
    cell = zone_cell * cell + (1.0 - zone_cell) * new_cell
    return hidden, cell, (gate_in, gate_keep, update, gate_out)


def gate_backward(gates, cell, zone_hidden, zone_cell, grad_hidden, grad_cell):
    units = cell.shape[1]
    gate_in = gates[:, :units]
    gate_keep = gates[:, units : 2 * units]
    update = gates[:, 2 * units : 3 * units]
    gate_out = gates[:, 3 * units :]
    bent = jnp.tanh(gate_keep * cell + gate_in * update)
    grad_new = (1.0 - zone_hidden) * grad_hidden
    grad_new_cell = grad_new * gate_out * (1.0 - bent * bent) + (1.0 - zone_cell) * grad_cell
    grad_sums = (
        grad_new_cell * update * gate_in * (1.0 - gate_in),
        grad_new_cell * cell * gate_keep * (1.0 - gate_keep),
        grad_new_cell * gate_in * (1.0 - update * update),
        grad_new * bent * gate_out * (1.0 - gate_out),
    )
    return grad_sums, zone_hidden * grad_hidden, zone_cell * grad_cell + grad_new_cell * gate_keep


def zone_masks(early_ref, late_ref):
    masks = []
    for which in range(2):
        pair = jnp.concatenate([early_ref[0, which], late_ref[0, which]], axis=0)
        masks.append(pair.astype(f32))
    return masks


def attention_forward_kernel(
    blocks,
    rows,
    positions,
    lag,
    weight_ref,
    prenet_ref,
    bias_ref,
    loc_map_ref,
    processed_ref,
    memory_ref,
    query_ref,
    energy_ref,
    zone_early_ref,
    zone_late_ref,
    resume_ref,
    allowed_ref,
    hidden_out,
    cell_out,
    context_out,
    gates_out,
    bent_out,
    weights_out,
    window_out,
    upper,
    lower,
    inputs,
    loc_upper,
    loc_lower,
    memory_upper,
    memory_lower,
    query_upper,
    query_lower,
    sums,
    hidden,
    cell,
    context,
    window,
):
    step = pl.program_id(0)
    prenet_width = prenet_ref.shape[1]
    context_width = context.shape[1]
    units = hidden.shape[1]
    width = shard_block * lanes

    @pl.when(step == 0)
    def prepare():
        loc_upper[...], loc_lower[...] = split(loc_map_ref[...])
        memory_upper[...], memory_lower[...] = split(memory_ref[...])
        query_upper[...], query_lower[...] = split(query_ref[...])
        hidden[...] = jnp.zeros_like(hidden)
        cell[...] = jnp.zeros_like(cell)
        context[...] = jnp.zeros_like(context)
        window[...] = jnp.zeros_like(window)

    @pl.when(step < blocks)
    def load():
        store_parts(weight_ref, prenet_width, weight_ref.shape[1], upper, lower, step)
        first = jnp.concatenate([weight_ref[place, :prenet_width, :] for place in range(shard_block)], axis=1)
        first_upper, first_lower = split(first)
        inputs[step] = product(prenet_ref[...], first_upper, first_lower) + bias_ref[0]

    @pl.when(step >= blocks)
    def advance():
        frame = step - blocks
        resume = resume_ref[0]
        hidden_now = hidden[...] * resume
        cell_now = cell[...] * resume
        context_now = context[...] * resume
        window_now = window[...] * resume
        early = pl.multiple_of(frame * rows, rows)
        late = pl.multiple_of((frame + lag) * rows, rows)
        for block in range(blocks):
            taken = slice(block * width, (block + 1) * width)
            sums[:rows, taken] = inputs[block, pl.ds(early, rows), :]
            sums[rows:, taken] = inputs[block, pl.ds(late, rows), :]

        @pl.when(frame > 0)
        def recur():
            state = jnp.concatenate([context_now, hidden_now], axis=1)
            for block in range(blocks):
                taken = slice(block * width, (block + 1) * width)
                sums[:, taken] += product(state, upper[block], lower[block])

        zone_hidden, zone_cell = zone_masks(zone_early_ref, zone_late_ref)
        hidden_new, cell_new, gates = gate_forward(sums[...], cell_now, hidden_now, zone_hidden, zone_cell)
        for place, gate in enumerate(gates):
            gates_out[0, :, place * units : (place + 1) * units] = gate
        hidden[...] = hidden_new
        cell[...] = cell_new
        hidden_out[0] = hidden_new
        cell_out[0] = cell_new
        query = product(hidden_new, query_upper[...], query_lower[...])
        located = product(window_now, loc_upper[...], loc_lower[...])
        energy_v = energy_ref[...]
        lane = lane_index((2 * rows, lanes))
        energy = jnp.zeros((2 * rows, lanes), f32)
        for place in range(positions):
            taken = slice(place * lanes, (place + 1) * lanes)
            ready = processed_ref[:, taken]
            bent = jnp.tanh(query + jnp.concatenate([ready, ready], axis=0) + located[:, taken])
            bent_out[0, :, taken] = bent
            energy = jnp.where(lane == place, jnp.sum(bent * energy_v, axis=1, keepdims=True), energy)
        masked = jnp.where(allowed_ref[...] > 0.5, energy, -1000000000.0)
        exponent = jnp.exp(masked - jnp.max(masked, axis=1, keepdims=True))
        weights = exponent / jnp.sum(exponent, axis=1, keepdims=True)
        weights = jnp.where(lane < positions, weights, 0.0)
        weights_out[0] = weights
        window_out[0] = window_now
        second = (lane >= positions) & (lane < 2 * positions)
        window[...] = weights + pltpu.roll(weights, positions, 1) + jnp.where(second, window_now, 0.0)
        context_new = product(spread(weights, rows, positions), memory_upper[...], memory_lower[...])
        context[...] = context_new
        context_out[0] = context_new


def decoder_forward_kernel(
    blocks,
    rows,
    lag,
    weight_in_ref,
    weight_own_ref,
    frames_ref,
    bias_ref,
    zone_early_ref,
    zone_late_ref,
    resume_ref,
    hidden_out,
    cell_out,
    gates_out,
    upper,
    lower,
    inputs,
    sums,
    hidden,
    cell,
):
    step = pl.program_id(0)
    units = hidden.shape[1]
    width = shard_block * lanes

    @pl.when(step == 0)
    def prepare():
        hidden[...] = jnp.zeros_like(hidden)
        cell[...] = jnp.zeros_like(cell)

    @pl.when(step < blocks)
    def load():
        store_parts(weight_own_ref, 0, weight_own_ref.shape[1], upper, lower, step)
        first = jnp.concatenate([weight_in_ref[place] for place in range(shard_block)], axis=1)
        first_upper, first_lower = split(first)
        inputs[step] = product(frames_ref[...], first_upper, first_lower) + bias_ref[0]

    @pl.when(step >= blocks)
    def advance():
        frame = step - blocks
        resume = resume_ref[0]
        hidden_now = hidden[...] * resume
        cell_now = cell[...] * resume
        early = pl.multiple_of(frame * rows, rows)
        late = pl.multiple_of((frame + lag) * rows, rows)
        for block in range(blocks):
            taken = slice(block * width, (block + 1) * width)
            sums[:rows, taken] = inputs[block, pl.ds(early, rows), :]
            sums[rows:, taken] = inputs[block, pl.ds(late, rows), :]

        @pl.when(frame > 0)
        def recur():
            for block in range(blocks):
                taken = slice(block * width, (block + 1) * width)
                sums[:, taken] += product(hidden_now, upper[block], lower[block])

        zone_hidden, zone_cell = zone_masks(zone_early_ref, zone_late_ref)
        hidden_new, cell_new, gates = gate_forward(sums[...], cell_now, hidden_now, zone_hidden, zone_cell)
        for place, gate in enumerate(gates):
            gates_out[0, :, place * units : (place + 1) * units] = gate
        hidden[...] = hidden_new
        cell[...] = cell_new
        hidden_out[0] = hidden_new
        cell_out[0] = cell_new


def add_frames(total_ref, grads, frame, rows, lag):
    early = pl.multiple_of(frame * rows, rows)
    late = pl.multiple_of((frame + lag) * rows, rows)
    total_ref[pl.ds(early, rows), :] += grads[:rows]
    total_ref[pl.ds(late, rows), :] += grads[rows:]


def decoder_backward_kernel(
    blocks,
    rows,
    lag,
    weight_own_ref,
    weight_in_ref,
    grad_ref,
    gates_ref,
    cell_ref,
    zone_early_ref,
    zone_late_ref,
    resume_ref,
    valid_ref,
    grad_sums_out,
    grad_in_out,
    upper,
    lower,
    frame_sums,
    grad_hidden,
    grad_cell,
):
    step = pl.program_id(0)
    units = grad_hidden.shape[1]
    width = shard_block * lanes

    @pl.when(step == 0)
    def prepare():
        grad_hidden[...] = jnp.zeros_like(grad_hidden)
        grad_cell[...] = jnp.zeros_like(grad_cell)
        frame_sums[...] = jnp.zeros_like(frame_sums)
        grad_in_out[...] = jnp.zeros_like(grad_in_out)

    @pl.when(step < blocks)
    def load():
        store_parts(weight_own_ref, 0, weight_own_ref.shape[1], upper, lower, step)

    @pl.when((step >= blocks) & (step < blocks + span))
    def retreat():
        frame = span - 1 - (step - blocks)
        resume = resume_ref[0]
        early = pl.multiple_of(frame * rows, rows)
        late = pl.multiple_of((frame + lag) * rows, rows)
        arriving = jnp.concatenate([grad_ref[pl.ds(early, rows), :], grad_ref[pl.ds(late, rows), :]], axis=0)
        total = grad_hidden[...] + arriving * valid_ref[0]
        cell_now = cell_ref[0] * jnp.where(frame > 0, resume, 0.0)
        zone_hidden, zone_cell = zone_masks(zone_early_ref, zone_late_ref)
        grad_sums, passed_hidden, passed_cell = gate_backward(
            gates_ref[0], cell_now, zone_hidden, zone_cell, total, grad_cell[...]
        )
        grad_cell[...] = passed_cell * resume
        grad_hidden[...] = passed_hidden
        for place, grads in enumerate(grad_sums):
            for part in range(units // width):
                block = place * (units // width) + part
                add_frames(frame_sums.at[block], grads[:, part * width : (part + 1) * width], frame, rows, lag)

        @pl.when(frame > 0)
        def recur():
            carried = grad_hidden[...]
            for place, grads in enumerate(grad_sums):
                for part in range(units // width):
                    block = place * (units // width) + part
                    taken = grads[:, part * width : (part + 1) * width]
                    carried = carried + product(taken, upper[block], lower[block], transposed=True)
            grad_hidden[...] = carried * resume

    @pl.when(step >= blocks + span)
    def pass_on():
        block = step - blocks - span
        grads = frame_sums[block]
        for place in range(shard_block):
            grad_sums_out[place] = grads[:, place * lanes : (place + 1) * lanes]
        first = jnp.concatenate([weight_in_ref[place] for place in range(shard_block)], axis=1)
        first_upper, first_lower = split(first)
        grad_in_out[...] += product(grads, first_upper, first_lower, transposed=True)


def attention_backward_kernel(
    blocks,
    rows,
    positions,
    lag,
    weight_ref,
    grad_hidden_ref,
    grad_context_ref,
    gates_ref,
    cell_ref,
    bent_ref,
    weights_ref,
    window_ref,
    loc_map_ref,
    memory_ref,
    query_ref,
    energy_ref,
    zone_early_ref,
    zone_late_ref,
    resume_ref,
    valid_ref,
    next_resume_ref,
    grad_sums_out,
    grad_bias_out,
    grad_prenet_out,
    grad_query_out,
    grad_processed_out,
    grad_memory_out,
    grad_loc_out,
    grad_energy_out,
    upper,
    lower,
    first_upper,
    first_lower,
    frame_sums,
    loc_upper,
    loc_lower,
    memory_upper,
    memory_lower,
    query_upper,
    query_lower,
    grad_bent,
    grad_contexts,
    diagonals,
    windows,
    grad_hidden,
    grad_cell,
    grad_context,
    grad_window,
):
    step = pl.program_id(0)
    units = grad_hidden.shape[1]
    context_width = grad_context.shape[1]
    prenet_width = first_upper.shape[1]
    width = shard_block * lanes
    pair = 2 * rows

    @pl.when(step == 0)
    def prepare():
        loc_upper[...], loc_lower[...] = split(loc_map_ref[...])
        memory_upper[...], memory_lower[...] = split(memory_ref[...])
        query_upper[...], query_lower[...] = split(query_ref[...])
        grad_hidden[...] = jnp.zeros_like(grad_hidden)
        grad_cell[...] = jnp.zeros_like(grad_cell)
        grad_context[...] = jnp.zeros_like(grad_context)
        grad_window[...] = jnp.zeros_like(grad_window)
        frame_sums[...] = jnp.zeros_like(frame_sums)
        grad_query_out[...] = jnp.zeros_like(grad_query_out)
        grad_processed_out[...] = jnp.zeros_like(grad_processed_out)
        grad_energy_out[...] = jnp.zeros_like(grad_energy_out)

    @pl.when(step < blocks)
    def load():
        store_parts(weight_ref, prenet_width, weight_ref.shape[1], upper, lower, step)
        store_parts(weight_ref, 0, prenet_width, first_upper, first_lower, step)

    @pl.when(step >= blocks)
    def retreat():
        frame = span - 1 - (step - blocks)
        resume = resume_ref[0]
        valid = valid_ref[0]
        early = pl.multiple_of(frame * rows, rows)
        late = pl.multiple_of((frame + lag) * rows, rows)
        here = pl.multiple_of(frame * pair, pair)
        lane = lane_index((pair, lanes))
        arriving = jnp.concatenate(
            [grad_context_ref[pl.ds(early, rows), :], grad_context_ref[pl.ds(late, rows), :]], axis=0
        )
        context_total = grad_context[...] + arriving * valid
        grad_contexts[pl.ds(here, pair), :] = context_total
        weights = weights_ref[0]
        diagonals[pl.ds(here, pair), :] = spread(weights, rows, positions)
        windows[pl.ds(here, pair), :] = window_ref[0]
        window_grad = grad_window[...]
        wide = product(context_total, memory_upper[...], memory_lower[...], transposed=True)
        grad_weights = collect(wide, rows, positions) + jnp.where(
            lane < positions, window_grad + pltpu.roll(window_grad, lanes - positions, 1), 0.0
        )
        inner = jnp.sum(weights * grad_weights, axis=1, keepdims=True)
        grad_energy = weights * (grad_weights - inner)
        energy_v = energy_ref[...]
        energy_total = jnp.zeros((pair, lanes), f32)
        query_total = jnp.zeros((pair, lanes), f32)
        for place in range(positions):
            taken = slice(place * lanes, (place + 1) * lanes)
            bent = bent_ref[0, :, taken]
            column = jnp.sum(jnp.where(lane == place, grad_energy, 0.0), axis=1, keepdims=True)
            energy_total = energy_total + column * bent
            slope = column * energy_v * (1.0 - bent * bent)
            query_total = query_total + slope
            grad_bent[pl.ds(here, pair), taken] = slope
            grad_processed_out[:, taken] += slope[:rows] + slope[rows:]
        grad_energy_out[...] += energy_total
        add_frames(grad_query_out, query_total, frame, rows, lag)
        slopes = grad_bent[pl.ds(here, pair), :]
        moved = product(slopes, loc_upper[...], loc_lower[...], transposed=True)
        second = (lane >= positions) & (lane < 2 * positions)
        grad_window[...] = resume * (moved + jnp.where(second, window_grad, 0.0))

        arriving = jnp.concatenate(
            [grad_hidden_ref[pl.ds(early, rows), :], grad_hidden_ref[pl.ds(late, rows), :]], axis=0
        )
        total = grad_hidden[...] + arriving * valid
        total = total + product(query_total, query_upper[...], query_lower[...], transposed=True)
        cell_now = cell_ref[0] * jnp.where(frame > 0, resume, 0.0)
        zone_hidden, zone_cell = zone_masks(zone_early_ref, zone_late_ref)
        grad_sums, passed_hidden, passed_cell = gate_backward(
            gates_ref[0], cell_now, zone_hidden, zone_cell, total, grad_cell[...]
        )
        grad_cell[...] = passed_cell * resume
        for place, grads in enumerate(grad_sums):
            for part in range(units // width):
                block = place * (units // width) + part
                add_frames(frame_sums.at[block], grads[:, part * width : (part + 1) * width], frame, rows, lag)

        @pl.when(frame > 0)
        def recur():
            carried = jnp.zeros((pair, context_width + units), f32)
            for place, grads in enumerate(grad_sums):
                for part in range(units // width):
                    block = place * (units // width) + part
                    taken = grads[:, part * width : (part + 1) * width]
                    carried = carried + product(taken, upper[block], lower[block], transposed=True)
            grad_context[...] = carried[:, :context_width] * resume
            grad_hidden[...] = (carried[:, context_width:] + passed_hidden) * resume

    @pl.when(step == blocks + span - 1)
    def finish():
        prenet_grad = jnp.zeros(grad_prenet_out.shape, f32)
        frame_rows = frame_sums.shape[1]
        for block in range(blocks):
            grads = frame_sums[block]
            prenet_grad = prenet_grad + product(grads, first_upper[block], first_lower[block], transposed=True)
            grad_bias_out[:, block * width : (block + 1) * width] = jnp.sum(grads, axis=0, keepdims=True)
            later = jnp.concatenate([grads[rows:], jnp.zeros((rows, width), f32)], axis=0) * next_resume_ref[...]
            for place in range(shard_block):
                grad_sums_out[block * shard_block + place] = later[:, place * lanes : (place + 1) * lanes]
        grad_prenet_out[...] = prenet_grad
        context_upper, context_lower = split(grad_contexts[...])
        grad_memory_out[...] = product(diagonals[...].T, context_upper, context_lower)
        window_turned = windows[...].T
        for block in range(blocks):
            taken = slice(block * width, (block + 1) * width)
            bent_upper, bent_lower = split(grad_bent[:, taken])
            grad_loc_out[:, taken] = product(window_turned, bent_upper, bent_lower)


def whole_spec(array):
    rank = len(array.shape)
    return pl.BlockSpec(array.shape, lambda step: (0,) * rank)


def timed_spec(array, place, depth=None):
    shape = (1,) + tuple(array.shape[1:])
    rank = len(array.shape)
    return pl.BlockSpec(shape, lambda step: (place(step),) + (0,) * (rank - 1))


def shard_spec(array, place):
    shape = (shard_block,) + tuple(array.shape[1:])
    return pl.BlockSpec(shape, lambda step: (place(step), 0, 0))


def zone_spec(zone, place, which):
    shape = (1, 2) + tuple(zone.shape[2:])
    return pl.BlockSpec(shape, lambda step: (place(step), which, 0, 0))


def out_spec(shape):
    rank = len(shape)
    return pl.BlockSpec(shape, lambda step: (0,) * rank)


def params():
    return pltpu.CompilerParams(vmem_limit_bytes=vmem_limit, dimension_semantics=("arbitrary",))


def attention_forward(
    weight, prenet_out, bias, loc_map, processed, memory, query_weight, energy_v, zone, resume, allowed, lag
):
    groups, depth = weight.shape[:2]
    blocks = groups // shard_block
    rows = memory.shape[0] // (processed.shape[1] // lanes)
    positions = processed.shape[1] // lanes
    columns = groups * lanes
    units = columns // 4
    context_width = memory.shape[1]
    frame_rows = prenet_out.shape[0]
    rest = depth - prenet_out.shape[1]
    width = shard_block * lanes
    pair = 2 * rows

    def shard(step):
        return jnp.minimum(step, blocks - 1)

    def timed(step):
        return jnp.clip(step - blocks, 0, span - 1)

    def later(step):
        return timed(step) + lag

    timed_shapes = [
        (span, pair, units),
        (span, pair, units),
        (span, pair, context_width),
        (span, pair, columns),
        (span, pair, positions * lanes),
        (span, pair, lanes),
        (span, pair, lanes),
    ]
    out_shape = [jax.ShapeDtypeStruct(shape, f32) for shape in timed_shapes]
    bias_blocks = bias.reshape(blocks, 1, width)
    return pl.pallas_call(
        functools.partial(attention_forward_kernel, blocks, rows, positions, lag),
        grid=(blocks + span,),
        in_specs=[
            shard_spec(weight, shard),
            whole_spec(prenet_out),
            timed_spec(bias_blocks, shard),
            whole_spec(loc_map),
            whole_spec(processed),
            whole_spec(memory),
            whole_spec(query_weight),
            whole_spec(energy_v),
            zone_spec(zone, timed, 0),
            zone_spec(zone, later, 0),
            timed_spec(resume, timed),
            whole_spec(allowed),
        ],
        out_specs=[timed_spec(shape, timed) for shape in out_shape],
        out_shape=out_shape,
        scratch_shapes=[
            pltpu.VMEM((blocks, rest, width), bf16),
            pltpu.VMEM((blocks, rest, width), bf16),
            pltpu.VMEM((blocks, frame_rows, width), f32),
            pltpu.VMEM(loc_map.shape, bf16),
            pltpu.VMEM(loc_map.shape, bf16),
            pltpu.VMEM(memory.shape, bf16),
            pltpu.VMEM(memory.shape, bf16),
            pltpu.VMEM(query_weight.shape, bf16),
            pltpu.VMEM(query_weight.shape, bf16),
            pltpu.VMEM((pair, columns), f32),
            pltpu.VMEM((pair, units), f32),
            pltpu.VMEM((pair, units), f32),
            pltpu.VMEM((pair, context_width), f32),
            pltpu.VMEM((pair, lanes), f32),
        ],
        compiler_params=params(),
        name="attention_forward",
    )(weight, prenet_out, bias_blocks, loc_map, processed, memory, query_weight, energy_v, zone, zone, resume, allowed)


def decoder_forward(weight_in, weight_own, frames, bias, zone, resume, rows, lag):
    groups = weight_in.shape[0]
    blocks = groups // shard_block
    columns = groups * lanes
    units = columns // 4
    width = shard_block * lanes
    pair = 2 * rows

    def shard(step):
        return jnp.minimum(step, blocks - 1)

    def timed(step):
        return jnp.clip(step - blocks, 0, span - 1)

    def later(step):
        return timed(step) + lag

    timed_shapes = [(span, pair, units), (span, pair, units), (span, pair, columns)]
    out_shape = [jax.ShapeDtypeStruct(shape, f32) for shape in timed_shapes]
    bias_blocks = bias.reshape(blocks, 1, width)
    return pl.pallas_call(
        functools.partial(decoder_forward_kernel, blocks, rows, lag),
        grid=(blocks + span,),
        in_specs=[
            shard_spec(weight_in, shard),
            shard_spec(weight_own, shard),
            whole_spec(frames),
            timed_spec(bias_blocks, shard),
            zone_spec(zone, timed, 1),
            zone_spec(zone, later, 1),
            timed_spec(resume, timed),
        ],
        out_specs=[timed_spec(shape, timed) for shape in out_shape],
        out_shape=out_shape,
        scratch_shapes=[
            pltpu.VMEM((blocks, weight_own.shape[1], width), bf16),
            pltpu.VMEM((blocks, weight_own.shape[1], width), bf16),
            pltpu.VMEM((blocks, frames.shape[0], width), f32),
            pltpu.VMEM((pair, columns), f32),
            pltpu.VMEM((pair, units), f32),
            pltpu.VMEM((pair, units), f32),
        ],
        compiler_params=params(),
        name="decoder_forward",
    )(weight_in, weight_own, frames, bias_blocks, zone, zone, resume)


def decoder_backward(weight_own, weight_in, grad, gates, cells, zone, resume, valid, rows, lag):
    groups = weight_in.shape[0]
    blocks = groups // shard_block
    columns = groups * lanes
    units = columns // 4
    width = shard_block * lanes
    pair = 2 * rows
    frame_rows = grad.shape[0]

    def shard(step):
        return jnp.minimum(step, blocks - 1)

    def last_shard(step):
        return jnp.clip(step - blocks - span, 0, blocks - 1)

    def timed(step):
        return span - 1 - jnp.clip(step - blocks, 0, span - 1)

    def later(step):
        return timed(step) + lag

    def before(step):
        return jnp.maximum(timed(step) - 1, 0)

    out_shape = [
        jax.ShapeDtypeStruct((groups, frame_rows, lanes), f32),
        jax.ShapeDtypeStruct((frame_rows, weight_in.shape[1]), f32),
    ]
    return pl.pallas_call(
        functools.partial(decoder_backward_kernel, blocks, rows, lag),
        grid=(2 * blocks + span,),
        in_specs=[
            shard_spec(weight_own, shard),
            shard_spec(weight_in, last_shard),
            whole_spec(grad),
            timed_spec(gates, timed),
            timed_spec(cells, before),
            zone_spec(zone, timed, 1),
            zone_spec(zone, later, 1),
            timed_spec(resume, timed),
            timed_spec(valid, timed),
        ],
        out_specs=[shard_spec(out_shape[0], last_shard), whole_spec(out_shape[1])],
        out_shape=out_shape,
        scratch_shapes=[
            pltpu.VMEM((blocks, weight_own.shape[1], width), bf16),
            pltpu.VMEM((blocks, weight_own.shape[1], width), bf16),
            pltpu.VMEM((blocks, frame_rows, width), f32),
            pltpu.VMEM((pair, units), f32),
            pltpu.VMEM((pair, units), f32),
        ],
        compiler_params=params(),
        name="decoder_backward",
    )(weight_own, weight_in, grad, gates, cells, zone, zone, resume, valid)


def attention_backward(
    weight,
    grad_hidden,
    grad_context,
    gates,
    cells,
    bent,
    weights,
    window,
    loc_map,
    memory,
    query_weight,
    energy_v,
    zone,
    resume,
    valid,
    next_resume,
    rows,
    positions,
    prenet_width,
    lag,
):
    groups, depth = weight.shape[:2]
    blocks = groups // shard_block
    columns = groups * lanes
    units = columns // 4
    width = shard_block * lanes
    pair = 2 * rows
    frame_rows = grad_hidden.shape[0]
    context_width = grad_context.shape[1]
    rest = depth - prenet_width

    def shard(step):
        return jnp.minimum(step, blocks - 1)

    def timed(step):
        return span - 1 - jnp.clip(step - blocks, 0, span - 1)

    def later(step):
        return timed(step) + lag

    def before(step):
        return jnp.maximum(timed(step) - 1, 0)

    shapes = [
        (groups, frame_rows, lanes),
        (1, columns),
        (frame_rows, prenet_width),
        (frame_rows, lanes),
        (rows, positions * lanes),
        (rows * positions, context_width),
        loc_map.shape,
        (pair, lanes),
    ]
    return pl.pallas_call(
        functools.partial(attention_backward_kernel, blocks, rows, positions, lag),
        grid=(blocks + span,),
        in_specs=[
            shard_spec(weight, shard),
            whole_spec(grad_hidden),
            whole_spec(grad_context),
            timed_spec(gates, timed),
            timed_spec(cells, before),
            timed_spec(bent, timed),
            timed_spec(weights, timed),
            timed_spec(window, timed),
            whole_spec(loc_map),
            whole_spec(memory),
            whole_spec(query_weight),
            whole_spec(energy_v),
            zone_spec(zone, timed, 0),
            zone_spec(zone, later, 0),
            timed_spec(resume, timed),
            timed_spec(valid, timed),
            whole_spec(next_resume),
        ],
        out_specs=[out_spec(shape) for shape in shapes],
        out_shape=[jax.ShapeDtypeStruct(shape, f32) for shape in shapes],
        scratch_shapes=[
            pltpu.VMEM((blocks, rest, width), bf16),
            pltpu.VMEM((blocks, rest, width), bf16),
            pltpu.VMEM((blocks, prenet_width, width), bf16),
            pltpu.VMEM((blocks, prenet_width, width), bf16),
            pltpu.VMEM((blocks, frame_rows, width), f32),
            pltpu.VMEM(loc_map.shape, bf16),
            pltpu.VMEM(loc_map.shape, bf16),
            pltpu.VMEM(memory.shape, bf16),
            pltpu.VMEM(memory.shape, bf16),
            pltpu.VMEM(query_weight.shape, bf16),
            pltpu.VMEM(query_weight.shape, bf16),
            pltpu.VMEM((span * pair, positions * lanes), f32),
            pltpu.VMEM((span * pair, context_width), f32),
            pltpu.VMEM((span * pair, rows * positions), f32),
            pltpu.VMEM((span * pair, lanes), f32),
            pltpu.VMEM((pair, units), f32),
            pltpu.VMEM((pair, units), f32),
            pltpu.VMEM((pair, context_width), f32),
            pltpu.VMEM((pair, lanes), f32),
        ],
        compiler_params=params(),
        name="attention_backward",
    )(
        weight,
        grad_hidden,
        grad_context,
        gates,
        cells,
        bent,
        weights,
        window,
        loc_map,
        memory,
        query_weight,
        energy_v,
        zone,
        zone,
        resume,
        valid,
        next_resume,
    )


def dot(left, right, left_dim=1, right_dim=0):
    return lax.dot_general(
        left, right, (((left_dim,), (right_dim,)), ((), ())), precision=high, preferred_element_type=f32
    )


def gather_columns(shard):
    depth, width = shard.shape
    if width % lanes:
        full = lax.all_gather(shard, both, axis=1, tiled=True)
        return full.reshape(depth, -1, lanes).swapaxes(0, 1)
    stacked = lax.all_gather(shard, both, axis=0)
    if width == lanes:
        return stacked
    return stacked.reshape(-1, depth, width // lanes, lanes).swapaxes(1, 2).reshape(-1, depth, lanes)


def exchange_columns(grads, devices):
    groups, frames, width = grads.shape
    if groups == devices:
        pieces = grads
    else:
        flat = grads.swapaxes(0, 1).reshape(frames, devices, groups * width // devices)
        pieces = flat.swapaxes(0, 1)
    received = lax.all_to_all(pieces, both, 0, 0)
    return received.reshape(devices * frames, -1)


def gathers_inputs(frame_rows, columns, devices):
    return frame_rows * devices <= columns


def column_gradients(inputs, grads, devices):
    groups, frames, width = grads.shape
    if gathers_inputs(frames, groups * width, devices):
        received = exchange_columns(grads, devices)
        return [dot(piece, received, 0, 0) for piece in inputs]
    flat = grads.swapaxes(0, 1).reshape(frames, groups * width)
    return [lax.psum_scatter(dot(piece, flat, 0, 0), both, scatter_dimension=1, tiled=True) for piece in inputs]


def quick_sum(values, devices):
    copies = jnp.broadcast_to(values[None], (devices,) + values.shape)
    return jnp.sum(lax.all_to_all(copies, both, 0, 0), axis=0)


def gelu_slope(values):
    return jax.vjp(jax.nn.gelu, values)


def location_map(loc_filters, loc_dense, positions):
    filters, channels, taps = loc_filters.shape
    features = loc_dense.shape[1]
    joined = dot(loc_filters.reshape(filters, channels * taps), loc_dense, 0, 0)
    joined = joined.reshape(channels, taps, features)
    margin = taps // 2
    padded = jnp.pad(joined, ((0, 0), (positions, positions), (0, 0)))
    columns = [
        padded[:, positions + margin - place : 2 * positions + margin - place] for place in range(positions)
    ]
    spread_map = jnp.stack(columns, axis=2).reshape(channels * positions, positions * features)
    return jnp.pad(spread_map, ((0, lanes - channels * positions), (0, 0)))


def location_unmap(grad_map, channels, taps, positions, features):
    margin = taps // 2
    grads = grad_map[: channels * positions].reshape(channels, positions, positions, features)
    total = jnp.zeros((channels, 3 * positions, features), f32)
    for place in range(positions):
        start = positions + margin - place
        total = total.at[:, start : start + positions].add(grads[:, :, place])
    return total[:, positions : positions + taps]


def tapped_frames(values, same_segment):
    frames, rows, channels = values.shape
    kernel = same_segment.shape[2]
    margin = kernel // 2
    padded = jnp.pad(values, ((margin, margin), (0, 0), (0, 0)))
    taps = [
        padded[offset : offset + frames] * same_segment[:, :, offset][:, :, None] for offset in range(kernel)
    ]
    return jnp.concatenate(taps, axis=2).reshape(frames * rows, kernel * channels)


def untapped_frames(grads, same_segment):
    frames, rows, kernel = same_segment.shape
    margin = kernel // 2
    channels = grads.shape[1] // kernel
    grads = grads.reshape(frames, rows, kernel * channels)
    total = jnp.zeros((frames + 2 * margin, rows, channels), f32)
    for offset in range(kernel):
        piece = grads[:, :, offset * channels : (offset + 1) * channels] * same_segment[:, :, offset][:, :, None]
        total = total + jnp.pad(piece, ((offset, 2 * margin - offset), (0, 0), (0, 0)))
    return total[margin : margin + frames]


def per_device(
    memory,
    enc_lengths,
    frame_segment,
    mel_target,
    prenet_keep,
    zone_keep,
    pre_first,
    pre_second,
    att_weight,
    att_bias,
    query_weight,
    memory_weight,
    loc_filters,
    loc_dense,
    energy_v,
    dec_weight,
    dec_bias,
    proj_weight,
    proj_bias,
    stop_weight,
    post_first,
    post_mid,
    post_last,
    norm_gain,
    norm_shift,
    last_gain,
    last_shift,
    grad_after,
    grad_stop,
):
    devices = lax.axis_size("dp") * lax.axis_size("section")
    rows, positions, context_width = memory.shape
    frames = frame_segment.shape[1]
    mel = mel_target.shape[2]
    units = att_bias.shape[0] // 4
    prenet_width = pre_first.shape[1]
    features = memory_weight.shape[1]
    lag = frames - span
    frame_rows = frames * rows

    att_all = gather_columns(att_weight)
    split_row = dec_weight.shape[0] - units
    dec_in_all = gather_columns(dec_weight[:split_row])
    dec_own_all = gather_columns(dec_weight[split_row:])
    mid_all = [lax.all_gather(post_mid[layer], "section", axis=2, tiled=True) for layer in range(3)]

    segment = frame_segment.T
    earlier = jnp.concatenate([segment[:1] - 1, segment[:-1]], axis=0)
    resume = (segment == earlier).astype(f32)
    shifted = jnp.concatenate([jnp.zeros_like(mel_target[:, :1]), mel_target[:, :-1]], axis=1)
    frames_in = (shifted.swapaxes(0, 1) * resume[:, :, None]).reshape(frame_rows, mel)
    keep = prenet_keep.transpose(1, 2, 0, 3).astype(f32) * 2.0
    keep_first = keep[:, 0].reshape(frame_rows, prenet_width)
    keep_second = keep[:, 1].reshape(frame_rows, prenet_width)
    gelu_first, first_back = gelu_slope(dot(frames_in, pre_first))
    pre_hidden = gelu_first * keep_first
    gelu_second, second_back = gelu_slope(dot(pre_hidden, pre_second))
    prenet_out = gelu_second * keep_second
    memory_flat = memory.reshape(rows * positions, context_width)
    processed = dot(memory_flat, memory_weight)
    loc_map = location_map(loc_filters, loc_dense, positions)
    zone = zone_keep.transpose(1, 2, 0, 3)

    first_part = segment == 0
    steps = jnp.arange(span)
    never = jnp.ones((span, rows), f32)
    resume_pair = jnp.concatenate([never, resume[lag:]], axis=1)[:, :, None]
    valid_pair = jnp.concatenate([first_part[:span], ~first_part[lag:]], axis=1).astype(f32)[:, :, None]
    encoder_first = jnp.arange(lanes)[None, :] < enc_lengths[:, :1]
    inside = jnp.arange(lanes)[None, :] < positions
    allowed = jnp.concatenate([encoder_first, inside & ~encoder_first], axis=0).astype(f32)
    next_resume = jnp.concatenate([resume[1:], jnp.zeros((1, rows), f32)], axis=0).reshape(frame_rows, 1)

    def to_frames(pairs):
        early = jnp.pad(pairs[:, :rows], ((0, lag), (0, 0), (0, 0)))
        late = jnp.pad(pairs[:, rows:], ((lag, 0), (0, 0), (0, 0)))
        return jnp.where(first_part[:, :, None], early, late).reshape(frame_rows, -1)

    energy_row = energy_v.reshape(1, features)
    processed_wide = processed.reshape(rows, positions * features)
    hidden, cells, contexts, gates, bent, weights, window = attention_forward(
        att_all,
        prenet_out,
        att_bias,
        loc_map,
        processed_wide,
        memory_flat,
        query_weight,
        energy_row,
        zone,
        resume_pair,
        allowed,
        lag,
    )
    att_frames = to_frames(hidden)
    context_frames = to_frames(contexts)
    dec_inputs = jnp.concatenate([att_frames, context_frames], axis=1)
    dec_hidden, dec_cells, dec_gates = decoder_forward(
        dec_in_all, dec_own_all, dec_inputs, dec_bias, zone, resume_pair, rows, lag
    )
    dec_frames = to_frames(dec_hidden)

    prenet_later = jnp.concatenate([prenet_out[rows:], jnp.zeros((rows, prenet_width), f32)], axis=0)
    att_inputs_all = jnp.concatenate([prenet_later, context_frames, att_frames], axis=1)
    dec_earlier = jnp.concatenate([jnp.zeros((rows, units), f32), dec_frames[:-rows]], axis=0)
    dec_earlier = dec_earlier * resume.reshape(frame_rows, 1)
    dec_inputs_all = dec_earlier
    if gathers_inputs(frame_rows, 4 * units, devices):
        att_inputs_all = lax.all_gather(att_inputs_all, both, axis=0, tiled=True)
        dec_inputs_all = lax.all_gather(dec_inputs_all, both, axis=0, tiled=True)

    out_frames = jnp.concatenate([dec_frames, context_frames], axis=1)
    mel_before = dot(out_frames, proj_weight) + proj_bias
    stop_logit = jnp.sum(out_frames * stop_weight, axis=1).reshape(frames, rows).T

    kernel = post_first.shape[0]
    margin = kernel // 2
    padded = jnp.pad(segment, ((margin, margin), (0, 0)), constant_values=-1)
    same_segment = jnp.stack(
        [padded[offset : offset + frames] == segment for offset in range(kernel)], axis=2
    ).astype(f32)
    frame_count = frame_rows * devices
    post_weights = [post_first] + mid_all + [post_last]
    post_weights = [weight.reshape(-1, weight.shape[-1]) for weight in post_weights]
    gains = [norm_gain[0], norm_gain[1], norm_gain[2], norm_gain[3], last_gain]
    shifts = [norm_shift[0], norm_shift[1], norm_shift[2], norm_shift[3], last_shift]
    kept_layers = []
    layer_in = mel_before
    for layer in range(5):
        tapped = tapped_frames(layer_in.reshape(frames, rows, -1), same_segment)
        conv_out = dot(tapped, post_weights[layer])
        stat_sums = quick_sum(
            jnp.stack([jnp.sum(conv_out, axis=0), jnp.sum(conv_out * conv_out, axis=0)]), devices
        )
        average = stat_sums[0] / frame_count
        inverse = lax.rsqrt(stat_sums[1] / frame_count - average * average + norm_eps)
        scaled = (conv_out - average) * inverse
        normed = scaled * gains[layer] + shifts[layer]
        activated = jnp.tanh(normed) if layer < 4 else normed
        kept_layers.append((tapped, scaled, inverse, activated))
        layer_in = activated
    mel_after = mel_before + layer_in

    grad_after_frames = grad_after.swapaxes(0, 1).reshape(frame_rows, mel)
    upstream = grad_after_frames
    weight_grads = [None] * 5
    gain_grads = [None] * 5
    shift_grads = [None] * 5
    for layer in reversed(range(5)):
        tapped, scaled, inverse, activated = kept_layers[layer]
        grad_normed = upstream * (1.0 - activated * activated) if layer < 4 else upstream
        grad_sums = quick_sum(
            jnp.stack([jnp.sum(grad_normed, axis=0), jnp.sum(grad_normed * scaled, axis=0)]), devices
        )
        shift_grads[layer] = grad_sums[0]
        gain_grads[layer] = grad_sums[1]
        grad_conv = (
            inverse * gains[layer] * (grad_normed - (grad_sums[0] + scaled * grad_sums[1]) / frame_count)
        )
        weight_grads[layer] = dot(tapped, grad_conv, 0, 0)
        upstream = untapped_frames(dot(grad_conv, post_weights[layer], 1, 1), same_segment)
        upstream = upstream.reshape(frame_rows, -1)
    mid_grad = jnp.stack([weight_grads[layer].reshape(post_mid.shape[1:3] + (-1,)) for layer in (1, 2, 3)])
    mid_part = lax.psum_scatter(mid_grad, "section", scatter_dimension=3, tiled=True)
    mid_part = lax.psum(mid_part, "dp")

    grad_mel = grad_after_frames + upstream
    grad_stop_frames = grad_stop.T.reshape(frame_rows, 1)
    grad_out = dot(grad_mel, proj_weight, 1, 1) + grad_stop_frames * stop_weight
    g_proj_weight = dot(out_frames, grad_mel, 0, 0)
    g_proj_bias = jnp.sum(grad_mel, axis=0)
    g_stop_weight = jnp.sum(out_frames * grad_stop_frames, axis=0)
    early_sums = lax.psum(
        (g_proj_weight, g_proj_bias, g_stop_weight, weight_grads[0], weight_grads[4]), both
    )

    dec_sums, grad_dec_inputs = decoder_backward(
        dec_own_all,
        dec_in_all,
        grad_out[:, :units],
        dec_gates,
        dec_cells,
        zone,
        resume_pair,
        valid_pair,
        rows,
        lag,
    )
    g_dec_bias = jnp.sum(dec_sums, axis=1).reshape(-1)
    context_end = prenet_width + context_width
    dec_parts = column_gradients(
        [att_inputs_all[:, context_end:], att_inputs_all[:, prenet_width:context_end], dec_inputs_all],
        dec_sums,
        devices,
    )
    dec_part = jnp.concatenate(dec_parts, axis=0)
    grad_context = grad_out[:, units:] + grad_dec_inputs[:, units:]
    (
        att_sums,
        g_att_bias,
        grad_prenet,
        grad_query,
        grad_processed,
        grad_memory,
        grad_loc,
        grad_energy,
    ) = attention_backward(
        att_all,
        grad_dec_inputs[:, :units],
        grad_context,
        gates,
        cells,
        bent,
        weights,
        window,
        loc_map,
        memory_flat,
        query_weight,
        energy_row,
        zone,
        resume_pair,
        valid_pair,
        next_resume,
        rows,
        positions,
        prenet_width,
        lag,
    )
    (att_part,) = column_gradients([att_inputs_all], att_sums, devices)

    grad_processed = grad_processed.reshape(rows * positions, features)
    grad_memory = grad_memory + dot(grad_processed, memory_weight, 1, 1)
    g_memory_weight = dot(memory_flat, grad_processed, 0, 0)
    g_query_weight = dot(att_frames, grad_query, 0, 0)
    (grad_second,) = second_back(grad_prenet * keep_second)
    g_pre_second = dot(pre_hidden, grad_second, 0, 0)
    (grad_first,) = first_back(dot(grad_second, pre_second, 1, 1) * keep_first)
    g_pre_first = dot(frames_in, grad_first, 0, 0)
    filters, channels, taps = loc_filters.shape
    grad_joined = location_unmap(grad_loc, channels, taps, positions, features)
    late_sums = lax.psum(
        (
            g_pre_first,
            g_pre_second,
            g_att_bias,
            g_query_weight,
            g_memory_weight,
            grad_joined,
            jnp.sum(grad_energy, axis=0),
            g_dec_bias,
        ),
        both,
    )
    grad_joined = late_sums[5].reshape(channels * taps, features)
    g_loc_filters = dot(loc_dense, grad_joined, 1, 1).reshape(loc_filters.shape)
    g_loc_dense = dot(loc_filters.reshape(filters, channels * taps), grad_joined)

    return (
        mel_after.reshape(frames, rows, mel).swapaxes(0, 1),
        stop_logit,
        grad_memory.reshape(memory.shape),
        late_sums[0],
        late_sums[1],
        att_part,
        late_sums[2].reshape(-1),
        late_sums[3],
        late_sums[4],
        g_loc_filters,
        g_loc_dense,
        late_sums[6],
        dec_part,
        late_sums[7],
        early_sums[0],
        early_sums[1],
        early_sums[2],
        early_sums[3].reshape(post_first.shape),
        mid_part,
        early_sums[4].reshape(post_last.shape),
        jnp.stack(gain_grads[:4]),
        jnp.stack(shift_grads[:4]),
        gain_grads[4],
        shift_grads[4],
    )


def solution(mesh):
    rows_only = P(both)
    columns_only = P(None, both)
    mid_spec = P(None, None, None, "section")
    placed = (
        (rows_only,) * 6
        + (P(), P(), columns_only)
        + (P(),) * 6
        + (columns_only,)
        + (P(),) * 5
        + (mid_spec,)
        + (P(),) * 5
        + (rows_only, rows_only)
    )
    given = (
        (rows_only,) * 3
        + (P(), P(), columns_only)
        + (P(),) * 6
        + (columns_only,)
        + (P(),) * 5
        + (mid_spec,)
        + (P(),) * 5
    )
    return jax.shard_map(per_device, mesh=mesh, in_specs=placed, out_specs=given, check_vma=False)
```

```python
import functools
import math

import jax
import jax.numpy as jnp
from jax import lax
from jax.experimental import pallas as pl
from jax.experimental.pallas import tpu as pltpu
from jax.sharding import PartitionSpec as P

high = lax.Precision.HIGH
norm_eps = 1e-05
f32 = jnp.float32
bf16 = jnp.bfloat16
both = ("dp", "section")
lanes = 128
vmem_limit = 62 * 1024 * 1024

span = 6
shard_block = 4


def split(values):
    upper = values.astype(bf16)
    lower = (values - upper.astype(f32)).astype(bf16)
    return upper, lower


def product(left, upper, lower, transposed=False):
    rows = left.shape[0]
    left_upper, left_lower = split(left)
    stacked = jnp.concatenate([left_upper, left_lower], axis=0)
    dims = (((1,), (1,)), ((), ())) if transposed else (((1,), (0,)), ((), ()))
    first = lax.dot_general(stacked, upper, dims, preferred_element_type=f32)
    second = lax.dot_general(left_upper, lower, dims, preferred_element_type=f32)
    return first[:rows] + first[rows:] + second


def sigmoid(values):
    return 0.5 * jnp.tanh(0.5 * values) + 0.5


def lane_index(shape):
    return lax.broadcasted_iota(jnp.int32, shape, 1)


def fold_lanes(values, positions):
    copies = values
    shift = positions
    while shift < lanes:
        copies = copies + pltpu.roll(copies, shift, 1)
        shift *= 2
    return copies


def diagonal_mask(rows, positions):
    shape = (2 * rows, rows * positions)
    row = lax.broadcasted_iota(jnp.int32, shape, 0)
    group = lax.broadcasted_iota(jnp.int32, shape, 1) // positions
    return group == jnp.where(row >= rows, row - rows, row)


def spread(weights, rows, positions):
    copies = fold_lanes(weights, positions)
    wide = jnp.concatenate([copies] * (rows * positions // lanes), axis=1)
    return jnp.where(diagonal_mask(rows, positions), wide, 0.0)


def collect(wide, rows, positions):
    kept = jnp.where(diagonal_mask(rows, positions), wide, 0.0)
    total = kept[:, :lanes]
    for start in range(lanes, rows * positions, lanes):
        total = total + kept[:, start : start + lanes]
    shift = positions
    while shift < lanes:
        total = total + pltpu.roll(total, shift, 1)
        shift *= 2
    return jnp.where(lane_index(total.shape) < positions, total, 0.0)


def store_parts(block_ref, first, last, upper_ref, lower_ref, index):
    for place in range(shard_block):
        upper, lower = split(block_ref[place, first:last, :])
        upper_ref[index, :, place * lanes : (place + 1) * lanes] = upper
        lower_ref[index, :, place * lanes : (place + 1) * lanes] = lower


def gate_forward(gate_sums, cell, hidden, zone_hidden, zone_cell):
    units = cell.shape[1]
    gate_in = sigmoid(gate_sums[:, :units])
    gate_keep = sigmoid(gate_sums[:, units : 2 * units])
    update = jnp.tanh(gate_sums[:, 2 * units : 3 * units])
    gate_out = sigmoid(gate_sums[:, 3 * units :])
    new_cell = gate_keep * cell + gate_in * update
    new_hidden = gate_out * jnp.tanh(new_cell)
    hidden = zone_hidden * hidden + (1.0 - zone_hidden) * new_hidden
    cell = zone_cell * cell + (1.0 - zone_cell) * new_cell
    return hidden, cell, (gate_in, gate_keep, update, gate_out)


def gate_backward(gates, cell, zone_hidden, zone_cell, grad_hidden, grad_cell):
    units = cell.shape[1]
    gate_in = gates[:, :units]
    gate_keep = gates[:, units : 2 * units]
    update = gates[:, 2 * units : 3 * units]
    gate_out = gates[:, 3 * units :]
    bent = jnp.tanh(gate_keep * cell + gate_in * update)
    grad_new = (1.0 - zone_hidden) * grad_hidden
    grad_new_cell = grad_new * gate_out * (1.0 - bent * bent) + (1.0 - zone_cell) * grad_cell
    grad_sums = (
        grad_new_cell * update * gate_in * (1.0 - gate_in),
        grad_new_cell * cell * gate_keep * (1.0 - gate_keep),
        grad_new_cell * gate_in * (1.0 - update * update),
        grad_new * bent * gate_out * (1.0 - gate_out),
    )
    return grad_sums, zone_hidden * grad_hidden, zone_cell * grad_cell + grad_new_cell * gate_keep


def zone_masks(early_ref, late_ref):
    masks = []
    for which in range(2):
        pair = jnp.concatenate([early_ref[0, which], late_ref[0, which]], axis=0)
        masks.append(pair.astype(f32))
    return masks


def attention_forward_kernel(
    blocks,
    rows,
    positions,
    lag,
    weight_ref,
    prenet_ref,
    bias_ref,
    loc_map_ref,
    processed_ref,
    memory_ref,
    query_ref,
    energy_ref,
    zone_early_ref,
    zone_late_ref,
    resume_ref,
    allowed_ref,
    awaited,
    hidden_out,
    cell_out,
    context_out,
    gates_out,
    bent_out,
    weights_out,
    window_out,
    upper,
    lower,
    inputs,
    loc_upper,
    loc_lower,
    memory_upper,
    memory_lower,
    query_upper,
    query_lower,
    sums,
    hidden,
    cell,
    context,
    window,
):
    step = pl.program_id(0)
    prenet_width = prenet_ref.shape[1]
    context_width = context.shape[1]
    units = hidden.shape[1]
    width = shard_block * lanes

    @pl.when(step == 0)
    def prepare():
        loc_upper[...], loc_lower[...] = split(loc_map_ref[...])
        memory_upper[...], memory_lower[...] = split(memory_ref[...])
        query_upper[...], query_lower[...] = split(query_ref[...])
        hidden[...] = jnp.zeros_like(hidden)
        cell[...] = jnp.zeros_like(cell)
        context[...] = jnp.zeros_like(context)
        window[...] = jnp.zeros_like(window)

    @pl.when(step < blocks)
    def load():
        store_parts(weight_ref, prenet_width, weight_ref.shape[1], upper, lower, step)
        first = jnp.concatenate([weight_ref[place, :prenet_width, :] for place in range(shard_block)], axis=1)
        first_upper, first_lower = split(first)
        inputs[step] = product(prenet_ref[...], first_upper, first_lower) + bias_ref[0]

    @pl.when(step >= blocks)
    def advance():
        frame = step - blocks
        resume = resume_ref[0]
        hidden_now = hidden[...] * resume
        cell_now = cell[...] * resume
        context_now = context[...] * resume
        window_now = window[...] * resume
        early = pl.multiple_of(frame * rows, rows)
        late = pl.multiple_of((frame + lag) * rows, rows)
        for block in range(blocks):
            taken = slice(block * width, (block + 1) * width)
            sums[:rows, taken] = inputs[block, pl.ds(early, rows), :]
            sums[rows:, taken] = inputs[block, pl.ds(late, rows), :]

        @pl.when(frame > 0)
        def recur():
            state = jnp.concatenate([context_now, hidden_now], axis=1)
            for block in range(blocks):
                taken = slice(block * width, (block + 1) * width)
                sums[:, taken] += product(state, upper[block], lower[block])

        zone_hidden, zone_cell = zone_masks(zone_early_ref, zone_late_ref)
        hidden_new, cell_new, gates = gate_forward(sums[...], cell_now, hidden_now, zone_hidden, zone_cell)
        for place, gate in enumerate(gates):
            gates_out[0, :, place * units : (place + 1) * units] = gate
        hidden[...] = hidden_new
        cell[...] = cell_new
        hidden_out[0] = hidden_new
        cell_out[0] = cell_new
        query = product(hidden_new, query_upper[...], query_lower[...])
        located = product(window_now, loc_upper[...], loc_lower[...])
        energy_v = energy_ref[...]
        lane = lane_index((2 * rows, lanes))
        energy = jnp.zeros((2 * rows, lanes), f32)
        for place in range(positions):
            taken = slice(place * lanes, (place + 1) * lanes)
            ready = processed_ref[:, taken]
            bent = jnp.tanh(query + jnp.concatenate([ready, ready], axis=0) + located[:, taken])
            bent_out[0, :, taken] = bent
            energy = jnp.where(lane == place, jnp.sum(bent * energy_v, axis=1, keepdims=True), energy)
        masked = jnp.where(allowed_ref[...] > 0.5, energy, -1000000000.0)
        exponent = jnp.exp(masked - jnp.max(masked, axis=1, keepdims=True))
        weights = exponent / jnp.sum(exponent, axis=1, keepdims=True)
        weights = jnp.where(lane < positions, weights, 0.0)
        weights_out[0] = weights
        window_out[0] = window_now
        second = (lane >= positions) & (lane < 2 * positions)
        window[...] = weights + pltpu.roll(weights, positions, 1) + jnp.where(second, window_now, 0.0)
        context_new = product(spread(weights, rows, positions), memory_upper[...], memory_lower[...])
        context[...] = context_new
        context_out[0] = context_new


def decoder_forward_kernel(
    blocks,
    rows,
    lag,
    awaited,
    weight_ref,
    frames_ref,
    bias_ref,
    zone_early_ref,
    zone_late_ref,
    resume_ref,
    *refs,
):
    hidden_out, cell_out, gates_out, upper, lower, inputs, sums, hidden, cell = refs[awaited:]
    step = pl.program_id(0)
    units = hidden.shape[1]
    width = shard_block * lanes

    @pl.when(step == 0)
    def prepare():
        hidden[...] = jnp.zeros_like(hidden)
        cell[...] = jnp.zeros_like(cell)

    @pl.when(step < blocks)
    def load():
        split_row = frames_ref.shape[1]
        store_parts(weight_ref, split_row, weight_ref.shape[1], upper, lower, step)
        first = jnp.concatenate([weight_ref[place, :split_row, :] for place in range(shard_block)], axis=1)
        first_upper, first_lower = split(first)
        inputs[step] = product(frames_ref[...], first_upper, first_lower) + bias_ref[0]

    @pl.when(step >= blocks)
    def advance():
        frame = step - blocks
        resume = resume_ref[0]
        hidden_now = hidden[...] * resume
        cell_now = cell[...] * resume
        early = pl.multiple_of(frame * rows, rows)
        late = pl.multiple_of((frame + lag) * rows, rows)
        for block in range(blocks):
            taken = slice(block * width, (block + 1) * width)
            sums[:rows, taken] = inputs[block, pl.ds(early, rows), :]
            sums[rows:, taken] = inputs[block, pl.ds(late, rows), :]

        @pl.when(frame > 0)
        def recur():
            for block in range(blocks):
                taken = slice(block * width, (block + 1) * width)
                sums[:, taken] += product(hidden_now, upper[block], lower[block])

        zone_hidden, zone_cell = zone_masks(zone_early_ref, zone_late_ref)
        hidden_new, cell_new, gates = gate_forward(sums[...], cell_now, hidden_now, zone_hidden, zone_cell)
        for place, gate in enumerate(gates):
            gates_out[0, :, place * units : (place + 1) * units] = gate
        hidden[...] = hidden_new
        cell[...] = cell_new
        hidden_out[0] = hidden_new
        cell_out[0] = cell_new


def add_frames(total_ref, grads, frame, rows, lag):
    early = pl.multiple_of(frame * rows, rows)
    late = pl.multiple_of((frame + lag) * rows, rows)
    total_ref[pl.ds(early, rows), :] += grads[:rows]
    total_ref[pl.ds(late, rows), :] += grads[rows:]


def decoder_backward_kernel(
    blocks,
    rows,
    lag,
    own_parts,
    in_parts,
    awaited,
    *refs,
):
    own_refs = refs[:own_parts]
    in_refs = refs[own_parts : own_parts + in_parts]
    (
        grad_ref,
        gates_ref,
        cell_ref,
        zone_early_ref,
        zone_late_ref,
        resume_ref,
        valid_ref,
    ) = refs[own_parts + in_parts : own_parts + in_parts + 7]
    grad_sums_out, grad_in_out, upper, lower, frame_sums, grad_hidden, grad_cell = refs[
        own_parts + in_parts + 7 + awaited :
    ]
    step = pl.program_id(0)
    units = grad_hidden.shape[1]
    width = shard_block * lanes

    @pl.when(step == 0)
    def prepare():
        grad_hidden[...] = jnp.zeros_like(grad_hidden)
        grad_cell[...] = jnp.zeros_like(grad_cell)
        frame_sums[...] = jnp.zeros_like(frame_sums)
        grad_in_out[...] = jnp.zeros_like(grad_in_out)

    @pl.when(step < blocks)
    def load():
        for which, own_ref in enumerate(own_refs):
            part = own_ref.shape[1]
            for place in range(shard_block):
                taken = slice(place * lanes, (place + 1) * lanes)
                own_upper, own_lower = split(own_ref[place])
                upper[step, which * part : (which + 1) * part, taken] = own_upper
                lower[step, which * part : (which + 1) * part, taken] = own_lower

    @pl.when((step >= blocks) & (step < blocks + span))
    def retreat():
        frame = span - 1 - (step - blocks)
        resume = resume_ref[0]
        early = pl.multiple_of(frame * rows, rows)
        late = pl.multiple_of((frame + lag) * rows, rows)
        arriving = jnp.concatenate([grad_ref[pl.ds(early, rows), :], grad_ref[pl.ds(late, rows), :]], axis=0)
        total = grad_hidden[...] + arriving * valid_ref[0]
        cell_now = cell_ref[0] * jnp.where(frame > 0, resume, 0.0)
        zone_hidden, zone_cell = zone_masks(zone_early_ref, zone_late_ref)
        grad_sums, passed_hidden, passed_cell = gate_backward(
            gates_ref[0], cell_now, zone_hidden, zone_cell, total, grad_cell[...]
        )
        grad_cell[...] = passed_cell * resume
        grad_hidden[...] = passed_hidden
        for place, grads in enumerate(grad_sums):
            for part in range(units // width):
                block = place * (units // width) + part
                add_frames(frame_sums.at[block], grads[:, part * width : (part + 1) * width], frame, rows, lag)

        @pl.when(frame > 0)
        def recur():
            carried = grad_hidden[...]
            for place, grads in enumerate(grad_sums):
                for part in range(units // width):
                    block = place * (units // width) + part
                    taken = grads[:, part * width : (part + 1) * width]
                    carried = carried + product(taken, upper[block], lower[block], transposed=True)
            grad_hidden[...] = carried * resume

    @pl.when(step >= blocks + span)
    def pass_on():
        block = step - blocks - span
        grads = frame_sums[block]
        for place in range(shard_block):
            grad_sums_out[place] = grads[:, place * lanes : (place + 1) * lanes]
        for which, in_ref in enumerate(in_refs):
            part = in_ref.shape[1]
            taken = slice(which * part, (which + 1) * part)
            first = jnp.concatenate([in_ref[place] for place in range(shard_block)], axis=1)
            first_upper, first_lower = split(first)
            grad_in_out[:, taken] += product(grads, first_upper, first_lower, transposed=True)


def attention_backward_kernel(
    blocks,
    rows,
    positions,
    lag,
    weight_ref,
    grad_hidden_ref,
    grad_context_ref,
    gates_ref,
    cell_ref,
    bent_ref,
    weights_ref,
    window_ref,
    loc_map_ref,
    memory_ref,
    query_ref,
    energy_ref,
    zone_early_ref,
    zone_late_ref,
    resume_ref,
    valid_ref,
    next_resume_ref,
    awaited,
    grad_sums_out,
    grad_bias_out,
    grad_prenet_out,
    grad_query_out,
    grad_processed_out,
    grad_memory_out,
    grad_loc_out,
    grad_energy_out,
    upper,
    lower,
    first_upper,
    first_lower,
    frame_sums,
    loc_upper,
    loc_lower,
    memory_upper,
    memory_lower,
    query_upper,
    query_lower,
    grad_bent,
    grad_contexts,
    diagonals,
    windows,
    grad_hidden,
    grad_cell,
    grad_context,
    grad_window,
):
    step = pl.program_id(0)
    units = grad_hidden.shape[1]
    context_width = grad_context.shape[1]
    prenet_width = first_upper.shape[1]
    width = shard_block * lanes
    pair = 2 * rows

    @pl.when(step == 0)
    def prepare():
        loc_upper[...], loc_lower[...] = split(loc_map_ref[...])
        memory_upper[...], memory_lower[...] = split(memory_ref[...])
        query_upper[...], query_lower[...] = split(query_ref[...])
        grad_hidden[...] = jnp.zeros_like(grad_hidden)
        grad_cell[...] = jnp.zeros_like(grad_cell)
        grad_context[...] = jnp.zeros_like(grad_context)
        grad_window[...] = jnp.zeros_like(grad_window)
        frame_sums[...] = jnp.zeros_like(frame_sums)
        grad_query_out[...] = jnp.zeros_like(grad_query_out)
        grad_processed_out[...] = jnp.zeros_like(grad_processed_out)
        grad_energy_out[...] = jnp.zeros_like(grad_energy_out)

    @pl.when(step < blocks)
    def load():
        store_parts(weight_ref, prenet_width, weight_ref.shape[1], upper, lower, step)
        store_parts(weight_ref, 0, prenet_width, first_upper, first_lower, step)

    @pl.when(step >= blocks)
    def retreat():
        frame = span - 1 - (step - blocks)
        resume = resume_ref[0]
        valid = valid_ref[0]
        early = pl.multiple_of(frame * rows, rows)
        late = pl.multiple_of((frame + lag) * rows, rows)
        here = pl.multiple_of(frame * pair, pair)
        lane = lane_index((pair, lanes))
        arriving = jnp.concatenate(
            [grad_context_ref[pl.ds(early, rows), :], grad_context_ref[pl.ds(late, rows), :]], axis=0
        )
        context_total = grad_context[...] + arriving * valid
        grad_contexts[pl.ds(here, pair), :] = context_total
        weights = weights_ref[0]
        diagonals[pl.ds(here, pair), :] = spread(weights, rows, positions)
        windows[pl.ds(here, pair), :] = window_ref[0]
        window_grad = grad_window[...]
        wide = product(context_total, memory_upper[...], memory_lower[...], transposed=True)
        grad_weights = collect(wide, rows, positions) + jnp.where(
            lane < positions, window_grad + pltpu.roll(window_grad, lanes - positions, 1), 0.0
        )
        inner = jnp.sum(weights * grad_weights, axis=1, keepdims=True)
        grad_energy = weights * (grad_weights - inner)
        energy_v = energy_ref[...]
        energy_total = jnp.zeros((pair, lanes), f32)
        query_total = jnp.zeros((pair, lanes), f32)
        for place in range(positions):
            taken = slice(place * lanes, (place + 1) * lanes)
            bent = bent_ref[0, :, taken]
            column = jnp.sum(jnp.where(lane == place, grad_energy, 0.0), axis=1, keepdims=True)
            energy_total = energy_total + column * bent
            slope = column * energy_v * (1.0 - bent * bent)
            query_total = query_total + slope
            grad_bent[pl.ds(here, pair), taken] = slope
            grad_processed_out[:, taken] += slope[:rows] + slope[rows:]
        grad_energy_out[...] += energy_total
        add_frames(grad_query_out, query_total, frame, rows, lag)
        slopes = grad_bent[pl.ds(here, pair), :]
        moved = product(slopes, loc_upper[...], loc_lower[...], transposed=True)
        second = (lane >= positions) & (lane < 2 * positions)
        grad_window[...] = resume * (moved + jnp.where(second, window_grad, 0.0))

        arriving = jnp.concatenate(
            [grad_hidden_ref[pl.ds(early, rows), :], grad_hidden_ref[pl.ds(late, rows), :]], axis=0
        )
        total = grad_hidden[...] + arriving * valid
        total = total + product(query_total, query_upper[...], query_lower[...], transposed=True)
        cell_now = cell_ref[0] * jnp.where(frame > 0, resume, 0.0)
        zone_hidden, zone_cell = zone_masks(zone_early_ref, zone_late_ref)
        grad_sums, passed_hidden, passed_cell = gate_backward(
            gates_ref[0], cell_now, zone_hidden, zone_cell, total, grad_cell[...]
        )
        grad_cell[...] = passed_cell * resume
        for place, grads in enumerate(grad_sums):
            for part in range(units // width):
                block = place * (units // width) + part
                add_frames(frame_sums.at[block], grads[:, part * width : (part + 1) * width], frame, rows, lag)

        @pl.when(frame > 0)
        def recur():
            carried = jnp.zeros((pair, context_width + units), f32)
            for place, grads in enumerate(grad_sums):
                for part in range(units // width):
                    block = place * (units // width) + part
                    taken = grads[:, part * width : (part + 1) * width]
                    carried = carried + product(taken, upper[block], lower[block], transposed=True)
            grad_context[...] = carried[:, :context_width] * resume
            grad_hidden[...] = (carried[:, context_width:] + passed_hidden) * resume

    @pl.when(step == blocks + span - 1)
    def finish():
        prenet_grad = jnp.zeros(grad_prenet_out.shape, f32)
        frame_rows = frame_sums.shape[1]
        for block in range(blocks):
            grads = frame_sums[block]
            prenet_grad = prenet_grad + product(grads, first_upper[block], first_lower[block], transposed=True)
            grad_bias_out[:, block * width : (block + 1) * width] = jnp.sum(grads, axis=0, keepdims=True)
            later = jnp.concatenate([grads[rows:], jnp.zeros((rows, width), f32)], axis=0) * next_resume_ref[...]
            for place in range(shard_block):
                grad_sums_out[block * shard_block + place] = later[:, place * lanes : (place + 1) * lanes]
        grad_prenet_out[...] = prenet_grad
        context_upper, context_lower = split(grad_contexts[...])
        grad_memory_out[...] = product(diagonals[...].T, context_upper, context_lower)
        window_turned = windows[...].T
        for block in range(blocks):
            taken = slice(block * width, (block + 1) * width)
            bent_upper, bent_lower = split(grad_bent[:, taken])
            grad_loc_out[:, taken] = product(window_turned, bent_upper, bent_lower)


def split_kernel(values_ref, upper_ref, lower_ref):
    upper_ref[...], lower_ref[...] = split(values_ref[...])


def split_matrix(values):
    shape = jax.ShapeDtypeStruct(values.shape, bf16)
    return pl.pallas_call(
        split_kernel,
        out_shape=[shape, shape],
        compiler_params=pltpu.CompilerParams(vmem_limit_bytes=vmem_limit),
        name="split_matrix",
    )(values)


def join_kernel(count, *refs):
    out_ref, token_ref = refs[-2:]
    start = 0
    for ref in refs[:count]:
        out_ref[start : start + ref.shape[0]] = ref[...]
        start += ref.shape[0]
    token_ref[...] = jnp.zeros_like(token_ref)


def join_rows(arrays, awaited):
    total = sum(array.shape[0] for array in arrays)
    return pl.pallas_call(
        functools.partial(join_kernel, len(arrays)),
        in_specs=[pl.BlockSpec(memory_space=pltpu.VMEM)] * len(arrays)
        + [pl.BlockSpec(memory_space=pl.ANY)] * len(awaited),
        out_shape=[jax.ShapeDtypeStruct((total, lanes), f32), jax.ShapeDtypeStruct((8, lanes), f32)],
        compiler_params=pltpu.CompilerParams(vmem_limit_bytes=vmem_limit),
        name="join_rows",
    )(*arrays, *awaited)


def pack_sums(first, second):
    rows = []
    for row in (first, second):
        channels = row.shape[1]
        if channels % lanes:
            row = jnp.concatenate([row, jnp.zeros((1, -channels % lanes), f32)], axis=1)
        rows += [row[:, start : start + lanes] for start in range(0, row.shape[1], lanes)]
    if len(rows) < 8:
        rows.append(jnp.zeros((8 - len(rows), lanes), f32))
    return jnp.concatenate(rows, axis=0)


def unpack_sums(packed, channels):
    count = -(-channels // lanes)
    rows = []
    for row in range(2):
        pieces = [packed[row * count + place : row * count + place + 1] for place in range(count)]
        rows.append(jnp.concatenate(pieces, axis=1)[:, :channels])
    return rows


def moved_rows(values, shift):
    if shift > 0:
        return jnp.concatenate([jnp.zeros((shift, values.shape[1]), f32), values[:-shift]], axis=0)
    if shift < 0:
        return jnp.concatenate([values[-shift:], jnp.zeros((-shift, values.shape[1]), f32)], axis=0)
    return values


def convolve(values, same, upper_ref, lower_ref, rows):
    kernel = upper_ref.shape[0] // values.shape[1]
    channels = values.shape[1]
    total = None
    for tap in range(kernel):
        taken = slice(tap * channels, (tap + 1) * channels)
        moved = moved_rows(values, (kernel // 2 - tap) * rows) * same[:, tap : tap + 1]
        piece = product(moved, upper_ref[taken, :], lower_ref[taken, :])
        total = piece if total is None else total + piece
    return total


def send_sums(copies_ref, first, second):
    packed = pack_sums(jnp.sum(first, axis=0, keepdims=True), jnp.sum(second, axis=0, keepdims=True))
    for place in range(copies_ref.shape[0]):
        copies_ref[place] = packed


def post_first_kernel(rows, values_ref, same_ref, upper_ref, lower_ref, conv_out, copies_out):
    conv = convolve(values_ref[...], same_ref[...], upper_ref, lower_ref, rows)
    conv_out[...] = conv
    send_sums(copies_out, conv, conv * conv)


def post_next_kernel(
    rows,
    frame_count,
    conv_ref,
    sums_ref,
    gain_ref,
    shift_ref,
    same_ref,
    upper_ref,
    lower_ref,
    scaled_out,
    active_out,
    inverse_out,
    conv_out,
    copies_out,
):
    conv = conv_ref[...]
    first, second = unpack_sums(jnp.sum(sums_ref[...], axis=0), conv.shape[1])
    average = first / frame_count
    inverse = lax.rsqrt(second / frame_count - average * average + norm_eps)
    scaled = (conv - average) * inverse
    active = jnp.tanh(scaled * gain_ref[...] + shift_ref[...])
    scaled_out[...] = scaled
    active_out[...] = active
    inverse_out[...] = inverse
    conv = convolve(active, same_ref[...], upper_ref, lower_ref, rows)
    conv_out[...] = conv
    send_sums(copies_out, conv, conv * conv)


def post_back_kernel(
    rows,
    frame_count,
    has_lower,
    awaited,
    grad_ref,
    scaled_ref,
    sums_ref,
    inverse_ref,
    gain_ref,
    same_ref,
    upper_ref,
    lower_ref,
    *refs,
):
    if has_lower:
        active_ref, scaled_below_ref = refs[:2]
        conv_out, sums_out, grad_out, copies_out = refs[2 + awaited :]
    else:
        conv_out, sums_out, grad_out = refs[awaited:]
    grad = grad_ref[...]
    scaled = scaled_ref[...]
    same = same_ref[...]
    packed = jnp.sum(sums_ref[...], axis=0)
    sums_out[...] = packed
    shift_grad, gain_grad = unpack_sums(packed, grad.shape[1])
    grad_conv = inverse_ref[...] * gain_ref[...] * (grad - (shift_grad + scaled * gain_grad) / frame_count)
    conv_out[...] = grad_conv
    channels = grad_out.shape[1]
    kernel = upper_ref.shape[0] // channels
    total = None
    for tap in range(kernel):
        taken = slice(tap * channels, (tap + 1) * channels)
        piece = product(grad_conv, upper_ref[taken, :], lower_ref[taken, :], transposed=True)
        piece = moved_rows(piece * same[:, tap : tap + 1], (tap - kernel // 2) * rows)
        total = piece if total is None else total + piece
    if has_lower:
        active = active_ref[...]
        total = total * (1.0 - active * active)
        send_sums(copies_out, total, total * scaled_below_ref[...])
    grad_out[...] = total


def post_call(kernel, outs, name, operands, awaited=()):
    shapes = [jax.ShapeDtypeStruct(shape, f32) for shape in outs]
    in_specs = [pl.BlockSpec(memory_space=pltpu.VMEM)] * len(operands)
    in_specs += [pl.BlockSpec(memory_space=pl.ANY)] * len(awaited)
    return pl.pallas_call(
        kernel,
        in_specs=in_specs,
        out_specs=[pl.BlockSpec(memory_space=pltpu.VMEM)] * len(outs),
        out_shape=shapes,
        compiler_params=pltpu.CompilerParams(vmem_limit_bytes=vmem_limit),
        name=name,
    )(*operands, *awaited)


def share_sums(copies):
    return lax.all_to_all(copies, both, 0, 0)


def tap_gradient_kernel(rows, inputs_ref, grads_ref, same_ref, out_ref):
    groups, frame_rows, columns = grads_ref.shape
    kernel = out_ref.shape[0]
    margin = kernel // 2
    moved = []
    for tap in range(kernel):
        pieces = []
        for group in range(groups):
            masked = grads_ref[group] * same_ref[group][:, tap : tap + 1]
            pieces.append(moved_rows(masked, (tap - margin) * rows))
        moved.append(jnp.concatenate(pieces, axis=0))
    upper, lower = split(jnp.concatenate(moved, axis=1))
    inputs = inputs_ref[...].reshape(groups * frame_rows, -1)
    result = product(inputs.T, upper, lower)
    for tap in range(kernel):
        out_ref[tap] = result[:, tap * columns : (tap + 1) * columns]


def tap_gradient(inputs, grads, same_segment, kernel, rows):
    out = jax.ShapeDtypeStruct((kernel, inputs.shape[2], grads.shape[2]), f32)
    return pl.pallas_call(
        functools.partial(tap_gradient_kernel, rows),
        out_shape=out,
        compiler_params=pltpu.CompilerParams(vmem_limit_bytes=vmem_limit),
        name="tap_gradient",
    )(inputs, grads, same_segment)


def frame_product_kernel(pieces, *refs):
    inputs = refs[:-4]
    near_ref, far_ref, out_ref, total = refs[-4:]
    step = pl.program_id(0)

    @pl.when(step == 0)
    def prepare():
        total[...] = jnp.zeros_like(total)

    blocks, groups = near_ref.shape[:2]
    grads = jnp.concatenate(
        [
            jnp.concatenate([ref[block, group] for group in range(groups)], axis=1)
            for ref in (near_ref, far_ref)
            for block in range(blocks)
        ],
        axis=0,
    )
    columns = grads.shape[1]
    turned_upper, turned_lower = split(grads.T)
    stacked = jnp.concatenate([turned_upper, turned_lower], axis=0)
    start = 0
    for which, first, last in pieces:
        values = jnp.concatenate([inputs[2 * which][:, first:last], inputs[2 * which + 1][:, first:last]], axis=0)
        upper, lower = split(values)
        one = jnp.dot(stacked, upper, preferred_element_type=f32)
        two = jnp.dot(turned_upper, lower, preferred_element_type=f32)
        total[:, start : start + last - first] += one[:columns] + one[columns:] + two
        start += last - first

    @pl.when(step == pl.num_programs(0) - 1)
    def finish():
        half = columns // 2
        out_ref[0] = total[:half].T
        out_ref[1] = total[half:].T


def frame_product(inputs, near, far, pieces):
    sources, groups, frames = near.shape[:3]
    block = 2 if sources % 2 == 0 else 1
    columns = groups // 2 * lanes
    depth = sum(last - first for _, first, last in pieces)
    arrays = [array for pair in inputs for array in pair]

    def block_spec(array):
        return pl.BlockSpec((block * frames, array.shape[1]), lambda step: (step, 0))

    def grad_spec():
        return pl.BlockSpec((block, groups, frames, lanes), lambda step: (step, 0, 0, 0))

    return pl.pallas_call(
        functools.partial(frame_product_kernel, pieces),
        grid=(sources // block,),
        in_specs=[block_spec(array) for array in arrays] + [grad_spec(), grad_spec()],
        out_specs=pl.BlockSpec((2, depth, columns), lambda step: (0, 0, 0)),
        out_shape=jax.ShapeDtypeStruct((2, depth, columns), f32),
        scratch_shapes=[pltpu.VMEM((2 * columns, depth), f32)],
        compiler_params=params(),
        name="frame_product",
    )(*arrays, near, far)


def whole_spec(array):
    rank = len(array.shape)
    return pl.BlockSpec(array.shape, lambda step: (0,) * rank)


def timed_spec(array, place, depth=None):
    shape = (1,) + tuple(array.shape[1:])
    rank = len(array.shape)
    return pl.BlockSpec(shape, lambda step: (place(step),) + (0,) * (rank - 1))


def shard_spec(array, place):
    shape = (shard_block,) + tuple(array.shape[1:])
    return pl.BlockSpec(shape, lambda step: (place(step), 0, 0))


def zone_spec(zone, place, which):
    shape = (1, 2) + tuple(zone.shape[2:])
    return pl.BlockSpec(shape, lambda step: (place(step), which, 0, 0))


def out_spec(shape):
    rank = len(shape)
    return pl.BlockSpec(shape, lambda step: (0,) * rank)


def cost(weights, passes):
    return pl.CostEstimate(flops=2 * 256 * weights * 2 * passes, bytes_accessed=4 * weights, transcendentals=0)


def params():
    return pltpu.CompilerParams(vmem_limit_bytes=vmem_limit, dimension_semantics=("arbitrary",))


def attention_forward(
    weight, prenet_out, bias, loc_map, processed, memory, query_weight, energy_v, zone, resume, allowed, lag, awaited
):
    groups, depth = weight.shape[:2]
    blocks = groups // shard_block
    rows = memory.shape[0] // (processed.shape[1] // lanes)
    positions = processed.shape[1] // lanes
    columns = groups * lanes
    units = columns // 4
    context_width = memory.shape[1]
    frame_rows = prenet_out.shape[0]
    rest = depth - prenet_out.shape[1]
    width = shard_block * lanes
    pair = 2 * rows

    def shard(step):
        return jnp.minimum(step, blocks - 1)

    def timed(step):
        return jnp.clip(step - blocks, 0, span - 1)

    def later(step):
        return timed(step) + lag

    timed_shapes = [
        (span, pair, units),
        (span, pair, units),
        (span, pair, context_width),
        (span, pair, columns),
        (span, pair, positions * lanes),
        (span, pair, lanes),
        (span, pair, lanes),
    ]
    out_shape = [jax.ShapeDtypeStruct(shape, f32) for shape in timed_shapes]
    bias_blocks = bias.reshape(blocks, 1, width)
    return pl.pallas_call(
        functools.partial(attention_forward_kernel, blocks, rows, positions, lag),
        grid=(blocks + span,),
        in_specs=[
            shard_spec(weight, shard),
            whole_spec(prenet_out),
            timed_spec(bias_blocks, shard),
            whole_spec(loc_map),
            whole_spec(processed),
            whole_spec(memory),
            whole_spec(query_weight),
            whole_spec(energy_v),
            zone_spec(zone, timed, 0),
            zone_spec(zone, later, 0),
            timed_spec(resume, timed),
            whole_spec(allowed),
            pl.BlockSpec(memory_space=pl.ANY),
        ],
        out_specs=[timed_spec(shape, timed) for shape in out_shape],
        out_shape=out_shape,
        scratch_shapes=[
            pltpu.VMEM((blocks, rest, width), bf16),
            pltpu.VMEM((blocks, rest, width), bf16),
            pltpu.VMEM((blocks, frame_rows, width), f32),
            pltpu.VMEM(loc_map.shape, bf16),
            pltpu.VMEM(loc_map.shape, bf16),
            pltpu.VMEM(memory.shape, bf16),
            pltpu.VMEM(memory.shape, bf16),
            pltpu.VMEM(query_weight.shape, bf16),
            pltpu.VMEM(query_weight.shape, bf16),
            pltpu.VMEM((pair, columns), f32),
            pltpu.VMEM((pair, units), f32),
            pltpu.VMEM((pair, units), f32),
            pltpu.VMEM((pair, context_width), f32),
            pltpu.VMEM((pair, lanes), f32),
        ],
        compiler_params=params(),
        cost_estimate=cost(depth * columns, span),
        name="attention_forward",
    )(
        weight,
        prenet_out,
        bias_blocks,
        loc_map,
        processed,
        memory,
        query_weight,
        energy_v,
        zone,
        zone,
        resume,
        allowed,
        awaited,
    )


def decoder_forward(weight, frames, bias, zone, resume, rows, lag, awaited):
    groups = weight.shape[0]
    blocks = groups // shard_block
    columns = groups * lanes
    units = columns // 4
    width = shard_block * lanes
    pair = 2 * rows

    def shard(step):
        return jnp.minimum(step, blocks - 1)

    def timed(step):
        return jnp.clip(step - blocks, 0, span - 1)

    def later(step):
        return timed(step) + lag

    timed_shapes = [(span, pair, units), (span, pair, units), (span, pair, columns)]
    out_shape = [jax.ShapeDtypeStruct(shape, f32) for shape in timed_shapes]
    bias_blocks = bias.reshape(blocks, 1, width)
    return pl.pallas_call(
        functools.partial(decoder_forward_kernel, blocks, rows, lag, len(awaited)),
        grid=(blocks + span,),
        in_specs=[
            shard_spec(weight, shard),
            whole_spec(frames),
            timed_spec(bias_blocks, shard),
            zone_spec(zone, timed, 1),
            zone_spec(zone, later, 1),
            timed_spec(resume, timed),
        ]
        + [pl.BlockSpec(memory_space=pl.ANY)] * len(awaited),
        out_specs=[timed_spec(shape, timed) for shape in out_shape],
        out_shape=out_shape,
        scratch_shapes=[
            pltpu.VMEM((blocks, units, width), bf16),
            pltpu.VMEM((blocks, units, width), bf16),
            pltpu.VMEM((blocks, frames.shape[0], width), f32),
            pltpu.VMEM((pair, columns), f32),
            pltpu.VMEM((pair, units), f32),
            pltpu.VMEM((pair, units), f32),
        ],
        compiler_params=params(),
        cost_estimate=cost(weight.shape[1] * columns, span // 2),
        name="decoder_forward",
    )(weight, frames, bias_blocks, zone, zone, resume, *awaited)


def decoder_backward(weight, grad, gates, cells, zone, resume, valid, rows, lag, awaited):
    groups, depth = weight.shape[:2]
    blocks = groups // shard_block
    columns = groups * lanes
    units = columns // 4
    split_row = depth - units
    width = shard_block * lanes
    pair = 2 * rows
    frame_rows = grad.shape[0]
    part = math.gcd(units, split_row)
    own_parts = units // part
    in_parts = split_row // part

    def part_spec(index):
        return pl.BlockSpec((shard_block, part, lanes), index)

    def own_spec(which):
        return part_spec(lambda step: (shard(step), in_parts + which, 0))

    def in_spec(which):
        return part_spec(lambda step: (last_shard(step), which, 0))

    def shard(step):
        return jnp.minimum(step, blocks - 1)

    def last_shard(step):
        return jnp.clip(step - blocks - span, 0, blocks - 1)

    def timed(step):
        return span - 1 - jnp.clip(step - blocks, 0, span - 1)

    def later(step):
        return timed(step) + lag

    def before(step):
        return jnp.maximum(timed(step) - 1, 0)

    out_shape = [
        jax.ShapeDtypeStruct((groups, frame_rows, lanes), f32),
        jax.ShapeDtypeStruct((frame_rows, split_row), f32),
    ]
    return pl.pallas_call(
        functools.partial(decoder_backward_kernel, blocks, rows, lag, own_parts, in_parts, len(awaited)),
        grid=(2 * blocks + span,),
        in_specs=[own_spec(which) for which in range(own_parts)]
        + [in_spec(which) for which in range(in_parts)]
        + [
            whole_spec(grad),
            timed_spec(gates, timed),
            timed_spec(cells, before),
            zone_spec(zone, timed, 1),
            zone_spec(zone, later, 1),
            timed_spec(resume, timed),
            timed_spec(valid, timed),
        ]
        + [pl.BlockSpec(memory_space=pl.ANY)] * len(awaited),
        out_specs=[shard_spec(out_shape[0], last_shard), whole_spec(out_shape[1])],
        out_shape=out_shape,
        scratch_shapes=[
            pltpu.VMEM((blocks, units, width), bf16),
            pltpu.VMEM((blocks, units, width), bf16),
            pltpu.VMEM((blocks, frame_rows, width), f32),
            pltpu.VMEM((pair, units), f32),
            pltpu.VMEM((pair, units), f32),
        ],
        compiler_params=params(),
        cost_estimate=cost(depth * columns, span // 2),
        name="decoder_backward",
    )(*[weight] * (own_parts + in_parts), grad, gates, cells, zone, zone, resume, valid, *awaited)


def attention_backward(
    weight,
    grad_hidden,
    grad_context,
    gates,
    cells,
    bent,
    weights,
    window,
    loc_map,
    memory,
    query_weight,
    energy_v,
    zone,
    resume,
    valid,
    next_resume,
    rows,
    positions,
    prenet_width,
    lag,
    awaited,
):
    groups, depth = weight.shape[:2]
    blocks = groups // shard_block
    columns = groups * lanes
    units = columns // 4
    width = shard_block * lanes
    pair = 2 * rows
    frame_rows = grad_hidden.shape[0]
    context_width = grad_context.shape[1]
    rest = depth - prenet_width

    def shard(step):
        return jnp.minimum(step, blocks - 1)

    def timed(step):
        return span - 1 - jnp.clip(step - blocks, 0, span - 1)

    def later(step):
        return timed(step) + lag

    def before(step):
        return jnp.maximum(timed(step) - 1, 0)

    shapes = [
        (groups, frame_rows, lanes),
        (1, columns),
        (frame_rows, prenet_width),
        (frame_rows, lanes),
        (rows, positions * lanes),
        (rows * positions, context_width),
        loc_map.shape,
        (pair, lanes),
    ]
    return pl.pallas_call(
        functools.partial(attention_backward_kernel, blocks, rows, positions, lag),
        grid=(blocks + span,),
        in_specs=[
            shard_spec(weight, shard),
            whole_spec(grad_hidden),
            whole_spec(grad_context),
            timed_spec(gates, timed),
            timed_spec(cells, before),
            timed_spec(bent, timed),
            timed_spec(weights, timed),
            timed_spec(window, timed),
            whole_spec(loc_map),
            whole_spec(memory),
            whole_spec(query_weight),
            whole_spec(energy_v),
            zone_spec(zone, timed, 0),
            zone_spec(zone, later, 0),
            timed_spec(resume, timed),
            timed_spec(valid, timed),
            whole_spec(next_resume),
        ]
        + [pl.BlockSpec(memory_space=pl.ANY)] * len(awaited),
        out_specs=[out_spec(shape) for shape in shapes],
        out_shape=[jax.ShapeDtypeStruct(shape, f32) for shape in shapes],
        scratch_shapes=[
            pltpu.VMEM((blocks, rest, width), bf16),
            pltpu.VMEM((blocks, rest, width), bf16),
            pltpu.VMEM((blocks, prenet_width, width), bf16),
            pltpu.VMEM((blocks, prenet_width, width), bf16),
            pltpu.VMEM((blocks, frame_rows, width), f32),
            pltpu.VMEM(loc_map.shape, bf16),
            pltpu.VMEM(loc_map.shape, bf16),
            pltpu.VMEM(memory.shape, bf16),
            pltpu.VMEM(memory.shape, bf16),
            pltpu.VMEM(query_weight.shape, bf16),
            pltpu.VMEM(query_weight.shape, bf16),
            pltpu.VMEM((span * pair, positions * lanes), f32),
            pltpu.VMEM((span * pair, context_width), f32),
            pltpu.VMEM((span * pair, rows * positions), f32),
            pltpu.VMEM((span * pair, lanes), f32),
            pltpu.VMEM((pair, units), f32),
            pltpu.VMEM((pair, units), f32),
            pltpu.VMEM((pair, context_width), f32),
            pltpu.VMEM((pair, lanes), f32),
        ],
        compiler_params=params(),
        cost_estimate=cost(depth * columns, 2 * span),
        name="attention_backward",
    )(
        weight,
        grad_hidden,
        grad_context,
        gates,
        cells,
        bent,
        weights,
        window,
        loc_map,
        memory,
        query_weight,
        energy_v,
        zone,
        zone,
        resume,
        valid,
        next_resume,
        *awaited,
    )


def dot(left, right, left_dim=1, right_dim=0):
    return lax.dot_general(
        left, right, (((left_dim,), (right_dim,)), ((), ())), precision=high, preferred_element_type=f32
    )


def gather_columns(shard):
    depth, width = shard.shape
    if width % lanes:
        full = lax.all_gather(shard, both, axis=1, tiled=True)
        return full.reshape(depth, -1, lanes).swapaxes(0, 1)
    stacked = lax.all_gather(shard, both, axis=0)
    if width == lanes:
        return stacked
    return stacked.reshape(-1, depth, width // lanes, lanes).swapaxes(1, 2).reshape(-1, depth, lanes)


def along_core(values):
    return lax.ppermute(values, "section", [(place, place ^ 1) for place in range(4)])


def along_y(values):
    return lax.ppermute(values, "section", [(place, place ^ 2) for place in range(4)])


def gather_y(values):
    return jnp.stack([values, along_y(values)])


def gather_core(two):
    return jnp.concatenate([two, along_core(two)], axis=0)


def gather_section(values):
    return gather_core(gather_y(values))


def section_order(four, own):
    entries = []
    for place in range(4):
        offset = own ^ place
        held = (offset % 2) * 2 + offset // 2
        entries.append(lax.dynamic_index_in_dim(four, held, 0, keepdims=False))
    return entries


def section_columns(pair, layers):
    own = lax.axis_index("section")
    four = gather_core(pair)
    depth = four.shape[1] // layers
    whole = []
    for layer in range(layers):
        blocks = section_order(four[:, layer * depth : (layer + 1) * depth], own)
        whole.append(jnp.concatenate(blocks, axis=1))
    return whole


def own_columns(values, columns):
    own = lax.axis_index("section")
    total = values[..., :columns]
    for place in range(1, values.shape[-1] // columns):
        total = jnp.where(own == place, values[..., place * columns : (place + 1) * columns], total)
    return total


def flat_join(arrays, devices):
    pieces = []
    for array in arrays:
        flat = array.reshape(-1)
        flat = jnp.pad(flat, (0, -flat.shape[0] % lanes))
        pieces.append(flat.reshape(-1, lanes))
    joined = jnp.concatenate(pieces, axis=0)
    joined = jnp.pad(joined, ((0, -joined.shape[0] % (8 * devices)), (0, 0)))
    return joined.reshape(devices, -1, lanes)


def part_sum(joined):
    return jnp.sum(lax.all_to_all(joined, both, 0, 0), axis=0)


def flat_whole(part, devices):
    return lax.all_to_all(jnp.broadcast_to(part[None], (devices,) + part.shape), both, 0, 0)


def flat_split(whole, arrays):
    whole = whole.reshape(-1, lanes)
    sums = []
    start = 0
    for array in arrays:
        count = -(-array.size // lanes)
        flat = whole[start : start + count].reshape(-1)
        sums.append(flat[: array.size].reshape(array.shape))
        start += count
    return sums


def gather_plane(values):
    near = lax.all_gather(values, "dp", axis=0, tiled=True)
    return near, along_core(near)


def exchange_plane(grads):
    groups, frames, width = grads.shape
    size = lax.axis_size("dp")
    received = lax.all_to_all(grads.reshape(size, groups // size, frames, width), "dp", 0, 0)
    received = received.reshape(size, 2, 2, -1, frames, width)
    core = lax.axis_index("section") % 2
    near = jnp.where(core == 0, received[:, :, 0], received[:, :, 1]).reshape(size, -1, frames, width)
    far = jnp.where(core == 0, received[:, :, 1], received[:, :, 0]).reshape(size, -1, frames, width)
    return near, along_core(far)


def sum_planes(parts):
    place = lax.axis_index("section") // 2
    mine = jnp.where(place == 0, parts[0], parts[1])
    other = jnp.where(place == 0, parts[1], parts[0])
    return mine + along_y(other)


def gathers_inputs(frame_rows, columns, devices):
    return frame_rows * devices <= columns


def column_gradients(inputs, pieces, received, grads):
    if received is not None:
        return sum_planes(frame_product(inputs, *received, pieces))
    groups, frames, width = grads.shape
    flat = grads.swapaxes(0, 1).reshape(frames, groups * width)
    parts = [
        lax.psum_scatter(dot(inputs[which][:, first:last], flat, 0, 0), both, scatter_dimension=1, tiled=True)
        for which, first, last in pieces
    ]
    return jnp.concatenate(parts, axis=0)


def gelu_slope(values):
    return jax.vjp(jax.nn.gelu, values)


def location_map(loc_filters, loc_dense, positions):
    filters, channels, taps = loc_filters.shape
    features = loc_dense.shape[1]
    joined = dot(loc_filters.reshape(filters, channels * taps), loc_dense, 0, 0)
    joined = joined.reshape(channels, taps, features)
    margin = taps // 2
    padded = jnp.pad(joined, ((0, 0), (positions, positions), (0, 0)))
    columns = [
        padded[:, positions + margin - place : 2 * positions + margin - place] for place in range(positions)
    ]
    spread_map = jnp.stack(columns, axis=2).reshape(channels * positions, positions * features)
    return jnp.pad(spread_map, ((0, lanes - channels * positions), (0, 0)))


def location_unmap(grad_map, channels, taps, positions, features):
    grads = grad_map[: channels * positions].reshape(channels, positions, positions, features)
    turned = jnp.flip(grads.swapaxes(1, 2), axis=1)
    padded = jnp.pad(turned, ((0, 0), (0, 0), (0, positions), (0, 0))).reshape(channels, -1, features)
    length = 2 * positions - 1
    skewed = padded[:, : positions * length].reshape(channels, positions, length, features)
    start = positions - 1 - taps // 2
    return jnp.sum(skewed[:, :, start : start + taps], axis=1)


def per_device(
    memory,
    enc_lengths,
    frame_segment,
    mel_target,
    prenet_keep,
    zone_keep,
    pre_first,
    pre_second,
    att_weight,
    att_bias,
    query_weight,
    memory_weight,
    loc_filters,
    loc_dense,
    energy_v,
    dec_weight,
    dec_bias,
    proj_weight,
    proj_bias,
    stop_weight,
    post_first,
    post_mid,
    post_last,
    norm_gain,
    norm_shift,
    last_gain,
    last_shift,
    grad_after,
    grad_stop,
):
    devices = lax.axis_size("dp") * lax.axis_size("section")
    rows, positions, context_width = memory.shape
    frames = frame_segment.shape[1]
    mel = mel_target.shape[2]
    units = att_bias.shape[0] // 4
    prenet_width = pre_first.shape[1]
    features = memory_weight.shape[1]
    lag = frames - span
    frame_rows = frames * rows

    att_all = gather_columns(att_weight)
    dec_all = gather_columns(dec_weight)
    mid_pair = gather_y(post_mid.reshape(-1, post_mid.shape[3]))
    mid_all = section_columns(mid_pair, 3)
    post_split = [split_matrix(weight.reshape(-1, weight.shape[-1])) for weight in [post_first] + mid_all + [post_last]]

    segment = frame_segment.T
    earlier = jnp.concatenate([segment[:1] - 1, segment[:-1]], axis=0)
    resume = (segment == earlier).astype(f32)
    shifted = jnp.concatenate([jnp.zeros_like(mel_target[:, :1]), mel_target[:, :-1]], axis=1)
    frames_in = (shifted.swapaxes(0, 1) * resume[:, :, None]).reshape(frame_rows, mel)
    keep = prenet_keep.transpose(1, 2, 0, 3).astype(f32) * 2.0
    keep_first = keep[:, 0].reshape(frame_rows, prenet_width)
    keep_second = keep[:, 1].reshape(frame_rows, prenet_width)
    gelu_first, first_back = gelu_slope(dot(frames_in, pre_first))
    pre_hidden = gelu_first * keep_first
    gelu_second, second_back = gelu_slope(dot(pre_hidden, pre_second))
    prenet_out = gelu_second * keep_second
    memory_flat = memory.reshape(rows * positions, context_width)
    processed = dot(memory_flat, memory_weight)
    loc_map = location_map(loc_filters, loc_dense, positions)
    zone = zone_keep.transpose(1, 2, 0, 3)

    first_part = segment == 0
    steps = jnp.arange(span)
    never = jnp.ones((span, rows), f32)
    resume_pair = jnp.concatenate([never, resume[lag:]], axis=1)[:, :, None]
    valid_pair = jnp.concatenate([first_part[:span], ~first_part[lag:]], axis=1).astype(f32)[:, :, None]
    encoder_first = jnp.arange(lanes)[None, :] < enc_lengths[:, :1]
    inside = jnp.arange(lanes)[None, :] < positions
    allowed = jnp.concatenate([encoder_first, inside & ~encoder_first], axis=0).astype(f32)
    next_resume = jnp.concatenate([resume[1:], jnp.zeros((1, rows), f32)], axis=0).reshape(frame_rows, 1)

    def to_frames(pairs):
        early = jnp.pad(pairs[:, :rows], ((0, lag), (0, 0), (0, 0)))
        late = jnp.pad(pairs[:, rows:], ((lag, 0), (0, 0), (0, 0)))
        return jnp.where(first_part[:, :, None], early, late).reshape(frame_rows, -1)

    energy_row = energy_v.reshape(1, features)
    processed_wide = processed.reshape(rows, positions * features)
    hidden, cells, contexts, gates, bent, weights, window = attention_forward(
        att_all,
        prenet_out,
        att_bias,
        loc_map,
        processed_wide,
        memory_flat,
        query_weight,
        energy_row,
        zone,
        resume_pair,
        allowed,
        lag,
        mid_pair,
    )
    att_frames = to_frames(hidden)
    context_frames = to_frames(contexts)
    dec_inputs = jnp.concatenate([att_frames, context_frames], axis=1)
    dec_hidden, dec_cells, dec_gates = decoder_forward(
        dec_all, dec_inputs, dec_bias, zone, resume_pair, rows, lag, [part for pair in post_split for part in pair]
    )
    dec_frames = to_frames(dec_hidden)

    prenet_later = jnp.concatenate([prenet_out[rows:], jnp.zeros((rows, prenet_width), f32)], axis=0)
    att_inputs_all = jnp.concatenate([prenet_later, context_frames, att_frames], axis=1)
    dec_earlier = jnp.concatenate([jnp.zeros((rows, units), f32), dec_frames[:-rows]], axis=0)
    dec_earlier = dec_earlier * resume.reshape(frame_rows, 1)
    dec_inputs_all = dec_earlier
    input_width = att_inputs_all.shape[1]
    input_pieces = []
    planes = gathers_inputs(frame_rows, 4 * units, devices)
    if planes:
        att_inputs_all = gather_plane(att_inputs_all)
        dec_inputs_all = gather_plane(dec_inputs_all)
        input_pieces = att_inputs_all + dec_inputs_all

    out_frames = jnp.concatenate([dec_frames, context_frames], axis=1)
    mel_before = dot(out_frames, proj_weight) + proj_bias
    stop_logit = jnp.sum(out_frames * stop_weight, axis=1).reshape(frames, rows).T

    section_size = lax.axis_size("section")
    kernel = post_first.shape[0]
    margin = kernel // 2
    padded = jnp.pad(segment, ((margin, margin), (0, 0)), constant_values=-1)
    same_segment = jnp.stack(
        [padded[offset : offset + frames] == segment for offset in range(kernel)], axis=2
    ).astype(f32)
    same = jnp.pad(same_segment, ((0, 0), (0, 0), (0, 8 - kernel))).reshape(frame_rows, 8)
    same_all = gather_section(same)
    frame_count = frame_rows * devices
    gains = [norm_gain[layer : layer + 1] for layer in range(4)] + [last_gain.reshape(1, mel)]
    shifts = [norm_shift[layer : layer + 1] for layer in range(4)] + [last_shift.reshape(1, mel)]
    widths = [post_first.shape[2]] * 4 + [mel]
    conv, copies = post_call(
        functools.partial(post_first_kernel, rows),
        [(frame_rows, widths[0]), (devices, 8, lanes)],
        "post_first",
        (mel_before, same, *post_split[0]),
    )
    scaled, inverse, active, inputs_all = [], [], [], []
    inputs_all.append(gather_section(jnp.pad(mel_before, ((0, 0), (0, lanes - mel)))))
    for layer in range(4):
        scaled_now, active_now, inverse_now, conv, copies = post_call(
            functools.partial(post_next_kernel, rows, frame_count),
            [
                (frame_rows, widths[layer]),
                (frame_rows, widths[layer]),
                (1, widths[layer]),
                (frame_rows, widths[layer + 1]),
                (devices, 8, lanes),
            ],
            "post_next",
            (conv, share_sums(copies), gains[layer], shifts[layer], same, *post_split[layer + 1]),
        )
        scaled.append(scaled_now)
        active.append(active_now)
        inverse.append(inverse_now)
        inputs_all.append(gather_section(active_now))
    first, second = unpack_sums(jnp.sum(share_sums(copies), axis=0), mel)
    average = first / frame_count
    inverse.append(lax.rsqrt(second / frame_count - average * average + norm_eps))
    scaled.append((conv - average) * inverse[4])
    mel_after = mel_before + scaled[4] * gains[4] + shifts[4]

    grad_after_frames = grad_after.swapaxes(0, 1).reshape(frame_rows, mel)
    upstream = grad_after_frames
    packed = pack_sums(
        jnp.sum(upstream, axis=0, keepdims=True), jnp.sum(upstream * scaled[4], axis=0, keepdims=True)
    )
    copies = jnp.broadcast_to(packed[None], (devices, 8, lanes))
    weight_grads = [None] * 5
    exchanged = []
    gain_grads = [None] * 5
    shift_grads = [None] * 5
    for layer in reversed(range(5)):
        below = (active[layer - 1], scaled[layer - 1]) if layer else ()
        awaited = (weight_grads[layer + 2],) if layer < 3 else ()
        outs = [(frame_rows, widths[layer]), (8, lanes), (frame_rows, widths[layer - 1] if layer else mel)]
        if layer:
            outs.append((devices, 8, lanes))
        results = post_call(
            functools.partial(post_back_kernel, rows, frame_count, layer > 0, len(awaited)),
            outs,
            "post_back",
            (
                upstream,
                scaled[layer],
                share_sums(copies),
                inverse[layer],
                gains[layer],
                same,
                *post_split[layer],
                *below,
            ),
            awaited,
        )
        grad_conv, packed, upstream = results[:3]
        if layer:
            copies = results[3]
        shift_grads[layer], gain_grads[layer] = [row.reshape(-1) for row in unpack_sums(packed, widths[layer])]
        channels = inputs_all[layer].shape[2]
        if layer < 4:
            grad_pair = gather_y(grad_conv)
            if layer < 2:
                exchanged.append(grad_pair)
            weight_grads[layer] = tap_gradient(
                inputs_all[layer],
                own_columns(gather_core(grad_pair), grad_conv.shape[1] // section_size),
                same_all,
                kernel,
                rows,
            )
        else:
            grads_all = gather_section(jnp.pad(grad_conv, ((0, 0), (0, lanes - mel))))
            weight_grads[layer] = tap_gradient(
                own_columns(inputs_all[layer], channels // section_size), grads_all, same_all, kernel, rows
            )

    grad_mel = grad_after_frames + upstream
    grad_stop_frames = grad_stop.T.reshape(frame_rows, 1)
    grad_out = dot(grad_mel, proj_weight, 1, 1) + grad_stop_frames * stop_weight
    mel_grads = jnp.pad(
        jnp.concatenate([grad_mel, grad_stop_frames], axis=1), ((0, 0), (0, lanes - mel - 1))
    )
    mel_pair = gather_y(mel_grads)
    mel_grads_all = gather_core(mel_pair).reshape(-1, lanes)
    outs_own = own_columns(gather_section(out_frames), out_frames.shape[1] // section_size)
    outs_own = outs_own.reshape(mel_grads_all.shape[0], -1)
    g_proj_part = dot(outs_own, mel_grads_all, 0, 0)
    dec_sums, grad_dec_inputs = decoder_backward(
        dec_all,
        grad_out[:, :units],
        dec_gates,
        dec_cells,
        zone,
        resume_pair,
        valid_pair,
        rows,
        lag,
        exchanged + [weight_grads[2], mel_pair, outs_own],
    )
    group_grads, group_token = join_rows(
        [grad.reshape(-1, lanes) for grad in weight_grads + [g_proj_part]]
        + [jnp.pad(jnp.sum(mel_grads_all, axis=0, keepdims=True), ((0, 7), (0, 0)))],
        input_pieces,
    )
    group_sums = lax.psum(group_grads, "dp")
    g_dec_bias = jnp.sum(dec_sums, axis=1).reshape(-1)
    grad_context = grad_out[:, units:] + grad_dec_inputs[:, units:]
    dec_columns = exchange_plane(dec_sums) if planes else None
    (
        att_sums,
        g_att_bias,
        grad_prenet,
        grad_query,
        grad_processed,
        grad_memory,
        grad_loc,
        grad_energy,
    ) = attention_backward(
        att_all,
        grad_dec_inputs[:, :units],
        grad_context,
        gates,
        cells,
        bent,
        weights,
        window,
        loc_map,
        memory_flat,
        query_weight,
        energy_row,
        zone,
        resume_pair,
        valid_pair,
        next_resume,
        rows,
        positions,
        prenet_width,
        lag,
        (group_token,),
    )
    att_columns = exchange_plane(att_sums) if planes else None
    grad_processed = grad_processed.reshape(rows * positions, features)
    grad_memory = grad_memory + dot(grad_processed, memory_weight, 1, 1)
    g_memory_weight = dot(memory_flat, grad_processed, 0, 0)
    g_query_weight = dot(att_frames, grad_query, 0, 0)
    (grad_second,) = second_back(grad_prenet * keep_second)
    g_pre_second = dot(pre_hidden, grad_second, 0, 0)
    (grad_first,) = first_back(dot(grad_second, pre_second, 1, 1) * keep_first)
    g_pre_first = dot(frames_in, grad_first, 0, 0)
    filters, channels, taps = loc_filters.shape
    grad_joined = location_unmap(grad_loc, channels, taps, positions, features)
    late_grads = (
        g_pre_first,
        g_pre_second,
        g_att_bias,
        g_query_weight,
        g_memory_weight,
        grad_joined,
        jnp.sum(grad_energy, axis=0),
        g_dec_bias,
    )
    late_part = part_sum(flat_join(late_grads, devices) + 0.0 * group_sums[0, 0])
    context_end = prenet_width + context_width
    dec_part = column_gradients(
        [att_inputs_all, dec_inputs_all],
        ((0, context_end, input_width), (0, prenet_width, context_end), (1, 0, units)),
        dec_columns,
        dec_sums,
    )
    att_part = column_gradients([att_inputs_all], ((0, 0, input_width),), att_columns, att_sums)

    late_sums = flat_split(flat_whole(late_part, devices), late_grads)
    grad_joined = late_sums[5].reshape(channels * taps, features)
    g_loc_filters = dot(loc_dense, grad_joined, 1, 1).reshape(loc_filters.shape)
    g_loc_dense = dot(loc_filters.reshape(filters, channels * taps), grad_joined)

    first_rows = kernel * lanes
    mid_end = first_rows + post_mid.size // lanes
    proj_start = mid_end + first_rows
    proj_end = proj_start + out_frames.shape[1] // section_size
    mid_part = group_sums[first_rows:mid_end].reshape(post_mid.shape)
    own = lax.axis_index("section")
    shared = jnp.concatenate([group_sums[:first_rows], group_sums[mid_end:proj_end]], axis=0)
    shared_all = section_order(gather_section(shared), own)
    g_post_first = jnp.concatenate(
        [piece[:first_rows].reshape(kernel, lanes, lanes)[:, :mel] for piece in shared_all], axis=2
    )
    g_post_last = jnp.concatenate(
        [piece[first_rows : 2 * first_rows].reshape(kernel, lanes, lanes)[:, :, :mel] for piece in shared_all], axis=1
    )
    g_proj = jnp.concatenate([piece[2 * first_rows :] for piece in shared_all], axis=0)
    g_proj_bias = group_sums[proj_end, :mel]
    return (
        mel_after.reshape(frames, rows, mel).swapaxes(0, 1),
        stop_logit,
        grad_memory.reshape(memory.shape),
        late_sums[0],
        late_sums[1],
        att_part,
        late_sums[2].reshape(-1),
        late_sums[3],
        late_sums[4],
        g_loc_filters,
        g_loc_dense,
        late_sums[6],
        dec_part,
        late_sums[7],
        g_proj[:, :mel],
        g_proj_bias,
        g_proj[:, mel],
        g_post_first,
        mid_part,
        g_post_last,
        jnp.stack(gain_grads[:4]),
        jnp.stack(shift_grads[:4]),
        gain_grads[4],
        shift_grads[4],
    )


def solution(mesh):
    rows_only = P(both)
    columns_only = P(None, both)
    mid_spec = P(None, None, None, "section")
    placed = (
        (rows_only,) * 6
        + (P(), P(), columns_only)
        + (P(),) * 6
        + (columns_only,)
        + (P(),) * 5
        + (mid_spec,)
        + (P(),) * 5
        + (rows_only, rows_only)
    )
    given = (
        (rows_only,) * 3
        + (P(), P(), columns_only)
        + (P(),) * 6
        + (columns_only,)
        + (P(),) * 5
        + (mid_spec,)
        + (P(),) * 5
    )
    return jax.shard_map(per_device, mesh=mesh, in_specs=placed, out_specs=given, check_vma=False)
```

```python
import functools
import math

import jax
import jax.numpy as jnp
from jax import lax
from jax.experimental import pallas as pl
from jax.experimental.pallas import tpu as pltpu
from jax.sharding import PartitionSpec as P

high = lax.Precision.HIGH
norm_eps = 1e-05
f32 = jnp.float32
bf16 = jnp.bfloat16
both = ("dp", "section")
lanes = 128
vmem_limit = 62 * 1024 * 1024

span = 6
shard_block = 4


def split(values):
    upper = values.astype(bf16)
    lower = (values - upper.astype(f32)).astype(bf16)
    return upper, lower


def product(left, upper, lower, transposed=False):
    rows = left.shape[0]
    left_upper, left_lower = split(left)
    stacked = jnp.concatenate([left_upper, left_lower], axis=0)
    dims = (((1,), (1,)), ((), ())) if transposed else (((1,), (0,)), ((), ()))
    first = lax.dot_general(stacked, upper, dims, preferred_element_type=f32)
    second = lax.dot_general(left_upper, lower, dims, preferred_element_type=f32)
    return first[:rows] + first[rows:] + second


def sigmoid(values):
    return 0.5 * jnp.tanh(0.5 * values) + 0.5


def lane_index(shape):
    return lax.broadcasted_iota(jnp.int32, shape, 1)


def fold_lanes(values, positions):
    copies = values
    shift = positions
    while shift < lanes:
        copies = copies + pltpu.roll(copies, shift, 1)
        shift *= 2
    return copies


def diagonal_mask(rows, positions):
    shape = (2 * rows, rows * positions)
    row = lax.broadcasted_iota(jnp.int32, shape, 0)
    group = lax.broadcasted_iota(jnp.int32, shape, 1) // positions
    return group == jnp.where(row >= rows, row - rows, row)


def spread(weights, rows, positions):
    copies = fold_lanes(weights, positions)
    wide = jnp.concatenate([copies] * (rows * positions // lanes), axis=1)
    return jnp.where(diagonal_mask(rows, positions), wide, 0.0)


def collect(wide, rows, positions):
    kept = jnp.where(diagonal_mask(rows, positions), wide, 0.0)
    total = kept[:, :lanes]
    for start in range(lanes, rows * positions, lanes):
        total = total + kept[:, start : start + lanes]
    shift = positions
    while shift < lanes:
        total = total + pltpu.roll(total, shift, 1)
        shift *= 2
    return jnp.where(lane_index(total.shape) < positions, total, 0.0)


def store_parts(block_ref, first, last, upper_ref, lower_ref, index):
    for place in range(shard_block):
        upper, lower = split(block_ref[place, first:last, :])
        upper_ref[index, :, place * lanes : (place + 1) * lanes] = upper
        lower_ref[index, :, place * lanes : (place + 1) * lanes] = lower


def gate_forward(gate_sums, cell, hidden, zone_hidden, zone_cell):
    units = cell.shape[1]
    gate_in = sigmoid(gate_sums[:, :units])
    gate_keep = sigmoid(gate_sums[:, units : 2 * units])
    update = jnp.tanh(gate_sums[:, 2 * units : 3 * units])
    gate_out = sigmoid(gate_sums[:, 3 * units :])
    new_cell = gate_keep * cell + gate_in * update
    new_hidden = gate_out * jnp.tanh(new_cell)
    hidden = zone_hidden * hidden + (1.0 - zone_hidden) * new_hidden
    cell = zone_cell * cell + (1.0 - zone_cell) * new_cell
    return hidden, cell, (gate_in, gate_keep, update, gate_out)


def gate_backward(gates, cell, zone_hidden, zone_cell, grad_hidden, grad_cell):
    units = cell.shape[1]
    gate_in = gates[:, :units]
    gate_keep = gates[:, units : 2 * units]
    update = gates[:, 2 * units : 3 * units]
    gate_out = gates[:, 3 * units :]
    bent = jnp.tanh(gate_keep * cell + gate_in * update)
    grad_new = (1.0 - zone_hidden) * grad_hidden
    grad_new_cell = grad_new * gate_out * (1.0 - bent * bent) + (1.0 - zone_cell) * grad_cell
    grad_sums = (
        grad_new_cell * update * gate_in * (1.0 - gate_in),
        grad_new_cell * cell * gate_keep * (1.0 - gate_keep),
        grad_new_cell * gate_in * (1.0 - update * update),
        grad_new * bent * gate_out * (1.0 - gate_out),
    )
    return grad_sums, zone_hidden * grad_hidden, zone_cell * grad_cell + grad_new_cell * gate_keep


def zone_masks(early_ref, late_ref):
    masks = []
    for which in range(2):
        pair = jnp.concatenate([early_ref[0, which], late_ref[0, which]], axis=0)
        masks.append(pair.astype(f32))
    return masks


def attention_forward_kernel(
    blocks,
    rows,
    positions,
    lag,
    weight_ref,
    prenet_ref,
    bias_ref,
    loc_map_ref,
    processed_ref,
    memory_ref,
    query_ref,
    energy_ref,
    zone_early_ref,
    zone_late_ref,
    resume_ref,
    allowed_ref,
    awaited,
    hidden_out,
    cell_out,
    context_out,
    gates_out,
    bent_out,
    weights_out,
    window_out,
    upper,
    lower,
    inputs,
    loc_upper,
    loc_lower,
    memory_upper,
    memory_lower,
    query_upper,
    query_lower,
    sums,
    hidden,
    cell,
    context,
    window,
):
    step = pl.program_id(0)
    prenet_width = prenet_ref.shape[1]
    context_width = context.shape[1]
    units = hidden.shape[1]
    width = shard_block * lanes

    @pl.when(step == 0)
    def prepare():
        loc_upper[...], loc_lower[...] = split(loc_map_ref[...])
        memory_upper[...], memory_lower[...] = split(memory_ref[...])
        query_upper[...], query_lower[...] = split(query_ref[...])
        hidden[...] = jnp.zeros_like(hidden)
        cell[...] = jnp.zeros_like(cell)
        context[...] = jnp.zeros_like(context)
        window[...] = jnp.zeros_like(window)

    @pl.when(step < blocks)
    def load():
        store_parts(weight_ref, prenet_width, weight_ref.shape[1], upper, lower, step)
        first = jnp.concatenate([weight_ref[place, :prenet_width, :] for place in range(shard_block)], axis=1)
        first_upper, first_lower = split(first)
        inputs[step] = product(prenet_ref[...], first_upper, first_lower) + bias_ref[0]

    @pl.when(step >= blocks)
    def advance():
        frame = step - blocks
        resume = resume_ref[0]
        hidden_now = hidden[...] * resume
        cell_now = cell[...] * resume
        context_now = context[...] * resume
        window_now = window[...] * resume
        early = pl.multiple_of(frame * rows, rows)
        late = pl.multiple_of((frame + lag) * rows, rows)
        for block in range(blocks):
            taken = slice(block * width, (block + 1) * width)
            sums[:rows, taken] = inputs[block, pl.ds(early, rows), :]
            sums[rows:, taken] = inputs[block, pl.ds(late, rows), :]

        @pl.when(frame > 0)
        def recur():
            state = jnp.concatenate([context_now, hidden_now], axis=1)
            for block in range(blocks):
                taken = slice(block * width, (block + 1) * width)
                sums[:, taken] += product(state, upper[block], lower[block])

        zone_hidden, zone_cell = zone_masks(zone_early_ref, zone_late_ref)
        hidden_new, cell_new, gates = gate_forward(sums[...], cell_now, hidden_now, zone_hidden, zone_cell)
        for place, gate in enumerate(gates):
            gates_out[0, :, place * units : (place + 1) * units] = gate
        hidden[...] = hidden_new
        cell[...] = cell_new
        hidden_out[0] = hidden_new
        cell_out[0] = cell_new
        query = product(hidden_new, query_upper[...], query_lower[...])
        located = product(window_now, loc_upper[...], loc_lower[...])
        energy_v = energy_ref[...]
        lane = lane_index((2 * rows, lanes))
        energy = jnp.zeros((2 * rows, lanes), f32)
        for place in range(positions):
            taken = slice(place * lanes, (place + 1) * lanes)
            ready = processed_ref[:, taken]
            bent = jnp.tanh(query + jnp.concatenate([ready, ready], axis=0) + located[:, taken])
            bent_out[0, :, taken] = bent
            energy = jnp.where(lane == place, jnp.sum(bent * energy_v, axis=1, keepdims=True), energy)
        masked = jnp.where(allowed_ref[...] > 0.5, energy, -1000000000.0)
        exponent = jnp.exp(masked - jnp.max(masked, axis=1, keepdims=True))
        weights = exponent / jnp.sum(exponent, axis=1, keepdims=True)
        weights = jnp.where(lane < positions, weights, 0.0)
        weights_out[0] = weights
        window_out[0] = window_now
        second = (lane >= positions) & (lane < 2 * positions)
        window[...] = weights + pltpu.roll(weights, positions, 1) + jnp.where(second, window_now, 0.0)
        context_new = product(spread(weights, rows, positions), memory_upper[...], memory_lower[...])
        context[...] = context_new
        context_out[0] = context_new


def decoder_forward_kernel(
    blocks,
    rows,
    lag,
    awaited,
    weight_ref,
    frames_ref,
    bias_ref,
    zone_early_ref,
    zone_late_ref,
    resume_ref,
    *refs,
):
    hidden_out, cell_out, gates_out, upper, lower, inputs, sums, hidden, cell = refs[awaited:]
    step = pl.program_id(0)
    units = hidden.shape[1]
    width = shard_block * lanes

    @pl.when(step == 0)
    def prepare():
        hidden[...] = jnp.zeros_like(hidden)
        cell[...] = jnp.zeros_like(cell)

    @pl.when(step < blocks)
    def load():
        split_row = frames_ref.shape[1]
        store_parts(weight_ref, split_row, weight_ref.shape[1], upper, lower, step)
        first = jnp.concatenate([weight_ref[place, :split_row, :] for place in range(shard_block)], axis=1)
        first_upper, first_lower = split(first)
        inputs[step] = product(frames_ref[...], first_upper, first_lower) + bias_ref[0]

    @pl.when(step >= blocks)
    def advance():
        frame = step - blocks
        resume = resume_ref[0]
        hidden_now = hidden[...] * resume
        cell_now = cell[...] * resume
        early = pl.multiple_of(frame * rows, rows)
        late = pl.multiple_of((frame + lag) * rows, rows)
        for block in range(blocks):
            taken = slice(block * width, (block + 1) * width)
            sums[:rows, taken] = inputs[block, pl.ds(early, rows), :]
            sums[rows:, taken] = inputs[block, pl.ds(late, rows), :]

        @pl.when(frame > 0)
        def recur():
            for block in range(blocks):
                taken = slice(block * width, (block + 1) * width)
                sums[:, taken] += product(hidden_now, upper[block], lower[block])

        zone_hidden, zone_cell = zone_masks(zone_early_ref, zone_late_ref)
        hidden_new, cell_new, gates = gate_forward(sums[...], cell_now, hidden_now, zone_hidden, zone_cell)
        for place, gate in enumerate(gates):
            gates_out[0, :, place * units : (place + 1) * units] = gate
        hidden[...] = hidden_new
        cell[...] = cell_new
        hidden_out[0] = hidden_new
        cell_out[0] = cell_new


def add_frames(total_ref, grads, frame, rows, lag):
    early = pl.multiple_of(frame * rows, rows)
    late = pl.multiple_of((frame + lag) * rows, rows)
    total_ref[pl.ds(early, rows), :] += grads[:rows]
    total_ref[pl.ds(late, rows), :] += grads[rows:]


def decoder_backward_kernel(
    blocks,
    rows,
    lag,
    own_parts,
    in_parts,
    awaited,
    *refs,
):
    own_refs = refs[:own_parts]
    in_refs = refs[own_parts : own_parts + in_parts]
    (
        grad_ref,
        gates_ref,
        cell_ref,
        zone_early_ref,
        zone_late_ref,
        resume_ref,
        valid_ref,
    ) = refs[own_parts + in_parts : own_parts + in_parts + 7]
    grad_sums_out, grad_in_out, upper, lower, frame_sums, grad_hidden, grad_cell = refs[
        own_parts + in_parts + 7 + awaited :
    ]
    step = pl.program_id(0)
    units = grad_hidden.shape[1]
    width = shard_block * lanes

    @pl.when(step == 0)
    def prepare():
        grad_hidden[...] = jnp.zeros_like(grad_hidden)
        grad_cell[...] = jnp.zeros_like(grad_cell)
        frame_sums[...] = jnp.zeros_like(frame_sums)
        grad_in_out[...] = jnp.zeros_like(grad_in_out)

    @pl.when(step < blocks)
    def load():
        for which, own_ref in enumerate(own_refs):
            part = own_ref.shape[1]
            for place in range(shard_block):
                taken = slice(place * lanes, (place + 1) * lanes)
                own_upper, own_lower = split(own_ref[place])
                upper[step, which * part : (which + 1) * part, taken] = own_upper
                lower[step, which * part : (which + 1) * part, taken] = own_lower

    @pl.when((step >= blocks) & (step < blocks + span))
    def retreat():
        frame = span - 1 - (step - blocks)
        resume = resume_ref[0]
        early = pl.multiple_of(frame * rows, rows)
        late = pl.multiple_of((frame + lag) * rows, rows)
        arriving = jnp.concatenate([grad_ref[pl.ds(early, rows), :], grad_ref[pl.ds(late, rows), :]], axis=0)
        total = grad_hidden[...] + arriving * valid_ref[0]
        cell_now = cell_ref[0] * jnp.where(frame > 0, resume, 0.0)
        zone_hidden, zone_cell = zone_masks(zone_early_ref, zone_late_ref)
        grad_sums, passed_hidden, passed_cell = gate_backward(
            gates_ref[0], cell_now, zone_hidden, zone_cell, total, grad_cell[...]
        )
        grad_cell[...] = passed_cell * resume
        grad_hidden[...] = passed_hidden
        for place, grads in enumerate(grad_sums):
            for part in range(units // width):
                block = place * (units // width) + part
                add_frames(frame_sums.at[block], grads[:, part * width : (part + 1) * width], frame, rows, lag)

        @pl.when(frame > 0)
        def recur():
            carried = grad_hidden[...]
            for place, grads in enumerate(grad_sums):
                for part in range(units // width):
                    block = place * (units // width) + part
                    taken = grads[:, part * width : (part + 1) * width]
                    carried = carried + product(taken, upper[block], lower[block], transposed=True)
            grad_hidden[...] = carried * resume

    @pl.when(step >= blocks + span)
    def pass_on():
        block = step - blocks - span
        grads = frame_sums[block]
        for place in range(shard_block):
            grad_sums_out[place] = grads[:, place * lanes : (place + 1) * lanes]
        for which, in_ref in enumerate(in_refs):
            part = in_ref.shape[1]
            taken = slice(which * part, (which + 1) * part)
            first = jnp.concatenate([in_ref[place] for place in range(shard_block)], axis=1)
            first_upper, first_lower = split(first)
            grad_in_out[:, taken] += product(grads, first_upper, first_lower, transposed=True)


def attention_backward_kernel(
    blocks,
    rows,
    positions,
    lag,
    weight_ref,
    grad_hidden_ref,
    grad_context_ref,
    gates_ref,
    cell_ref,
    bent_ref,
    weights_ref,
    window_ref,
    loc_map_ref,
    memory_ref,
    query_ref,
    energy_ref,
    zone_early_ref,
    zone_late_ref,
    resume_ref,
    valid_ref,
    next_resume_ref,
    awaited,
    grad_sums_out,
    grad_bias_out,
    grad_prenet_out,
    grad_query_out,
    grad_processed_out,
    grad_memory_out,
    grad_loc_out,
    grad_energy_out,
    upper,
    lower,
    first_upper,
    first_lower,
    frame_sums,
    loc_upper,
    loc_lower,
    memory_upper,
    memory_lower,
    query_upper,
    query_lower,
    grad_bent,
    grad_contexts,
    diagonals,
    windows,
    grad_hidden,
    grad_cell,
    grad_context,
    grad_window,
):
    step = pl.program_id(0)
    units = grad_hidden.shape[1]
    context_width = grad_context.shape[1]
    prenet_width = first_upper.shape[1]
    width = shard_block * lanes
    pair = 2 * rows

    @pl.when(step == 0)
    def prepare():
        loc_upper[...], loc_lower[...] = split(loc_map_ref[...])
        memory_upper[...], memory_lower[...] = split(memory_ref[...])
        query_upper[...], query_lower[...] = split(query_ref[...])
        grad_hidden[...] = jnp.zeros_like(grad_hidden)
        grad_cell[...] = jnp.zeros_like(grad_cell)
        grad_context[...] = jnp.zeros_like(grad_context)
        grad_window[...] = jnp.zeros_like(grad_window)
        frame_sums[...] = jnp.zeros_like(frame_sums)
        grad_query_out[...] = jnp.zeros_like(grad_query_out)
        grad_processed_out[...] = jnp.zeros_like(grad_processed_out)
        grad_energy_out[...] = jnp.zeros_like(grad_energy_out)

    @pl.when(step < blocks)
    def load():
        store_parts(weight_ref, prenet_width, weight_ref.shape[1], upper, lower, step)
        store_parts(weight_ref, 0, prenet_width, first_upper, first_lower, step)

    @pl.when(step >= blocks)
    def retreat():
        frame = span - 1 - (step - blocks)
        resume = resume_ref[0]
        valid = valid_ref[0]
        early = pl.multiple_of(frame * rows, rows)
        late = pl.multiple_of((frame + lag) * rows, rows)
        here = pl.multiple_of(frame * pair, pair)
        lane = lane_index((pair, lanes))
        arriving = jnp.concatenate(
            [grad_context_ref[pl.ds(early, rows), :], grad_context_ref[pl.ds(late, rows), :]], axis=0
        )
        context_total = grad_context[...] + arriving * valid
        grad_contexts[pl.ds(here, pair), :] = context_total
        weights = weights_ref[0]
        diagonals[pl.ds(here, pair), :] = spread(weights, rows, positions)
        windows[pl.ds(here, pair), :] = window_ref[0]
        window_grad = grad_window[...]
        wide = product(context_total, memory_upper[...], memory_lower[...], transposed=True)
        grad_weights = collect(wide, rows, positions) + jnp.where(
            lane < positions, window_grad + pltpu.roll(window_grad, lanes - positions, 1), 0.0
        )
        inner = jnp.sum(weights * grad_weights, axis=1, keepdims=True)
        grad_energy = weights * (grad_weights - inner)
        energy_v = energy_ref[...]
        energy_total = jnp.zeros((pair, lanes), f32)
        query_total = jnp.zeros((pair, lanes), f32)
        for place in range(positions):
            taken = slice(place * lanes, (place + 1) * lanes)
            bent = bent_ref[0, :, taken]
            column = jnp.sum(jnp.where(lane == place, grad_energy, 0.0), axis=1, keepdims=True)
            energy_total = energy_total + column * bent
            slope = column * energy_v * (1.0 - bent * bent)
            query_total = query_total + slope
            grad_bent[pl.ds(here, pair), taken] = slope
            grad_processed_out[:, taken] += slope[:rows] + slope[rows:]
        grad_energy_out[...] += energy_total
        add_frames(grad_query_out, query_total, frame, rows, lag)
        slopes = grad_bent[pl.ds(here, pair), :]
        moved = product(slopes, loc_upper[...], loc_lower[...], transposed=True)
        second = (lane >= positions) & (lane < 2 * positions)
        grad_window[...] = resume * (moved + jnp.where(second, window_grad, 0.0))

        arriving = jnp.concatenate(
            [grad_hidden_ref[pl.ds(early, rows), :], grad_hidden_ref[pl.ds(late, rows), :]], axis=0
        )
        total = grad_hidden[...] + arriving * valid
        total = total + product(query_total, query_upper[...], query_lower[...], transposed=True)
        cell_now = cell_ref[0] * jnp.where(frame > 0, resume, 0.0)
        zone_hidden, zone_cell = zone_masks(zone_early_ref, zone_late_ref)
        grad_sums, passed_hidden, passed_cell = gate_backward(
            gates_ref[0], cell_now, zone_hidden, zone_cell, total, grad_cell[...]
        )
        grad_cell[...] = passed_cell * resume
        for place, grads in enumerate(grad_sums):
            for part in range(units // width):
                block = place * (units // width) + part
                add_frames(frame_sums.at[block], grads[:, part * width : (part + 1) * width], frame, rows, lag)

        @pl.when(frame > 0)
        def recur():
            carried = jnp.zeros((pair, context_width + units), f32)
            for place, grads in enumerate(grad_sums):
                for part in range(units // width):
                    block = place * (units // width) + part
                    taken = grads[:, part * width : (part + 1) * width]
                    carried = carried + product(taken, upper[block], lower[block], transposed=True)
            grad_context[...] = carried[:, :context_width] * resume
            grad_hidden[...] = (carried[:, context_width:] + passed_hidden) * resume

    @pl.when(step == blocks + span - 1)
    def finish():
        prenet_grad = jnp.zeros(grad_prenet_out.shape, f32)
        frame_rows = frame_sums.shape[1]
        for block in range(blocks):
            grads = frame_sums[block]
            prenet_grad = prenet_grad + product(grads, first_upper[block], first_lower[block], transposed=True)
            grad_bias_out[:, block * width : (block + 1) * width] = jnp.sum(grads, axis=0, keepdims=True)
            later = jnp.concatenate([grads[rows:], jnp.zeros((rows, width), f32)], axis=0) * next_resume_ref[...]
            for place in range(shard_block):
                grad_sums_out[block * shard_block + place] = later[:, place * lanes : (place + 1) * lanes]
        grad_prenet_out[...] = prenet_grad
        context_upper, context_lower = split(grad_contexts[...])
        grad_memory_out[...] = product(diagonals[...].T, context_upper, context_lower)
        window_turned = windows[...].T
        for block in range(blocks):
            taken = slice(block * width, (block + 1) * width)
            bent_upper, bent_lower = split(grad_bent[:, taken])
            grad_loc_out[:, taken] = product(window_turned, bent_upper, bent_lower)


def split_kernel(values_ref, upper_ref, lower_ref):
    upper_ref[...], lower_ref[...] = split(values_ref[...])


def split_matrix(values):
    shape = jax.ShapeDtypeStruct(values.shape, bf16)
    return pl.pallas_call(
        split_kernel,
        out_shape=[shape, shape],
        compiler_params=pltpu.CompilerParams(vmem_limit_bytes=vmem_limit),
        name="split_matrix",
    )(values)


def join_kernel(count, *refs):
    out_ref, token_ref = refs[-2:]
    start = 0
    for ref in refs[:count]:
        out_ref[start : start + ref.shape[0]] = ref[...]
        start += ref.shape[0]
    token_ref[...] = jnp.zeros_like(token_ref)


def join_rows(arrays, awaited):
    total = sum(array.shape[0] for array in arrays)
    return pl.pallas_call(
        functools.partial(join_kernel, len(arrays)),
        in_specs=[pl.BlockSpec(memory_space=pltpu.VMEM)] * len(arrays)
        + [pl.BlockSpec(memory_space=pl.ANY)] * len(awaited),
        out_shape=[jax.ShapeDtypeStruct((total, lanes), f32), jax.ShapeDtypeStruct((8, lanes), f32)],
        compiler_params=pltpu.CompilerParams(vmem_limit_bytes=vmem_limit),
        name="join_rows",
    )(*arrays, *awaited)


def pack_sums(*sums):
    rows = []
    for row in sums:
        channels = row.shape[1]
        if channels % lanes:
            row = jnp.concatenate([row, jnp.zeros((1, -channels % lanes), f32)], axis=1)
        rows += [row[:, start : start + lanes] for start in range(0, row.shape[1], lanes)]
    if len(rows) < 8:
        rows.append(jnp.zeros((8 - len(rows), lanes), f32))
    return jnp.concatenate(rows, axis=0)


def unpack_sums(packed, channels, number=2):
    count = -(-channels // lanes)
    rows = []
    for row in range(number):
        pieces = [packed[row * count + place : row * count + place + 1] for place in range(count)]
        rows.append(jnp.concatenate(pieces, axis=1)[:, :channels])
    return rows


def moved_rows(values, shift):
    if shift > 0:
        return jnp.concatenate([jnp.zeros((shift, values.shape[1]), f32), values[:-shift]], axis=0)
    if shift < 0:
        return jnp.concatenate([values[-shift:], jnp.zeros((-shift, values.shape[1]), f32)], axis=0)
    return values


def convolve(values, same, upper_ref, lower_ref, rows):
    kernel = upper_ref.shape[0] // values.shape[1]
    channels = values.shape[1]
    total = None
    for tap in range(kernel):
        taken = slice(tap * channels, (tap + 1) * channels)
        moved = moved_rows(values, (kernel // 2 - tap) * rows) * same[:, tap : tap + 1]
        piece = product(moved, upper_ref[taken, :], lower_ref[taken, :])
        total = piece if total is None else total + piece
    return total


def send_sums(copies_ref, *values):
    packed = pack_sums(*[jnp.sum(value, axis=0, keepdims=True) for value in values])
    for place in range(copies_ref.shape[0]):
        copies_ref[place] = packed


def post_first_kernel(rows, values_ref, same_ref, upper_ref, lower_ref, conv_out, copies_out):
    conv = convolve(values_ref[...], same_ref[...], upper_ref, lower_ref, rows)
    conv_out[...] = conv
    send_sums(copies_out, conv, conv * conv)


def post_next_kernel(
    rows,
    frame_count,
    conv_ref,
    sums_ref,
    gain_ref,
    shift_ref,
    same_ref,
    upper_ref,
    lower_ref,
    *refs,
):
    *grad_refs, scaled_out, active_out, inverse_out, conv_out, copies_out = refs
    conv = conv_ref[...]
    first, second = unpack_sums(jnp.sum(sums_ref[...], axis=0), conv.shape[1])
    average = first / frame_count
    inverse = lax.rsqrt(second / frame_count - average * average + norm_eps)
    scaled = (conv - average) * inverse
    active = jnp.tanh(scaled * gain_ref[...] + shift_ref[...])
    scaled_out[...] = scaled
    active_out[...] = active
    inverse_out[...] = inverse
    conv = convolve(active, same_ref[...], upper_ref, lower_ref, rows)
    conv_out[...] = conv
    grads = [piece for ref in grad_refs for piece in (ref[...], ref[...] * conv)]
    send_sums(copies_out, conv, conv * conv, *grads)


def conv_back(grad_conv, same, upper_ref, lower_ref, channels, rows):
    kernel = upper_ref.shape[0] // channels
    total = None
    for tap in range(kernel):
        taken = slice(tap * channels, (tap + 1) * channels)
        piece = product(grad_conv, upper_ref[taken, :], lower_ref[taken, :], transposed=True)
        piece = moved_rows(piece * same[:, tap : tap + 1], (tap - kernel // 2) * rows)
        total = piece if total is None else total + piece
    return total


def post_turn_kernel(
    rows,
    frame_count,
    grad_ref,
    conv_ref,
    sums_ref,
    before_ref,
    gain_ref,
    shift_ref,
    same_ref,
    upper_ref,
    lower_ref,
    active_ref,
    scaled_below_ref,
    after_out,
    conv_out,
    sums_out,
    grad_out,
    copies_out,
):
    conv = conv_ref[...]
    grad = grad_ref[...]
    gain = gain_ref[...]
    first, second, shift_grad, mixed = unpack_sums(jnp.sum(sums_ref[...], axis=0), conv.shape[1], 4)
    average = first / frame_count
    inverse = lax.rsqrt(second / frame_count - average * average + norm_eps)
    scaled = (conv - average) * inverse
    after_out[...] = before_ref[...] + scaled * gain + shift_ref[...]
    gain_grad = inverse * (mixed - average * shift_grad)
    sums_out[...] = pack_sums(shift_grad, gain_grad)
    grad_conv = inverse * gain * (grad - (shift_grad + scaled * gain_grad) / frame_count)
    conv_out[...] = jnp.concatenate([grad_conv, jnp.zeros((conv.shape[0], -conv.shape[1] % lanes), f32)], axis=1)
    active = active_ref[...]
    total = conv_back(grad_conv, same_ref[...], upper_ref, lower_ref, active.shape[1], rows)
    total = total * (1.0 - active * active)
    send_sums(copies_out, total, total * scaled_below_ref[...])
    grad_out[...] = total


def post_back_kernel(
    rows,
    frame_count,
    has_lower,
    awaited,
    grad_ref,
    scaled_ref,
    sums_ref,
    inverse_ref,
    gain_ref,
    same_ref,
    upper_ref,
    lower_ref,
    *refs,
):
    if has_lower:
        active_ref, scaled_below_ref = refs[:2]
        conv_out, sums_out, grad_out, copies_out = refs[2 + awaited :]
    else:
        conv_out, sums_out, grad_out = refs[awaited:]
    grad = grad_ref[...]
    scaled = scaled_ref[...]
    same = same_ref[...]
    packed = jnp.sum(sums_ref[...], axis=0)
    sums_out[...] = packed
    shift_grad, gain_grad = unpack_sums(packed, grad.shape[1])
    grad_conv = inverse_ref[...] * gain_ref[...] * (grad - (shift_grad + scaled * gain_grad) / frame_count)
    conv_out[...] = grad_conv
    total = conv_back(grad_conv, same, upper_ref, lower_ref, grad_out.shape[1], rows)
    if has_lower:
        active = active_ref[...]
        total = total * (1.0 - active * active)
        send_sums(copies_out, total, total * scaled_below_ref[...])
    grad_out[...] = total


def post_call(kernel, outs, name, operands, awaited=()):
    shapes = [jax.ShapeDtypeStruct(shape, f32) for shape in outs]
    in_specs = [pl.BlockSpec(memory_space=pltpu.VMEM)] * len(operands)
    in_specs += [pl.BlockSpec(memory_space=pl.ANY)] * len(awaited)
    return pl.pallas_call(
        kernel,
        in_specs=in_specs,
        out_specs=[pl.BlockSpec(memory_space=pltpu.VMEM)] * len(outs),
        out_shape=shapes,
        compiler_params=pltpu.CompilerParams(vmem_limit_bytes=vmem_limit),
        name=name,
    )(*operands, *awaited)


def share_sums(copies):
    return lax.all_to_all(copies, both, 0, 0)


def tap_gradient_kernel(rows, inputs_ref, grads_ref, same_ref, out_ref):
    groups, frame_rows, columns = grads_ref.shape
    kernel = out_ref.shape[0]
    margin = kernel // 2
    moved = []
    for tap in range(kernel):
        pieces = []
        for group in range(groups):
            masked = grads_ref[group] * same_ref[group][:, tap : tap + 1]
            pieces.append(moved_rows(masked, (tap - margin) * rows))
        moved.append(jnp.concatenate(pieces, axis=0))
    upper, lower = split(jnp.concatenate(moved, axis=1))
    inputs = inputs_ref[...].reshape(groups * frame_rows, -1)
    result = product(inputs.T, upper, lower)
    for tap in range(kernel):
        out_ref[tap] = result[:, tap * columns : (tap + 1) * columns]


def tap_gradient(inputs, grads, same_segment, kernel, rows):
    out = jax.ShapeDtypeStruct((kernel, inputs.shape[2], grads.shape[2]), f32)
    return pl.pallas_call(
        functools.partial(tap_gradient_kernel, rows),
        out_shape=out,
        compiler_params=pltpu.CompilerParams(vmem_limit_bytes=vmem_limit),
        name="tap_gradient",
    )(inputs, grads, same_segment)


def frame_product_kernel(pieces, *refs):
    inputs = refs[:-3]
    grads_ref, out_ref, total = refs[-3:]
    step = pl.program_id(0)

    @pl.when(step == 0)
    def prepare():
        total[...] = jnp.zeros_like(total)

    blocks, groups = grads_ref.shape[:2]
    grads = jnp.concatenate(
        [jnp.concatenate([grads_ref[block, group] for group in range(groups)], axis=1) for block in range(blocks)],
        axis=0,
    )
    columns = grads.shape[1]
    turned_upper, turned_lower = split(grads.T)
    stacked = jnp.concatenate([turned_upper, turned_lower], axis=0)
    start = 0
    for which, first, last in pieces:
        upper, lower = split(inputs[which][:, first:last])
        one = jnp.dot(stacked, upper, preferred_element_type=f32)
        two = jnp.dot(turned_upper, lower, preferred_element_type=f32)
        total[:, start : start + last - first] += one[:columns] + one[columns:] + two
        start += last - first

    @pl.when(step == pl.num_programs(0) - 1)
    def finish():
        parts, _, width = out_ref.shape
        for part in range(parts):
            out_ref[part] = total[part * width : (part + 1) * width].T


def frame_product(inputs, grads, pieces):
    sources, groups, frames = grads.shape[:3]
    parts = lax.axis_size("section")
    block = 4 if sources % 4 == 0 else 1
    columns = groups // parts * lanes
    depth = sum(last - first for _, first, last in pieces)

    def block_spec(array):
        return pl.BlockSpec((block * frames, array.shape[1]), lambda step: (step, 0))

    return pl.pallas_call(
        functools.partial(frame_product_kernel, pieces),
        grid=(sources // block,),
        in_specs=[block_spec(array) for array in inputs]
        + [pl.BlockSpec((block, groups, frames, lanes), lambda step: (step, 0, 0, 0))],
        out_specs=pl.BlockSpec((parts, depth, columns), lambda step: (0, 0, 0)),
        out_shape=jax.ShapeDtypeStruct((parts, depth, columns), f32),
        scratch_shapes=[pltpu.VMEM((parts * columns, depth), f32)],
        compiler_params=params(),
        name="frame_product",
    )(*inputs, grads)


def whole_spec(array):
    rank = len(array.shape)
    return pl.BlockSpec(array.shape, lambda step: (0,) * rank)


def timed_spec(array, place, depth=None):
    shape = (1,) + tuple(array.shape[1:])
    rank = len(array.shape)
    return pl.BlockSpec(shape, lambda step: (place(step),) + (0,) * (rank - 1))


def shard_spec(array, place):
    shape = (shard_block,) + tuple(array.shape[1:])
    return pl.BlockSpec(shape, lambda step: (place(step), 0, 0))


def zone_spec(zone, place, which):
    shape = (1, 2) + tuple(zone.shape[2:])
    return pl.BlockSpec(shape, lambda step: (place(step), which, 0, 0))


def out_spec(shape):
    rank = len(shape)
    return pl.BlockSpec(shape, lambda step: (0,) * rank)


def cost(weights, passes):
    return pl.CostEstimate(flops=2 * 256 * weights * 2 * passes, bytes_accessed=4 * weights, transcendentals=0)


def params():
    return pltpu.CompilerParams(vmem_limit_bytes=vmem_limit, dimension_semantics=("arbitrary",))


def attention_forward(
    weight, prenet_out, bias, loc_map, processed, memory, query_weight, energy_v, zone, resume, allowed, lag, awaited
):
    groups, depth = weight.shape[:2]
    blocks = groups // shard_block
    rows = memory.shape[0] // (processed.shape[1] // lanes)
    positions = processed.shape[1] // lanes
    columns = groups * lanes
    units = columns // 4
    context_width = memory.shape[1]
    frame_rows = prenet_out.shape[0]
    rest = depth - prenet_out.shape[1]
    width = shard_block * lanes
    pair = 2 * rows

    def shard(step):
        return jnp.minimum(step, blocks - 1)

    def timed(step):
        return jnp.clip(step - blocks, 0, span - 1)

    def later(step):
        return timed(step) + lag

    timed_shapes = [
        (span, pair, units),
        (span, pair, units),
        (span, pair, context_width),
        (span, pair, columns),
        (span, pair, positions * lanes),
        (span, pair, lanes),
        (span, pair, lanes),
    ]
    out_shape = [jax.ShapeDtypeStruct(shape, f32) for shape in timed_shapes]
    bias_blocks = bias.reshape(blocks, 1, width)
    return pl.pallas_call(
        functools.partial(attention_forward_kernel, blocks, rows, positions, lag),
        grid=(blocks + span,),
        in_specs=[
            shard_spec(weight, shard),
            whole_spec(prenet_out),
            timed_spec(bias_blocks, shard),
            whole_spec(loc_map),
            whole_spec(processed),
            whole_spec(memory),
            whole_spec(query_weight),
            whole_spec(energy_v),
            zone_spec(zone, timed, 0),
            zone_spec(zone, later, 0),
            timed_spec(resume, timed),
            whole_spec(allowed),
            pl.BlockSpec(memory_space=pl.ANY),
        ],
        out_specs=[timed_spec(shape, timed) for shape in out_shape],
        out_shape=out_shape,
        scratch_shapes=[
            pltpu.VMEM((blocks, rest, width), bf16),
            pltpu.VMEM((blocks, rest, width), bf16),
            pltpu.VMEM((blocks, frame_rows, width), f32),
            pltpu.VMEM(loc_map.shape, bf16),
            pltpu.VMEM(loc_map.shape, bf16),
            pltpu.VMEM(memory.shape, bf16),
            pltpu.VMEM(memory.shape, bf16),
            pltpu.VMEM(query_weight.shape, bf16),
            pltpu.VMEM(query_weight.shape, bf16),
            pltpu.VMEM((pair, columns), f32),
            pltpu.VMEM((pair, units), f32),
            pltpu.VMEM((pair, units), f32),
            pltpu.VMEM((pair, context_width), f32),
            pltpu.VMEM((pair, lanes), f32),
        ],
        compiler_params=params(),
        cost_estimate=cost(depth * columns, span),
        name="attention_forward",
    )(
        weight,
        prenet_out,
        bias_blocks,
        loc_map,
        processed,
        memory,
        query_weight,
        energy_v,
        zone,
        zone,
        resume,
        allowed,
        awaited,
    )


def decoder_forward(weight, frames, bias, zone, resume, rows, lag, awaited):
    groups = weight.shape[0]
    blocks = groups // shard_block
    columns = groups * lanes
    units = columns // 4
    width = shard_block * lanes
    pair = 2 * rows

    def shard(step):
        return jnp.minimum(step, blocks - 1)

    def timed(step):
        return jnp.clip(step - blocks, 0, span - 1)

    def later(step):
        return timed(step) + lag

    timed_shapes = [(span, pair, units), (span, pair, units), (span, pair, columns)]
    out_shape = [jax.ShapeDtypeStruct(shape, f32) for shape in timed_shapes]
    bias_blocks = bias.reshape(blocks, 1, width)
    return pl.pallas_call(
        functools.partial(decoder_forward_kernel, blocks, rows, lag, len(awaited)),
        grid=(blocks + span,),
        in_specs=[
            shard_spec(weight, shard),
            whole_spec(frames),
            timed_spec(bias_blocks, shard),
            zone_spec(zone, timed, 1),
            zone_spec(zone, later, 1),
            timed_spec(resume, timed),
        ]
        + [pl.BlockSpec(memory_space=pl.ANY)] * len(awaited),
        out_specs=[timed_spec(shape, timed) for shape in out_shape],
        out_shape=out_shape,
        scratch_shapes=[
            pltpu.VMEM((blocks, units, width), bf16),
            pltpu.VMEM((blocks, units, width), bf16),
            pltpu.VMEM((blocks, frames.shape[0], width), f32),
            pltpu.VMEM((pair, columns), f32),
            pltpu.VMEM((pair, units), f32),
            pltpu.VMEM((pair, units), f32),
        ],
        compiler_params=params(),
        cost_estimate=cost(weight.shape[1] * columns, span // 2),
        name="decoder_forward",
    )(weight, frames, bias_blocks, zone, zone, resume, *awaited)


def decoder_backward(weight, grad, gates, cells, zone, resume, valid, rows, lag, awaited):
    groups, depth = weight.shape[:2]
    blocks = groups // shard_block
    columns = groups * lanes
    units = columns // 4
    split_row = depth - units
    width = shard_block * lanes
    pair = 2 * rows
    frame_rows = grad.shape[0]
    part = math.gcd(units, split_row)
    own_parts = units // part
    in_parts = split_row // part

    def part_spec(index):
        return pl.BlockSpec((shard_block, part, lanes), index)

    def own_spec(which):
        return part_spec(lambda step: (shard(step), in_parts + which, 0))

    def in_spec(which):
        return part_spec(lambda step: (last_shard(step), which, 0))

    def shard(step):
        return jnp.minimum(step, blocks - 1)

    def last_shard(step):
        return jnp.clip(step - blocks - span, 0, blocks - 1)

    def timed(step):
        return span - 1 - jnp.clip(step - blocks, 0, span - 1)

    def later(step):
        return timed(step) + lag

    def before(step):
        return jnp.maximum(timed(step) - 1, 0)

    out_shape = [
        jax.ShapeDtypeStruct((groups, frame_rows, lanes), f32),
        jax.ShapeDtypeStruct((frame_rows, split_row), f32),
    ]
    return pl.pallas_call(
        functools.partial(decoder_backward_kernel, blocks, rows, lag, own_parts, in_parts, len(awaited)),
        grid=(2 * blocks + span,),
        in_specs=[own_spec(which) for which in range(own_parts)]
        + [in_spec(which) for which in range(in_parts)]
        + [
            whole_spec(grad),
            timed_spec(gates, timed),
            timed_spec(cells, before),
            zone_spec(zone, timed, 1),
            zone_spec(zone, later, 1),
            timed_spec(resume, timed),
            timed_spec(valid, timed),
        ]
        + [pl.BlockSpec(memory_space=pl.ANY)] * len(awaited),
        out_specs=[shard_spec(out_shape[0], last_shard), whole_spec(out_shape[1])],
        out_shape=out_shape,
        scratch_shapes=[
            pltpu.VMEM((blocks, units, width), bf16),
            pltpu.VMEM((blocks, units, width), bf16),
            pltpu.VMEM((blocks, frame_rows, width), f32),
            pltpu.VMEM((pair, units), f32),
            pltpu.VMEM((pair, units), f32),
        ],
        compiler_params=params(),
        cost_estimate=cost(depth * columns, 4 * span),
        name="decoder_backward",
    )(*[weight] * (own_parts + in_parts), grad, gates, cells, zone, zone, resume, valid, *awaited)


def attention_backward(
    weight,
    grad_hidden,
    grad_context,
    gates,
    cells,
    bent,
    weights,
    window,
    loc_map,
    memory,
    query_weight,
    energy_v,
    zone,
    resume,
    valid,
    next_resume,
    rows,
    positions,
    prenet_width,
    lag,
    awaited,
):
    groups, depth = weight.shape[:2]
    blocks = groups // shard_block
    columns = groups * lanes
    units = columns // 4
    width = shard_block * lanes
    pair = 2 * rows
    frame_rows = grad_hidden.shape[0]
    context_width = grad_context.shape[1]
    rest = depth - prenet_width

    def shard(step):
        return jnp.minimum(step, blocks - 1)

    def timed(step):
        return span - 1 - jnp.clip(step - blocks, 0, span - 1)

    def later(step):
        return timed(step) + lag

    def before(step):
        return jnp.maximum(timed(step) - 1, 0)

    shapes = [
        (groups, frame_rows, lanes),
        (1, columns),
        (frame_rows, prenet_width),
        (frame_rows, lanes),
        (rows, positions * lanes),
        (rows * positions, context_width),
        loc_map.shape,
        (pair, lanes),
    ]
    return pl.pallas_call(
        functools.partial(attention_backward_kernel, blocks, rows, positions, lag),
        grid=(blocks + span,),
        in_specs=[
            shard_spec(weight, shard),
            whole_spec(grad_hidden),
            whole_spec(grad_context),
            timed_spec(gates, timed),
            timed_spec(cells, before),
            timed_spec(bent, timed),
            timed_spec(weights, timed),
            timed_spec(window, timed),
            whole_spec(loc_map),
            whole_spec(memory),
            whole_spec(query_weight),
            whole_spec(energy_v),
            zone_spec(zone, timed, 0),
            zone_spec(zone, later, 0),
            timed_spec(resume, timed),
            timed_spec(valid, timed),
            whole_spec(next_resume),
        ]
        + [pl.BlockSpec(memory_space=pl.ANY)] * len(awaited),
        out_specs=[out_spec(shape) for shape in shapes],
        out_shape=[jax.ShapeDtypeStruct(shape, f32) for shape in shapes],
        scratch_shapes=[
            pltpu.VMEM((blocks, rest, width), bf16),
            pltpu.VMEM((blocks, rest, width), bf16),
            pltpu.VMEM((blocks, prenet_width, width), bf16),
            pltpu.VMEM((blocks, prenet_width, width), bf16),
            pltpu.VMEM((blocks, frame_rows, width), f32),
            pltpu.VMEM(loc_map.shape, bf16),
            pltpu.VMEM(loc_map.shape, bf16),
            pltpu.VMEM(memory.shape, bf16),
            pltpu.VMEM(memory.shape, bf16),
            pltpu.VMEM(query_weight.shape, bf16),
            pltpu.VMEM(query_weight.shape, bf16),
            pltpu.VMEM((span * pair, positions * lanes), f32),
            pltpu.VMEM((span * pair, context_width), f32),
            pltpu.VMEM((span * pair, rows * positions), f32),
            pltpu.VMEM((span * pair, lanes), f32),
            pltpu.VMEM((pair, units), f32),
            pltpu.VMEM((pair, units), f32),
            pltpu.VMEM((pair, context_width), f32),
            pltpu.VMEM((pair, lanes), f32),
        ],
        compiler_params=params(),
        cost_estimate=cost(lanes * lanes, 1),
        name="attention_backward",
    )(
        weight,
        grad_hidden,
        grad_context,
        gates,
        cells,
        bent,
        weights,
        window,
        loc_map,
        memory,
        query_weight,
        energy_v,
        zone,
        zone,
        resume,
        valid,
        next_resume,
        *awaited,
    )


def dot(left, right, left_dim=1, right_dim=0):
    return lax.dot_general(
        left, right, (((left_dim,), (right_dim,)), ((), ())), precision=high, preferred_element_type=f32
    )


def gather_columns(shard):
    depth, width = shard.shape
    if width % lanes:
        full = lax.all_gather(shard, both, axis=1, tiled=True)
        return full.reshape(depth, -1, lanes).swapaxes(0, 1)
    stacked = lax.all_gather(shard, both, axis=0)
    if width == lanes:
        return stacked
    return stacked.reshape(-1, depth, width // lanes, lanes).swapaxes(1, 2).reshape(-1, depth, lanes)


def along_core(values):
    return lax.ppermute(values, "section", [(place, place ^ 1) for place in range(4)])


def along_y(values):
    return lax.ppermute(values, "section", [(place, place ^ 2) for place in range(4)])


def gather_y(values):
    return jnp.stack([values, along_y(values)])


def gather_core(two):
    return jnp.concatenate([two, along_core(two)], axis=0)


def gather_section(values):
    return gather_core(gather_y(values))


def section_order(four, own):
    entries = []
    for place in range(4):
        offset = own ^ place
        held = (offset % 2) * 2 + offset // 2
        entries.append(lax.dynamic_index_in_dim(four, held, 0, keepdims=False))
    return entries


def section_columns(pair, layers):
    own = lax.axis_index("section")
    four = gather_core(pair)
    depth = four.shape[1] // layers
    whole = []
    for layer in range(layers):
        blocks = section_order(four[:, layer * depth : (layer + 1) * depth], own)
        whole.append(jnp.concatenate(blocks, axis=1))
    return whole


def own_columns(values, columns):
    own = lax.axis_index("section")
    total = values[..., :columns]
    for place in range(1, values.shape[-1] // columns):
        total = jnp.where(own == place, values[..., place * columns : (place + 1) * columns], total)
    return total


def flat_join(arrays, devices):
    pieces = []
    for array in arrays:
        flat = array.reshape(-1)
        flat = jnp.pad(flat, (0, -flat.shape[0] % lanes))
        pieces.append(flat.reshape(-1, lanes))
    joined = jnp.concatenate(pieces, axis=0)
    joined = jnp.pad(joined, ((0, -joined.shape[0] % (8 * devices)), (0, 0)))
    return joined.reshape(devices, -1, lanes)


def part_sum(joined):
    return jnp.sum(lax.all_to_all(joined, both, 0, 0), axis=0)


def flat_whole(part, devices):
    return lax.all_to_all(jnp.broadcast_to(part[None], (devices,) + part.shape), both, 0, 0)


def flat_split(whole, arrays):
    whole = whole.reshape(-1, lanes)
    sums = []
    start = 0
    for array in arrays:
        count = -(-array.size // lanes)
        flat = whole[start : start + count].reshape(-1)
        sums.append(flat[: array.size].reshape(array.shape))
        start += count
    return sums


def exchange_ring(grads, extra=None):
    groups, frames, width = grads.shape
    size = lax.axis_size("dp")
    if extra is None:
        return lax.all_to_all(grads.reshape(size, groups // size, frames, width), "dp", 0, 0)
    joined = jnp.concatenate([grads.reshape(size, -1, width), extra], axis=1)
    received = lax.all_to_all(joined, "dp", 0, 0)
    count = groups // size * frames
    return received[:, :count].reshape(size, -1, frames, width), jnp.sum(received[:, count:], axis=0)


def sum_section(parts):
    own = lax.axis_index("section")
    core, place = own % 2, own // 2
    pairs = parts.reshape((2, 2) + parts.shape[1:])
    mine = jnp.where(core == 0, pairs[:, 0], pairs[:, 1])
    other = jnp.where(core == 0, pairs[:, 1], pairs[:, 0])
    pair = mine + along_core(other)
    mine = jnp.where(place == 0, pair[0], pair[1])
    other = jnp.where(place == 0, pair[1], pair[0])
    return mine + along_y(other)


def gathers_inputs(frame_rows, columns, devices):
    return frame_rows * devices <= columns


def column_gradients(inputs, pieces, received, grads):
    if received is not None:
        return sum_section(frame_product(inputs, received, pieces))
    groups, frames, width = grads.shape
    flat = grads.swapaxes(0, 1).reshape(frames, groups * width)
    parts = [
        lax.psum_scatter(dot(inputs[which][:, first:last], flat, 0, 0), both, scatter_dimension=1, tiled=True)
        for which, first, last in pieces
    ]
    return jnp.concatenate(parts, axis=0)


def gelu_slope(values):
    return jax.vjp(jax.nn.gelu, values)


def location_map(loc_filters, loc_dense, positions):
    filters, channels, taps = loc_filters.shape
    features = loc_dense.shape[1]
    joined = dot(loc_filters.reshape(filters, channels * taps), loc_dense, 0, 0)
    joined = joined.reshape(channels, taps, features)
    margin = taps // 2
    padded = jnp.pad(joined, ((0, 0), (positions, positions), (0, 0)))
    columns = [
        padded[:, positions + margin - place : 2 * positions + margin - place] for place in range(positions)
    ]
    spread_map = jnp.stack(columns, axis=2).reshape(channels * positions, positions * features)
    return jnp.pad(spread_map, ((0, lanes - channels * positions), (0, 0)))


def location_unmap(grad_map, channels, taps, positions, features):
    grads = grad_map[: channels * positions].reshape(channels, positions, positions, features)
    turned = jnp.flip(grads.swapaxes(1, 2), axis=1)
    padded = jnp.pad(turned, ((0, 0), (0, 0), (0, positions), (0, 0))).reshape(channels, -1, features)
    length = 2 * positions - 1
    skewed = padded[:, : positions * length].reshape(channels, positions, length, features)
    start = positions - 1 - taps // 2
    return jnp.sum(skewed[:, :, start : start + taps], axis=1)


def per_device(
    memory,
    enc_lengths,
    frame_segment,
    mel_target,
    prenet_keep,
    zone_keep,
    pre_first,
    pre_second,
    att_weight,
    att_bias,
    query_weight,
    memory_weight,
    loc_filters,
    loc_dense,
    energy_v,
    dec_weight,
    dec_bias,
    proj_weight,
    proj_bias,
    stop_weight,
    post_first,
    post_mid,
    post_last,
    norm_gain,
    norm_shift,
    last_gain,
    last_shift,
    grad_after,
    grad_stop,
):
    devices = lax.axis_size("dp") * lax.axis_size("section")
    rows, positions, context_width = memory.shape
    frames = frame_segment.shape[1]
    mel = mel_target.shape[2]
    units = att_bias.shape[0] // 4
    prenet_width = pre_first.shape[1]
    features = memory_weight.shape[1]
    lag = frames - span
    frame_rows = frames * rows

    att_all = gather_columns(att_weight)
    dec_all = gather_columns(dec_weight)
    mid_pair = gather_y(post_mid.reshape(-1, post_mid.shape[3]))
    mid_all = section_columns(mid_pair, 3)
    post_split = [split_matrix(weight.reshape(-1, weight.shape[-1])) for weight in [post_first] + mid_all + [post_last]]

    segment = frame_segment.T
    earlier = jnp.concatenate([segment[:1] - 1, segment[:-1]], axis=0)
    resume = (segment == earlier).astype(f32)
    shifted = jnp.concatenate([jnp.zeros_like(mel_target[:, :1]), mel_target[:, :-1]], axis=1)
    frames_in = (shifted.swapaxes(0, 1) * resume[:, :, None]).reshape(frame_rows, mel)
    keep = prenet_keep.transpose(1, 2, 0, 3).astype(f32) * 2.0
    keep_first = keep[:, 0].reshape(frame_rows, prenet_width)
    keep_second = keep[:, 1].reshape(frame_rows, prenet_width)
    gelu_first, first_back = gelu_slope(dot(frames_in, pre_first))
    pre_hidden = gelu_first * keep_first
    gelu_second, second_back = gelu_slope(dot(pre_hidden, pre_second))
    prenet_out = gelu_second * keep_second
    memory_flat = memory.reshape(rows * positions, context_width)
    processed = dot(memory_flat, memory_weight)
    loc_map = location_map(loc_filters, loc_dense, positions)
    zone = zone_keep.transpose(1, 2, 0, 3)

    first_part = segment == 0
    steps = jnp.arange(span)
    never = jnp.ones((span, rows), f32)
    resume_pair = jnp.concatenate([never, resume[lag:]], axis=1)[:, :, None]
    valid_pair = jnp.concatenate([first_part[:span], ~first_part[lag:]], axis=1).astype(f32)[:, :, None]
    encoder_first = jnp.arange(lanes)[None, :] < enc_lengths[:, :1]
    inside = jnp.arange(lanes)[None, :] < positions
    allowed = jnp.concatenate([encoder_first, inside & ~encoder_first], axis=0).astype(f32)
    next_resume = jnp.concatenate([resume[1:], jnp.zeros((1, rows), f32)], axis=0).reshape(frame_rows, 1)

    def to_frames(pairs):
        early = jnp.pad(pairs[:, :rows], ((0, lag), (0, 0), (0, 0)))
        late = jnp.pad(pairs[:, rows:], ((lag, 0), (0, 0), (0, 0)))
        return jnp.where(first_part[:, :, None], early, late).reshape(frame_rows, -1)

    energy_row = energy_v.reshape(1, features)
    processed_wide = processed.reshape(rows, positions * features)
    hidden, cells, contexts, gates, bent, weights, window = attention_forward(
        att_all,
        prenet_out,
        att_bias,
        loc_map,
        processed_wide,
        memory_flat,
        query_weight,
        energy_row,
        zone,
        resume_pair,
        allowed,
        lag,
        mid_pair,
    )
    att_frames = to_frames(hidden)
    context_frames = to_frames(contexts)
    dec_inputs = jnp.concatenate([att_frames, context_frames], axis=1)
    dec_hidden, dec_cells, dec_gates = decoder_forward(
        dec_all, dec_inputs, dec_bias, zone, resume_pair, rows, lag, [part for pair in post_split for part in pair]
    )
    dec_frames = to_frames(dec_hidden)

    prenet_later = jnp.concatenate([prenet_out[rows:], jnp.zeros((rows, prenet_width), f32)], axis=0)
    att_inputs_all = jnp.concatenate([prenet_later, context_frames, att_frames], axis=1)
    dec_earlier = jnp.concatenate([jnp.zeros((rows, units), f32), dec_frames[:-rows]], axis=0)
    dec_earlier = dec_earlier * resume.reshape(frame_rows, 1)
    dec_inputs_all = dec_earlier
    input_width = att_inputs_all.shape[1]
    input_pieces = []
    rings = gathers_inputs(frame_rows, 4 * units, devices)
    if rings:
        att_inputs_all = lax.all_gather(att_inputs_all, "dp", axis=0, tiled=True)
        dec_inputs_all = lax.all_gather(dec_inputs_all, "dp", axis=0, tiled=True)
        input_pieces = [att_inputs_all, dec_inputs_all]

    out_frames = jnp.concatenate([dec_frames, context_frames], axis=1)
    mel_before = dot(out_frames, proj_weight) + proj_bias
    stop_logit = jnp.sum(out_frames * stop_weight, axis=1).reshape(frames, rows).T

    section_size = lax.axis_size("section")
    kernel = post_first.shape[0]
    margin = kernel // 2
    padded = jnp.pad(segment, ((margin, margin), (0, 0)), constant_values=-1)
    same_segment = jnp.stack(
        [padded[offset : offset + frames] == segment for offset in range(kernel)], axis=2
    ).astype(f32)
    same = jnp.pad(same_segment, ((0, 0), (0, 0), (0, 8 - kernel))).reshape(frame_rows, 8)
    same_all = gather_section(same)
    frame_count = frame_rows * devices
    gains = [norm_gain[layer : layer + 1] for layer in range(4)] + [last_gain.reshape(1, mel)]
    shifts = [norm_shift[layer : layer + 1] for layer in range(4)] + [last_shift.reshape(1, mel)]
    widths = [post_first.shape[2]] * 4 + [mel]
    grad_after_frames = grad_after.swapaxes(0, 1).reshape(frame_rows, mel)
    conv, copies = post_call(
        functools.partial(post_first_kernel, rows),
        [(frame_rows, widths[0]), (devices, 8, lanes)],
        "post_first",
        (mel_before, same, *post_split[0]),
    )
    scaled, inverse, active, inputs_all = [], [], [], []
    inputs_all.append(gather_section(jnp.pad(mel_before, ((0, 0), (0, lanes - mel)))))
    for layer in range(4):
        scaled_now, active_now, inverse_now, conv, copies = post_call(
            functools.partial(post_next_kernel, rows, frame_count),
            [
                (frame_rows, widths[layer]),
                (frame_rows, widths[layer]),
                (1, widths[layer]),
                (frame_rows, widths[layer + 1]),
                (devices, 8, lanes),
            ],
            "post_next",
            (conv, share_sums(copies), gains[layer], shifts[layer], same, *post_split[layer + 1])
            + ((grad_after_frames,) if layer == 3 else ()),
        )
        scaled.append(scaled_now)
        active.append(active_now)
        inverse.append(inverse_now)
        inputs_all.append(gather_section(active_now))
    mel_after, grad_conv, packed, upstream, copies = post_call(
        functools.partial(post_turn_kernel, rows, frame_count),
        [(frame_rows, mel), (frame_rows, lanes), (8, lanes), (frame_rows, widths[3]), (devices, 8, lanes)],
        "post_turn",
        (
            grad_after_frames,
            conv,
            share_sums(copies),
            mel_before,
            gains[4],
            shifts[4],
            same,
            *post_split[4],
            active[3],
            scaled[3],
        ),
    )
    weight_grads = [None] * 5
    gain_grads = [None] * 5
    shift_grads = [None] * 5
    shift_grads[4], gain_grads[4] = [row.reshape(-1) for row in unpack_sums(packed, mel)]
    weight_grads[4] = tap_gradient(
        own_columns(inputs_all[4], inputs_all[4].shape[2] // section_size),
        gather_section(grad_conv),
        same_all,
        kernel,
        rows,
    )
    for layer in reversed(range(4)):
        below = (active[layer - 1], scaled[layer - 1]) if layer else ()
        awaited = (weight_grads[layer + 2],) if layer < 3 else ()
        outs = [(frame_rows, widths[layer]), (8, lanes), (frame_rows, widths[layer - 1] if layer else mel)]
        if layer:
            outs.append((devices, 8, lanes))
        results = post_call(
            functools.partial(post_back_kernel, rows, frame_count, layer > 0, len(awaited)),
            outs,
            "post_back",
            (
                upstream,
                scaled[layer],
                share_sums(copies),
                inverse[layer],
                gains[layer],
                same,
                *post_split[layer],
                *below,
            ),
            awaited,
        )
        grad_conv, packed, upstream = results[:3]
        if layer:
            copies = results[3]
        shift_grads[layer], gain_grads[layer] = [row.reshape(-1) for row in unpack_sums(packed, widths[layer])]
        weight_grads[layer] = tap_gradient(
            inputs_all[layer],
            own_columns(gather_section(grad_conv), grad_conv.shape[1] // section_size),
            same_all,
            kernel,
            rows,
        )

    grad_mel = grad_after_frames + upstream
    grad_stop_frames = grad_stop.T.reshape(frame_rows, 1)
    grad_out = dot(grad_mel, proj_weight, 1, 1) + grad_stop_frames * stop_weight
    mel_grads = jnp.pad(
        jnp.concatenate([grad_mel, grad_stop_frames], axis=1), ((0, 0), (0, lanes - mel - 1))
    )
    mel_pair = gather_y(mel_grads)
    mel_grads_all = gather_core(mel_pair).reshape(-1, lanes)
    outs_own = own_columns(gather_section(out_frames), out_frames.shape[1] // section_size)
    outs_own = outs_own.reshape(mel_grads_all.shape[0], -1)
    g_proj_part = dot(outs_own, mel_grads_all, 0, 0)
    group_grads, group_token = join_rows(
        [grad.reshape(-1, lanes) for grad in weight_grads + [g_proj_part]]
        + [jnp.pad(jnp.sum(mel_grads_all, axis=0, keepdims=True), ((0, 7), (0, 0)))],
        input_pieces,
    )
    group_sums = lax.psum(group_grads, "dp")
    dec_sums, grad_dec_inputs = decoder_backward(
        dec_all,
        grad_out[:, :units],
        dec_gates,
        dec_cells,
        zone,
        resume_pair,
        valid_pair,
        rows,
        lag,
        [group_token],
    )
    g_dec_bias = jnp.sum(dec_sums, axis=1).reshape(-1)
    grad_context = grad_out[:, units:] + grad_dec_inputs[:, units:]
    dec_columns = exchange_ring(dec_sums) if rings else None
    (
        att_sums,
        g_att_bias,
        grad_prenet,
        grad_query,
        grad_processed,
        grad_memory,
        grad_loc,
        grad_energy,
    ) = attention_backward(
        att_all,
        grad_dec_inputs[:, :units],
        grad_context,
        gates,
        cells,
        bent,
        weights,
        window,
        loc_map,
        memory_flat,
        query_weight,
        energy_row,
        zone,
        resume_pair,
        valid_pair,
        next_resume,
        rows,
        positions,
        prenet_width,
        lag,
        (group_token,),
    )

    grad_processed = grad_processed.reshape(rows * positions, features)
    grad_memory = grad_memory + dot(grad_processed, memory_weight, 1, 1)
    g_memory_weight = dot(memory_flat, grad_processed, 0, 0)
    g_query_weight = dot(att_frames, grad_query, 0, 0)
    (grad_second,) = second_back(grad_prenet * keep_second)
    g_pre_second = dot(pre_hidden, grad_second, 0, 0)
    (grad_first,) = first_back(dot(grad_second, pre_second, 1, 1) * keep_first)
    g_pre_first = dot(frames_in, grad_first, 0, 0)
    filters, channels, taps = loc_filters.shape
    grad_joined = location_unmap(grad_loc, channels, taps, positions, features)
    late_grads = (
        g_pre_first,
        g_pre_second,
        g_att_bias,
        g_query_weight,
        g_memory_weight,
        grad_joined,
        jnp.sum(grad_energy, axis=0),
        g_dec_bias,
    )
    context_end = prenet_width + context_width
    dec_part = column_gradients(
        [att_inputs_all, dec_inputs_all],
        ((0, context_end, input_width), (0, prenet_width, context_end), (1, 0, units)),
        dec_columns,
        dec_sums,
    )
    late_joined = flat_join(late_grads, devices)
    if rings:
        late_ring = sum_section(late_joined.reshape((-1, 4) + late_joined.shape[1:]).swapaxes(0, 1))
        late_ring = late_ring + 0.0 * (dec_columns[0, 0, 0, 0] + group_sums[0, 0])
        att_columns, late_part = exchange_ring(att_sums, late_ring)
    else:
        att_columns = None
        late_part = part_sum(late_joined)
    att_part = column_gradients([att_inputs_all], ((0, 0, input_width),), att_columns, att_sums)

    late_sums = flat_split(flat_whole(late_part, devices), late_grads)
    grad_joined = late_sums[5].reshape(channels * taps, features)
    g_loc_filters = dot(loc_dense, grad_joined, 1, 1).reshape(loc_filters.shape)
    g_loc_dense = dot(loc_filters.reshape(filters, channels * taps), grad_joined)

    first_rows = kernel * lanes
    mid_end = first_rows + post_mid.size // lanes
    proj_start = mid_end + first_rows
    proj_end = proj_start + out_frames.shape[1] // section_size
    mid_part = group_sums[first_rows:mid_end].reshape(post_mid.shape)
    own = lax.axis_index("section")
    shared = jnp.concatenate([group_sums[:first_rows], group_sums[mid_end:proj_end]], axis=0)
    shared_all = section_order(gather_section(shared), own)
    g_post_first = jnp.concatenate(
        [piece[:first_rows].reshape(kernel, lanes, lanes)[:, :mel] for piece in shared_all], axis=2
    )
    g_post_last = jnp.concatenate(
        [piece[first_rows : 2 * first_rows].reshape(kernel, lanes, lanes)[:, :, :mel] for piece in shared_all], axis=1
    )
    g_proj = jnp.concatenate([piece[2 * first_rows :] for piece in shared_all], axis=0)
    g_proj_bias = group_sums[proj_end, :mel]
    return (
        mel_after.reshape(frames, rows, mel).swapaxes(0, 1),
        stop_logit,
        grad_memory.reshape(memory.shape),
        late_sums[0],
        late_sums[1],
        att_part,
        late_sums[2].reshape(-1),
        late_sums[3],
        late_sums[4],
        g_loc_filters,
        g_loc_dense,
        late_sums[6],
        dec_part,
        late_sums[7],
        g_proj[:, :mel],
        g_proj_bias,
        g_proj[:, mel],
        g_post_first,
        mid_part,
        g_post_last,
        jnp.stack(gain_grads[:4]),
        jnp.stack(shift_grads[:4]),
        gain_grads[4],
        shift_grads[4],
    )


def solution(mesh):
    rows_only = P(both)
    columns_only = P(None, both)
    mid_spec = P(None, None, None, "section")
    placed = (
        (rows_only,) * 6
        + (P(), P(), columns_only)
        + (P(),) * 6
        + (columns_only,)
        + (P(),) * 5
        + (mid_spec,)
        + (P(),) * 5
        + (rows_only, rows_only)
    )
    given = (
        (rows_only,) * 3
        + (P(), P(), columns_only)
        + (P(),) * 6
        + (columns_only,)
        + (P(),) * 5
        + (mid_spec,)
        + (P(),) * 5
    )
    return jax.shard_map(per_device, mesh=mesh, in_specs=placed, out_specs=given, check_vma=False)
```

```python
import functools
import math

import jax
import jax.numpy as jnp
from jax import lax
from jax.experimental import pallas as pl
from jax.experimental.pallas import tpu as pltpu
from jax.sharding import PartitionSpec as P

high = lax.Precision.HIGH
norm_eps = 1e-05
f32 = jnp.float32
bf16 = jnp.bfloat16
both = ("dp", "section")
lanes = 128
vmem_limit = 62 * 1024 * 1024

span = 6
shard_block = 4


def split(values):
    upper = values.astype(bf16)
    lower = (values - upper.astype(f32)).astype(bf16)
    return upper, lower


def product(left, upper, lower, transposed=False):
    rows = left.shape[0]
    left_upper, left_lower = split(left)
    stacked = jnp.concatenate([left_upper, left_lower], axis=0)
    dims = (((1,), (1,)), ((), ())) if transposed else (((1,), (0,)), ((), ()))
    first = lax.dot_general(stacked, upper, dims, preferred_element_type=f32)
    second = lax.dot_general(left_upper, lower, dims, preferred_element_type=f32)
    return first[:rows] + first[rows:] + second


def sigmoid(values):
    return 0.5 * jnp.tanh(0.5 * values) + 0.5


def lane_index(shape):
    return lax.broadcasted_iota(jnp.int32, shape, 1)


def fold_lanes(values, positions):
    copies = values
    shift = positions
    while shift < lanes:
        copies = copies + pltpu.roll(copies, shift, 1)
        shift *= 2
    return copies


def diagonal_mask(rows, positions):
    shape = (2 * rows, rows * positions)
    row = lax.broadcasted_iota(jnp.int32, shape, 0)
    group = lax.broadcasted_iota(jnp.int32, shape, 1) // positions
    return group == jnp.where(row >= rows, row - rows, row)


def spread(weights, rows, positions):
    copies = fold_lanes(weights, positions)
    wide = jnp.concatenate([copies] * (rows * positions // lanes), axis=1)
    return jnp.where(diagonal_mask(rows, positions), wide, 0.0)


def collect(wide, rows, positions):
    kept = jnp.where(diagonal_mask(rows, positions), wide, 0.0)
    total = kept[:, :lanes]
    for start in range(lanes, rows * positions, lanes):
        total = total + kept[:, start : start + lanes]
    shift = positions
    while shift < lanes:
        total = total + pltpu.roll(total, shift, 1)
        shift *= 2
    return jnp.where(lane_index(total.shape) < positions, total, 0.0)


def store_parts(block_ref, first, last, upper_ref, lower_ref, index):
    for place in range(shard_block):
        upper, lower = split(block_ref[place, first:last, :])
        upper_ref[index, :, place * lanes : (place + 1) * lanes] = upper
        lower_ref[index, :, place * lanes : (place + 1) * lanes] = lower


def gate_forward(gate_sums, cell, hidden, zone_hidden, zone_cell):
    units = cell.shape[1]
    gate_in = sigmoid(gate_sums[:, :units])
    gate_keep = sigmoid(gate_sums[:, units : 2 * units])
    update = jnp.tanh(gate_sums[:, 2 * units : 3 * units])
    gate_out = sigmoid(gate_sums[:, 3 * units :])
    new_cell = gate_keep * cell + gate_in * update
    new_hidden = gate_out * jnp.tanh(new_cell)
    hidden = zone_hidden * hidden + (1.0 - zone_hidden) * new_hidden
    cell = zone_cell * cell + (1.0 - zone_cell) * new_cell
    return hidden, cell, (gate_in, gate_keep, update, gate_out)


def gate_backward(gates, cell, zone_hidden, zone_cell, grad_hidden, grad_cell):
    units = cell.shape[1]
    gate_in = gates[:, :units]
    gate_keep = gates[:, units : 2 * units]
    update = gates[:, 2 * units : 3 * units]
    gate_out = gates[:, 3 * units :]
    bent = jnp.tanh(gate_keep * cell + gate_in * update)
    grad_new = (1.0 - zone_hidden) * grad_hidden
    grad_new_cell = grad_new * gate_out * (1.0 - bent * bent) + (1.0 - zone_cell) * grad_cell
    grad_sums = (
        grad_new_cell * update * gate_in * (1.0 - gate_in),
        grad_new_cell * cell * gate_keep * (1.0 - gate_keep),
        grad_new_cell * gate_in * (1.0 - update * update),
        grad_new * bent * gate_out * (1.0 - gate_out),
    )
    return grad_sums, zone_hidden * grad_hidden, zone_cell * grad_cell + grad_new_cell * gate_keep


def zone_masks(early_ref, late_ref):
    masks = []
    for which in range(2):
        pair = jnp.concatenate([early_ref[0, which], late_ref[0, which]], axis=0)
        masks.append(pair.astype(f32))
    return masks


def attention_forward_kernel(
    blocks,
    rows,
    positions,
    lag,
    weight_ref,
    prenet_ref,
    bias_ref,
    loc_map_ref,
    processed_ref,
    memory_ref,
    query_ref,
    energy_ref,
    zone_early_ref,
    zone_late_ref,
    resume_ref,
    allowed_ref,
    awaited,
    hidden_out,
    cell_out,
    context_out,
    gates_out,
    bent_out,
    weights_out,
    window_out,
    upper,
    lower,
    inputs,
    loc_upper,
    loc_lower,
    memory_upper,
    memory_lower,
    query_upper,
    query_lower,
    sums,
    hidden,
    cell,
    context,
    window,
):
    step = pl.program_id(0)
    prenet_width = prenet_ref.shape[1]
    context_width = context.shape[1]
    units = hidden.shape[1]
    width = shard_block * lanes

    @pl.when(step == 0)
    def prepare():
        loc_upper[...], loc_lower[...] = split(loc_map_ref[...])
        memory_upper[...], memory_lower[...] = split(memory_ref[...])
        query_upper[...], query_lower[...] = split(query_ref[...])
        hidden[...] = jnp.zeros_like(hidden)
        cell[...] = jnp.zeros_like(cell)
        context[...] = jnp.zeros_like(context)
        window[...] = jnp.zeros_like(window)

    @pl.when(step < blocks)
    def load():
        store_parts(weight_ref, prenet_width, weight_ref.shape[1], upper, lower, step)
        first = jnp.concatenate([weight_ref[place, :prenet_width, :] for place in range(shard_block)], axis=1)
        first_upper, first_lower = split(first)
        inputs[step] = product(prenet_ref[...], first_upper, first_lower) + bias_ref[0]

    @pl.when(step >= blocks)
    def advance():
        frame = step - blocks
        resume = resume_ref[0]
        hidden_now = hidden[...] * resume
        cell_now = cell[...] * resume
        context_now = context[...] * resume
        window_now = window[...] * resume
        early = pl.multiple_of(frame * rows, rows)
        late = pl.multiple_of((frame + lag) * rows, rows)
        for block in range(blocks):
            taken = slice(block * width, (block + 1) * width)
            sums[:rows, taken] = inputs[block, pl.ds(early, rows), :]
            sums[rows:, taken] = inputs[block, pl.ds(late, rows), :]

        @pl.when(frame > 0)
        def recur():
            state = jnp.concatenate([context_now, hidden_now], axis=1)
            for block in range(blocks):
                taken = slice(block * width, (block + 1) * width)
                sums[:, taken] += product(state, upper[block], lower[block])

        zone_hidden, zone_cell = zone_masks(zone_early_ref, zone_late_ref)
        hidden_new, cell_new, gates = gate_forward(sums[...], cell_now, hidden_now, zone_hidden, zone_cell)
        for place, gate in enumerate(gates):
            gates_out[0, :, place * units : (place + 1) * units] = gate
        hidden[...] = hidden_new
        cell[...] = cell_new
        hidden_out[0] = hidden_new
        cell_out[0] = cell_new
        query = product(hidden_new, query_upper[...], query_lower[...])
        located = product(window_now, loc_upper[...], loc_lower[...])
        energy_v = energy_ref[...]
        lane = lane_index((2 * rows, lanes))
        energy = jnp.zeros((2 * rows, lanes), f32)
        for place in range(positions):
            taken = slice(place * lanes, (place + 1) * lanes)
            ready = processed_ref[:, taken]
            bent = jnp.tanh(query + jnp.concatenate([ready, ready], axis=0) + located[:, taken])
            bent_out[0, :, taken] = bent
            energy = jnp.where(lane == place, jnp.sum(bent * energy_v, axis=1, keepdims=True), energy)
        masked = jnp.where(allowed_ref[...] > 0.5, energy, -1000000000.0)
        exponent = jnp.exp(masked - jnp.max(masked, axis=1, keepdims=True))
        weights = exponent / jnp.sum(exponent, axis=1, keepdims=True)
        weights = jnp.where(lane < positions, weights, 0.0)
        weights_out[0] = weights
        window_out[0] = window_now
        second = (lane >= positions) & (lane < 2 * positions)
        window[...] = weights + pltpu.roll(weights, positions, 1) + jnp.where(second, window_now, 0.0)
        context_new = product(spread(weights, rows, positions), memory_upper[...], memory_lower[...])
        context[...] = context_new
        context_out[0] = context_new


def decoder_forward_kernel(
    blocks,
    rows,
    lag,
    awaited,
    weight_ref,
    frames_ref,
    bias_ref,
    zone_early_ref,
    zone_late_ref,
    resume_ref,
    *refs,
):
    hidden_out, cell_out, gates_out, upper, lower, inputs, sums, hidden, cell = refs[awaited:]
    step = pl.program_id(0)
    units = hidden.shape[1]
    width = shard_block * lanes

    @pl.when(step == 0)
    def prepare():
        hidden[...] = jnp.zeros_like(hidden)
        cell[...] = jnp.zeros_like(cell)

    @pl.when(step < blocks)
    def load():
        split_row = frames_ref.shape[1]
        store_parts(weight_ref, split_row, weight_ref.shape[1], upper, lower, step)
        first = jnp.concatenate([weight_ref[place, :split_row, :] for place in range(shard_block)], axis=1)
        first_upper, first_lower = split(first)
        inputs[step] = product(frames_ref[...], first_upper, first_lower) + bias_ref[0]

    @pl.when(step >= blocks)
    def advance():
        frame = step - blocks
        resume = resume_ref[0]
        hidden_now = hidden[...] * resume
        cell_now = cell[...] * resume
        early = pl.multiple_of(frame * rows, rows)
        late = pl.multiple_of((frame + lag) * rows, rows)
        for block in range(blocks):
            taken = slice(block * width, (block + 1) * width)
            sums[:rows, taken] = inputs[block, pl.ds(early, rows), :]
            sums[rows:, taken] = inputs[block, pl.ds(late, rows), :]

        @pl.when(frame > 0)
        def recur():
            for block in range(blocks):
                taken = slice(block * width, (block + 1) * width)
                sums[:, taken] += product(hidden_now, upper[block], lower[block])

        zone_hidden, zone_cell = zone_masks(zone_early_ref, zone_late_ref)
        hidden_new, cell_new, gates = gate_forward(sums[...], cell_now, hidden_now, zone_hidden, zone_cell)
        for place, gate in enumerate(gates):
            gates_out[0, :, place * units : (place + 1) * units] = gate
        hidden[...] = hidden_new
        cell[...] = cell_new
        hidden_out[0] = hidden_new
        cell_out[0] = cell_new


def add_frames(total_ref, grads, frame, rows, lag):
    early = pl.multiple_of(frame * rows, rows)
    late = pl.multiple_of((frame + lag) * rows, rows)
    total_ref[pl.ds(early, rows), :] += grads[:rows]
    total_ref[pl.ds(late, rows), :] += grads[rows:]


def decoder_backward_kernel(
    blocks,
    rows,
    lag,
    own_parts,
    in_parts,
    awaited,
    *refs,
):
    own_refs = refs[:own_parts]
    in_refs = refs[own_parts : own_parts + in_parts]
    (
        grad_ref,
        gates_ref,
        cell_ref,
        zone_early_ref,
        zone_late_ref,
        resume_ref,
        valid_ref,
    ) = refs[own_parts + in_parts : own_parts + in_parts + 7]
    grad_sums_out, grad_in_out, upper, lower, frame_sums, grad_hidden, grad_cell = refs[
        own_parts + in_parts + 7 + awaited :
    ]
    step = pl.program_id(0)
    units = grad_hidden.shape[1]
    width = shard_block * lanes

    @pl.when(step == 0)
    def prepare():
        grad_hidden[...] = jnp.zeros_like(grad_hidden)
        grad_cell[...] = jnp.zeros_like(grad_cell)
        frame_sums[...] = jnp.zeros_like(frame_sums)
        grad_in_out[...] = jnp.zeros_like(grad_in_out)

    @pl.when(step < blocks)
    def load():
        for which, own_ref in enumerate(own_refs):
            part = own_ref.shape[1]
            for place in range(shard_block):
                taken = slice(place * lanes, (place + 1) * lanes)
                own_upper, own_lower = split(own_ref[place])
                upper[step, which * part : (which + 1) * part, taken] = own_upper
                lower[step, which * part : (which + 1) * part, taken] = own_lower

    @pl.when((step >= blocks) & (step < blocks + span))
    def retreat():
        frame = span - 1 - (step - blocks)
        resume = resume_ref[0]
        early = pl.multiple_of(frame * rows, rows)
        late = pl.multiple_of((frame + lag) * rows, rows)
        arriving = jnp.concatenate(
            [grad_ref[pl.ds(early, rows), :units], grad_ref[pl.ds(late, rows), :units]], axis=0
        )
        total = grad_hidden[...] + arriving * valid_ref[0]
        cell_now = cell_ref[0] * jnp.where(frame > 0, resume, 0.0)
        zone_hidden, zone_cell = zone_masks(zone_early_ref, zone_late_ref)
        grad_sums, passed_hidden, passed_cell = gate_backward(
            gates_ref[0], cell_now, zone_hidden, zone_cell, total, grad_cell[...]
        )
        grad_cell[...] = passed_cell * resume
        grad_hidden[...] = passed_hidden
        for place, grads in enumerate(grad_sums):
            for part in range(units // width):
                block = place * (units // width) + part
                add_frames(frame_sums.at[block], grads[:, part * width : (part + 1) * width], frame, rows, lag)

        @pl.when(frame > 0)
        def recur():
            carried = grad_hidden[...]
            for place, grads in enumerate(grad_sums):
                for part in range(units // width):
                    block = place * (units // width) + part
                    taken = grads[:, part * width : (part + 1) * width]
                    carried = carried + product(taken, upper[block], lower[block], transposed=True)
            grad_hidden[...] = carried * resume

    @pl.when(step >= blocks + span)
    def pass_on():
        block = step - blocks - span
        grads = frame_sums[block]
        for place in range(shard_block):
            grad_sums_out[place] = grads[:, place * lanes : (place + 1) * lanes]
        for which, in_ref in enumerate(in_refs):
            part = in_ref.shape[1]
            taken = slice(which * part, (which + 1) * part)
            first = jnp.concatenate([in_ref[place] for place in range(shard_block)], axis=1)
            first_upper, first_lower = split(first)
            grad_in_out[:, taken] += product(grads, first_upper, first_lower, transposed=True)


def attention_backward_kernel(
    blocks,
    rows,
    positions,
    lag,
    weight_ref,
    grad_in_ref,
    grad_out_ref,
    gates_ref,
    cell_ref,
    bent_ref,
    weights_ref,
    window_ref,
    loc_map_ref,
    memory_ref,
    query_ref,
    energy_ref,
    zone_early_ref,
    zone_late_ref,
    resume_ref,
    valid_ref,
    next_resume_ref,
    awaited,
    grad_sums_out,
    grad_bias_out,
    grad_prenet_out,
    grad_query_out,
    grad_processed_out,
    grad_memory_out,
    grad_loc_out,
    grad_energy_out,
    upper,
    lower,
    first_upper,
    first_lower,
    frame_sums,
    loc_upper,
    loc_lower,
    memory_upper,
    memory_lower,
    query_upper,
    query_lower,
    grad_bent,
    grad_contexts,
    diagonals,
    windows,
    grad_hidden,
    grad_cell,
    grad_context,
    grad_window,
):
    step = pl.program_id(0)
    units = grad_hidden.shape[1]
    context_width = grad_context.shape[1]
    prenet_width = first_upper.shape[1]
    width = shard_block * lanes
    pair = 2 * rows

    @pl.when(step == 0)
    def prepare():
        loc_upper[...], loc_lower[...] = split(loc_map_ref[...])
        memory_upper[...], memory_lower[...] = split(memory_ref[...])
        query_upper[...], query_lower[...] = split(query_ref[...])
        grad_hidden[...] = jnp.zeros_like(grad_hidden)
        grad_cell[...] = jnp.zeros_like(grad_cell)
        grad_context[...] = jnp.zeros_like(grad_context)
        grad_window[...] = jnp.zeros_like(grad_window)
        frame_sums[...] = jnp.zeros_like(frame_sums)
        grad_query_out[...] = jnp.zeros_like(grad_query_out)
        grad_processed_out[...] = jnp.zeros_like(grad_processed_out)
        grad_energy_out[...] = jnp.zeros_like(grad_energy_out)

    @pl.when(step < blocks)
    def load():
        store_parts(weight_ref, prenet_width, weight_ref.shape[1], upper, lower, step)
        store_parts(weight_ref, 0, prenet_width, first_upper, first_lower, step)

    @pl.when(step >= blocks)
    def retreat():
        frame = span - 1 - (step - blocks)
        resume = resume_ref[0]
        valid = valid_ref[0]
        early = pl.multiple_of(frame * rows, rows)
        late = pl.multiple_of((frame + lag) * rows, rows)
        here = pl.multiple_of(frame * pair, pair)
        lane = lane_index((pair, lanes))
        arriving = jnp.concatenate(
            [
                grad_in_ref[pl.ds(start, rows), units:] + grad_out_ref[pl.ds(start, rows), units:]
                for start in (early, late)
            ],
            axis=0,
        )
        context_total = grad_context[...] + arriving * valid
        grad_contexts[pl.ds(here, pair), :] = context_total
        weights = weights_ref[0]
        diagonals[pl.ds(here, pair), :] = spread(weights, rows, positions)
        windows[pl.ds(here, pair), :] = window_ref[0]
        window_grad = grad_window[...]
        wide = product(context_total, memory_upper[...], memory_lower[...], transposed=True)
        grad_weights = collect(wide, rows, positions) + jnp.where(
            lane < positions, window_grad + pltpu.roll(window_grad, lanes - positions, 1), 0.0
        )
        inner = jnp.sum(weights * grad_weights, axis=1, keepdims=True)
        grad_energy = weights * (grad_weights - inner)
        energy_v = energy_ref[...]
        energy_total = jnp.zeros((pair, lanes), f32)
        query_total = jnp.zeros((pair, lanes), f32)
        for place in range(positions):
            taken = slice(place * lanes, (place + 1) * lanes)
            bent = bent_ref[0, :, taken]
            column = jnp.sum(jnp.where(lane == place, grad_energy, 0.0), axis=1, keepdims=True)
            energy_total = energy_total + column * bent
            slope = column * energy_v * (1.0 - bent * bent)
            query_total = query_total + slope
            grad_bent[pl.ds(here, pair), taken] = slope
            grad_processed_out[:, taken] += slope[:rows] + slope[rows:]
        grad_energy_out[...] += energy_total
        add_frames(grad_query_out, query_total, frame, rows, lag)
        slopes = grad_bent[pl.ds(here, pair), :]
        moved = product(slopes, loc_upper[...], loc_lower[...], transposed=True)
        second = (lane >= positions) & (lane < 2 * positions)
        grad_window[...] = resume * (moved + jnp.where(second, window_grad, 0.0))

        arriving = jnp.concatenate(
            [grad_in_ref[pl.ds(early, rows), :units], grad_in_ref[pl.ds(late, rows), :units]], axis=0
        )
        total = grad_hidden[...] + arriving * valid
        total = total + product(query_total, query_upper[...], query_lower[...], transposed=True)
        cell_now = cell_ref[0] * jnp.where(frame > 0, resume, 0.0)
        zone_hidden, zone_cell = zone_masks(zone_early_ref, zone_late_ref)
        grad_sums, passed_hidden, passed_cell = gate_backward(
            gates_ref[0], cell_now, zone_hidden, zone_cell, total, grad_cell[...]
        )
        grad_cell[...] = passed_cell * resume
        for place, grads in enumerate(grad_sums):
            for part in range(units // width):
                block = place * (units // width) + part
                add_frames(frame_sums.at[block], grads[:, part * width : (part + 1) * width], frame, rows, lag)

        @pl.when(frame > 0)
        def recur():
            carried = jnp.zeros((pair, context_width + units), f32)
            for place, grads in enumerate(grad_sums):
                for part in range(units // width):
                    block = place * (units // width) + part
                    taken = grads[:, part * width : (part + 1) * width]
                    carried = carried + product(taken, upper[block], lower[block], transposed=True)
            grad_context[...] = carried[:, :context_width] * resume
            grad_hidden[...] = (carried[:, context_width:] + passed_hidden) * resume

    @pl.when(step == blocks + span - 1)
    def finish():
        prenet_grad = jnp.zeros(grad_prenet_out.shape, f32)
        frame_rows = frame_sums.shape[1]
        for block in range(blocks):
            grads = frame_sums[block]
            prenet_grad = prenet_grad + product(grads, first_upper[block], first_lower[block], transposed=True)
            grad_bias_out[:, block * width : (block + 1) * width] = jnp.sum(grads, axis=0, keepdims=True)
            later = jnp.concatenate([grads[rows:], jnp.zeros((rows, width), f32)], axis=0) * next_resume_ref[...]
            for place in range(shard_block):
                grad_sums_out[block * shard_block + place] = later[:, place * lanes : (place + 1) * lanes]
        grad_prenet_out[...] = prenet_grad
        context_upper, context_lower = split(grad_contexts[...])
        grad_memory_out[...] = product(diagonals[...].T, context_upper, context_lower)
        window_turned = windows[...].T
        for block in range(blocks):
            taken = slice(block * width, (block + 1) * width)
            bent_upper, bent_lower = split(grad_bent[:, taken])
            grad_loc_out[:, taken] = product(window_turned, bent_upper, bent_lower)


def split_kernel(values_ref, upper_ref, lower_ref):
    upper_ref[...], lower_ref[...] = split(values_ref[...])


def split_matrix(values):
    shape = jax.ShapeDtypeStruct(values.shape, bf16)
    return pl.pallas_call(
        split_kernel,
        out_shape=[shape, shape],
        compiler_params=pltpu.CompilerParams(vmem_limit_bytes=vmem_limit),
        name="split_matrix",
    )(values)


def join_kernel(count, *refs):
    out_ref, token_ref = refs[-2:]
    start = 0
    for ref in refs[:count]:
        out_ref[start : start + ref.shape[0]] = ref[...]
        start += ref.shape[0]
    token_ref[...] = jnp.zeros_like(token_ref)


def join_rows(arrays, awaited):
    total = sum(array.shape[0] for array in arrays)
    return pl.pallas_call(
        functools.partial(join_kernel, len(arrays)),
        in_specs=[pl.BlockSpec(memory_space=pltpu.VMEM)] * len(arrays)
        + [pl.BlockSpec(memory_space=pl.ANY)] * len(awaited),
        out_shape=[jax.ShapeDtypeStruct((total, lanes), f32), jax.ShapeDtypeStruct((8, lanes), f32)],
        compiler_params=pltpu.CompilerParams(vmem_limit_bytes=vmem_limit),
        name="join_rows",
    )(*arrays, *awaited)


def pack_sums(*sums):
    rows = []
    for row in sums:
        channels = row.shape[1]
        if channels % lanes:
            row = jnp.concatenate([row, jnp.zeros((1, -channels % lanes), f32)], axis=1)
        rows += [row[:, start : start + lanes] for start in range(0, row.shape[1], lanes)]
    if len(rows) < 8:
        rows.append(jnp.zeros((8 - len(rows), lanes), f32))
    return jnp.concatenate(rows, axis=0)


def unpack_sums(packed, channels, number=2):
    count = -(-channels // lanes)
    rows = []
    for row in range(number):
        pieces = [packed[row * count + place : row * count + place + 1] for place in range(count)]
        rows.append(jnp.concatenate(pieces, axis=1)[:, :channels])
    return rows


def moved_rows(values, shift):
    if shift > 0:
        return jnp.concatenate([jnp.zeros((shift, values.shape[1]), f32), values[:-shift]], axis=0)
    if shift < 0:
        return jnp.concatenate([values[-shift:], jnp.zeros((-shift, values.shape[1]), f32)], axis=0)
    return values


def convolve(values, same, upper_ref, lower_ref, rows):
    kernel = upper_ref.shape[0] // values.shape[1]
    channels = values.shape[1]
    total = None
    for tap in range(kernel):
        taken = slice(tap * channels, (tap + 1) * channels)
        moved = moved_rows(values, (kernel // 2 - tap) * rows) * same[:, tap : tap + 1]
        piece = product(moved, upper_ref[taken, :], lower_ref[taken, :])
        total = piece if total is None else total + piece
    return total


def send_sums(copies_ref, *values):
    packed = pack_sums(*[jnp.sum(value, axis=0, keepdims=True) for value in values])
    for place in range(copies_ref.shape[0]):
        copies_ref[place] = packed


def post_first_kernel(rows, values_ref, same_ref, upper_ref, lower_ref, conv_out, copies_out):
    conv = convolve(values_ref[...], same_ref[...], upper_ref, lower_ref, rows)
    conv_out[...] = conv
    send_sums(copies_out, conv, conv * conv)


def post_next_kernel(
    rows,
    frame_count,
    conv_ref,
    sums_ref,
    gain_ref,
    shift_ref,
    same_ref,
    upper_ref,
    lower_ref,
    *refs,
):
    *grad_refs, scaled_out, active_out, inverse_out, conv_out, copies_out = refs
    conv = conv_ref[...]
    first, second = unpack_sums(jnp.sum(sums_ref[...], axis=0), conv.shape[1])
    average = first / frame_count
    inverse = lax.rsqrt(second / frame_count - average * average + norm_eps)
    scaled = (conv - average) * inverse
    active = jnp.tanh(scaled * gain_ref[...] + shift_ref[...])
    scaled_out[...] = scaled
    active_out[...] = active
    inverse_out[...] = inverse
    conv = convolve(active, same_ref[...], upper_ref, lower_ref, rows)
    conv_out[...] = conv
    grads = [piece for ref in grad_refs for piece in (ref[...], ref[...] * conv)]
    send_sums(copies_out, conv, conv * conv, *grads)


def conv_back(grad_conv, same, upper_ref, lower_ref, channels, rows):
    kernel = upper_ref.shape[0] // channels
    total = None
    for tap in range(kernel):
        taken = slice(tap * channels, (tap + 1) * channels)
        piece = product(grad_conv, upper_ref[taken, :], lower_ref[taken, :], transposed=True)
        piece = moved_rows(piece * same[:, tap : tap + 1], (tap - kernel // 2) * rows)
        total = piece if total is None else total + piece
    return total


def post_turn_kernel(
    rows,
    frame_count,
    grad_ref,
    conv_ref,
    sums_ref,
    before_ref,
    gain_ref,
    shift_ref,
    same_ref,
    upper_ref,
    lower_ref,
    active_ref,
    scaled_below_ref,
    after_out,
    conv_out,
    sums_out,
    grad_out,
    copies_out,
):
    conv = conv_ref[...]
    grad = grad_ref[...]
    gain = gain_ref[...]
    first, second, shift_grad, mixed = unpack_sums(jnp.sum(sums_ref[...], axis=0), conv.shape[1], 4)
    average = first / frame_count
    inverse = lax.rsqrt(second / frame_count - average * average + norm_eps)
    scaled = (conv - average) * inverse
    after_out[...] = before_ref[...] + scaled * gain + shift_ref[...]
    gain_grad = inverse * (mixed - average * shift_grad)
    sums_out[...] = pack_sums(shift_grad, gain_grad)
    grad_conv = inverse * gain * (grad - (shift_grad + scaled * gain_grad) / frame_count)
    conv_out[...] = jnp.concatenate([grad_conv, jnp.zeros((conv.shape[0], -conv.shape[1] % lanes), f32)], axis=1)
    active = active_ref[...]
    total = conv_back(grad_conv, same_ref[...], upper_ref, lower_ref, active.shape[1], rows)
    total = total * (1.0 - active * active)
    send_sums(copies_out, total, total * scaled_below_ref[...])
    grad_out[...] = total


def post_back_kernel(
    rows,
    frame_count,
    has_lower,
    awaited,
    grad_ref,
    scaled_ref,
    sums_ref,
    inverse_ref,
    gain_ref,
    same_ref,
    upper_ref,
    lower_ref,
    *refs,
):
    if has_lower:
        active_ref, scaled_below_ref = refs[:2]
        conv_out, sums_out, grad_out, copies_out = refs[2 + awaited :]
    else:
        conv_out, sums_out, grad_out = refs[awaited:]
    grad = grad_ref[...]
    scaled = scaled_ref[...]
    same = same_ref[...]
    packed = jnp.sum(sums_ref[...], axis=0)
    sums_out[...] = packed
    shift_grad, gain_grad = unpack_sums(packed, grad.shape[1])
    grad_conv = inverse_ref[...] * gain_ref[...] * (grad - (shift_grad + scaled * gain_grad) / frame_count)
    conv_out[...] = grad_conv
    total = conv_back(grad_conv, same, upper_ref, lower_ref, grad_out.shape[1], rows)
    if has_lower:
        active = active_ref[...]
        total = total * (1.0 - active * active)
        send_sums(copies_out, total, total * scaled_below_ref[...])
    grad_out[...] = total


def post_call(kernel, outs, name, operands, awaited=()):
    shapes = [jax.ShapeDtypeStruct(shape, f32) for shape in outs]
    in_specs = [pl.BlockSpec(memory_space=pltpu.VMEM)] * len(operands)
    in_specs += [pl.BlockSpec(memory_space=pl.ANY)] * len(awaited)
    return pl.pallas_call(
        kernel,
        in_specs=in_specs,
        out_specs=[pl.BlockSpec(memory_space=pltpu.VMEM)] * len(outs),
        out_shape=shapes,
        compiler_params=pltpu.CompilerParams(vmem_limit_bytes=vmem_limit),
        name=name,
    )(*operands, *awaited)


def share_sums(copies):
    return lax.all_to_all(copies, both, 0, 0)


def tap_gradient_kernel(rows, kernel, split_inputs, own_ref, *refs):
    count = (len(refs) - 1) // 3
    input_refs, grad_refs, same_refs = refs[:count], refs[count : 2 * count], refs[2 * count : 3 * count]
    out_ref = refs[-1]
    margin = kernel // 2
    place = pl.ds(pl.multiple_of(own_ref[0] * lanes, lanes), lanes)
    if split_inputs:
        inputs = [ref[:, place] for ref in input_refs]
        grads = [ref[...] for ref in grad_refs]
    else:
        inputs = [ref[...] for ref in input_refs]
        grads = [ref[:, place] for ref in grad_refs]
    moved = []
    for tap in range(kernel):
        pieces = [
            moved_rows(grad * same[:, tap : tap + 1], (tap - margin) * rows) for grad, same in zip(grads, same_refs)
        ]
        moved.append(jnp.concatenate(pieces, axis=0))
    upper, lower = split(jnp.concatenate(moved, axis=1))
    result = product(jnp.concatenate(inputs, axis=0).T, upper, lower)
    depth = out_ref.shape[1]
    for tap in range(kernel):
        block = result[:, tap * lanes : (tap + 1) * lanes]
        out_ref[tap] = block.T[:depth] if split_inputs else block[:depth]


def tap_gradient(inputs, grads, same, kernel, rows, depth, split_inputs=False):
    own = lax.axis_index("section").astype(jnp.int32).reshape(1)
    return pl.pallas_call(
        functools.partial(tap_gradient_kernel, rows, kernel, split_inputs),
        in_specs=[pl.BlockSpec(memory_space=pltpu.SMEM)]
        + [pl.BlockSpec(memory_space=pltpu.VMEM)] * (len(inputs) + len(grads) + len(same)),
        out_shape=jax.ShapeDtypeStruct((kernel, depth, lanes), f32),
        compiler_params=pltpu.CompilerParams(vmem_limit_bytes=vmem_limit),
        name="tap_gradient",
    )(own, *inputs, *grads, *same)


def frame_product_kernel(pieces, *refs):
    inputs = refs[:-3]
    grads_ref, out_ref, total = refs[-3:]
    step = pl.program_id(0)

    @pl.when(step == 0)
    def prepare():
        total[...] = jnp.zeros_like(total)

    blocks, groups = grads_ref.shape[:2]
    grads = jnp.concatenate(
        [jnp.concatenate([grads_ref[block, group] for group in range(groups)], axis=1) for block in range(blocks)],
        axis=0,
    )
    columns = grads.shape[1]
    turned_upper, turned_lower = split(grads.T)
    stacked = jnp.concatenate([turned_upper, turned_lower], axis=0)
    start = 0
    for which, first, last in pieces:
        upper, lower = split(inputs[which][:, first:last])
        one = jnp.dot(stacked, upper, preferred_element_type=f32)
        two = jnp.dot(turned_upper, lower, preferred_element_type=f32)
        total[:, start : start + last - first] += one[:columns] + one[columns:] + two
        start += last - first

    @pl.when(step == pl.num_programs(0) - 1)
    def finish():
        parts, _, width = out_ref.shape
        for part in range(parts):
            out_ref[part] = total[part * width : (part + 1) * width].T


def frame_product(inputs, grads, pieces):
    sources, groups, frames = grads.shape[:3]
    parts = lax.axis_size("section")
    block = 4 if sources % 4 == 0 else 1
    columns = groups // parts * lanes
    depth = sum(last - first for _, first, last in pieces)

    def block_spec(array):
        return pl.BlockSpec((block * frames, array.shape[1]), lambda step: (step, 0))

    return pl.pallas_call(
        functools.partial(frame_product_kernel, pieces),
        grid=(sources // block,),
        in_specs=[block_spec(array) for array in inputs]
        + [pl.BlockSpec((block, groups, frames, lanes), lambda step: (step, 0, 0, 0))],
        out_specs=pl.BlockSpec((parts, depth, columns), lambda step: (0, 0, 0)),
        out_shape=jax.ShapeDtypeStruct((parts, depth, columns), f32),
        scratch_shapes=[pltpu.VMEM((parts * columns, depth), f32)],
        compiler_params=params(),
        name="frame_product",
    )(*inputs, grads)


def whole_spec(array):
    rank = len(array.shape)
    return pl.BlockSpec(array.shape, lambda step: (0,) * rank)


def timed_spec(array, place, depth=None):
    shape = (1,) + tuple(array.shape[1:])
    rank = len(array.shape)
    return pl.BlockSpec(shape, lambda step: (place(step),) + (0,) * (rank - 1))


def shard_spec(array, place):
    shape = (shard_block,) + tuple(array.shape[1:])
    return pl.BlockSpec(shape, lambda step: (place(step), 0, 0))


def zone_spec(zone, place, which):
    shape = (1, 2) + tuple(zone.shape[2:])
    return pl.BlockSpec(shape, lambda step: (place(step), which, 0, 0))


def out_spec(shape):
    rank = len(shape)
    return pl.BlockSpec(shape, lambda step: (0,) * rank)


def cost(weights, passes):
    return pl.CostEstimate(flops=2 * 256 * weights * 2 * passes, bytes_accessed=4 * weights, transcendentals=0)


def params():
    return pltpu.CompilerParams(vmem_limit_bytes=vmem_limit, dimension_semantics=("arbitrary",))


def attention_forward(
    weight, prenet_out, bias, loc_map, processed, memory, query_weight, energy_v, zone, resume, allowed, lag, awaited
):
    groups, depth = weight.shape[:2]
    blocks = groups // shard_block
    rows = memory.shape[0] // (processed.shape[1] // lanes)
    positions = processed.shape[1] // lanes
    columns = groups * lanes
    units = columns // 4
    context_width = memory.shape[1]
    frame_rows = prenet_out.shape[0]
    rest = depth - prenet_out.shape[1]
    width = shard_block * lanes
    pair = 2 * rows

    def shard(step):
        return jnp.minimum(step, blocks - 1)

    def timed(step):
        return jnp.clip(step - blocks, 0, span - 1)

    def later(step):
        return timed(step) + lag

    timed_shapes = [
        (span, pair, units),
        (span, pair, units),
        (span, pair, context_width),
        (span, pair, columns),
        (span, pair, positions * lanes),
        (span, pair, lanes),
        (span, pair, lanes),
    ]
    out_shape = [jax.ShapeDtypeStruct(shape, f32) for shape in timed_shapes]
    bias_blocks = bias.reshape(blocks, 1, width)
    return pl.pallas_call(
        functools.partial(attention_forward_kernel, blocks, rows, positions, lag),
        grid=(blocks + span,),
        in_specs=[
            shard_spec(weight, shard),
            whole_spec(prenet_out),
            timed_spec(bias_blocks, shard),
            whole_spec(loc_map),
            whole_spec(processed),
            whole_spec(memory),
            whole_spec(query_weight),
            whole_spec(energy_v),
            zone_spec(zone, timed, 0),
            zone_spec(zone, later, 0),
            timed_spec(resume, timed),
            whole_spec(allowed),
            pl.BlockSpec(memory_space=pl.ANY),
        ],
        out_specs=[timed_spec(shape, timed) for shape in out_shape],
        out_shape=out_shape,
        scratch_shapes=[
            pltpu.VMEM((blocks, rest, width), bf16),
            pltpu.VMEM((blocks, rest, width), bf16),
            pltpu.VMEM((blocks, frame_rows, width), f32),
            pltpu.VMEM(loc_map.shape, bf16),
            pltpu.VMEM(loc_map.shape, bf16),
            pltpu.VMEM(memory.shape, bf16),
            pltpu.VMEM(memory.shape, bf16),
            pltpu.VMEM(query_weight.shape, bf16),
            pltpu.VMEM(query_weight.shape, bf16),
            pltpu.VMEM((pair, columns), f32),
            pltpu.VMEM((pair, units), f32),
            pltpu.VMEM((pair, units), f32),
            pltpu.VMEM((pair, context_width), f32),
            pltpu.VMEM((pair, lanes), f32),
        ],
        compiler_params=params(),
        cost_estimate=cost(depth * columns, span),
        name="attention_forward",
    )(
        weight,
        prenet_out,
        bias_blocks,
        loc_map,
        processed,
        memory,
        query_weight,
        energy_v,
        zone,
        zone,
        resume,
        allowed,
        awaited,
    )


def decoder_forward(weight, frames, bias, zone, resume, rows, lag, awaited):
    groups = weight.shape[0]
    blocks = groups // shard_block
    columns = groups * lanes
    units = columns // 4
    width = shard_block * lanes
    pair = 2 * rows

    def shard(step):
        return jnp.minimum(step, blocks - 1)

    def timed(step):
        return jnp.clip(step - blocks, 0, span - 1)

    def later(step):
        return timed(step) + lag

    timed_shapes = [(span, pair, units), (span, pair, units), (span, pair, columns)]
    out_shape = [jax.ShapeDtypeStruct(shape, f32) for shape in timed_shapes]
    bias_blocks = bias.reshape(blocks, 1, width)
    return pl.pallas_call(
        functools.partial(decoder_forward_kernel, blocks, rows, lag, len(awaited)),
        grid=(blocks + span,),
        in_specs=[
            shard_spec(weight, shard),
            whole_spec(frames),
            timed_spec(bias_blocks, shard),
            zone_spec(zone, timed, 1),
            zone_spec(zone, later, 1),
            timed_spec(resume, timed),
        ]
        + [pl.BlockSpec(memory_space=pl.ANY)] * len(awaited),
        out_specs=[timed_spec(shape, timed) for shape in out_shape],
        out_shape=out_shape,
        scratch_shapes=[
            pltpu.VMEM((blocks, units, width), bf16),
            pltpu.VMEM((blocks, units, width), bf16),
            pltpu.VMEM((blocks, frames.shape[0], width), f32),
            pltpu.VMEM((pair, columns), f32),
            pltpu.VMEM((pair, units), f32),
            pltpu.VMEM((pair, units), f32),
        ],
        compiler_params=params(),
        cost_estimate=cost(weight.shape[1] * columns, span // 2),
        name="decoder_forward",
    )(weight, frames, bias_blocks, zone, zone, resume, *awaited)


def decoder_backward(weight, grad, gates, cells, zone, resume, valid, rows, lag, awaited):
    groups, depth = weight.shape[:2]
    blocks = groups // shard_block
    columns = groups * lanes
    units = columns // 4
    split_row = depth - units
    width = shard_block * lanes
    pair = 2 * rows
    frame_rows = grad.shape[0]
    part = math.gcd(units, split_row)
    own_parts = units // part
    in_parts = split_row // part

    def part_spec(index):
        return pl.BlockSpec((shard_block, part, lanes), index)

    def own_spec(which):
        return part_spec(lambda step: (shard(step), in_parts + which, 0))

    def in_spec(which):
        return part_spec(lambda step: (last_shard(step), which, 0))

    def shard(step):
        return jnp.minimum(step, blocks - 1)

    def last_shard(step):
        return jnp.clip(step - blocks - span, 0, blocks - 1)

    def timed(step):
        return span - 1 - jnp.clip(step - blocks, 0, span - 1)

    def later(step):
        return timed(step) + lag

    def before(step):
        return jnp.maximum(timed(step) - 1, 0)

    out_shape = [
        jax.ShapeDtypeStruct((groups, frame_rows, lanes), f32),
        jax.ShapeDtypeStruct((frame_rows, split_row), f32),
    ]
    return pl.pallas_call(
        functools.partial(decoder_backward_kernel, blocks, rows, lag, own_parts, in_parts, len(awaited)),
        grid=(2 * blocks + span,),
        in_specs=[own_spec(which) for which in range(own_parts)]
        + [in_spec(which) for which in range(in_parts)]
        + [
            whole_spec(grad),
            timed_spec(gates, timed),
            timed_spec(cells, before),
            zone_spec(zone, timed, 1),
            zone_spec(zone, later, 1),
            timed_spec(resume, timed),
            timed_spec(valid, timed),
        ]
        + [pl.BlockSpec(memory_space=pl.ANY)] * len(awaited),
        out_specs=[shard_spec(out_shape[0], last_shard), whole_spec(out_shape[1])],
        out_shape=out_shape,
        scratch_shapes=[
            pltpu.VMEM((blocks, units, width), bf16),
            pltpu.VMEM((blocks, units, width), bf16),
            pltpu.VMEM((blocks, frame_rows, width), f32),
            pltpu.VMEM((pair, units), f32),
            pltpu.VMEM((pair, units), f32),
        ],
        compiler_params=params(),
        cost_estimate=cost(depth * columns, 4 * span),
        name="decoder_backward",
    )(*[weight] * (own_parts + in_parts), grad, gates, cells, zone, zone, resume, valid, *awaited)


def attention_backward(
    weight,
    grad_in,
    grad_out,
    gates,
    cells,
    bent,
    weights,
    window,
    loc_map,
    memory,
    query_weight,
    energy_v,
    zone,
    resume,
    valid,
    next_resume,
    rows,
    positions,
    prenet_width,
    lag,
    awaited,
):
    groups, depth = weight.shape[:2]
    blocks = groups // shard_block
    columns = groups * lanes
    units = columns // 4
    width = shard_block * lanes
    pair = 2 * rows
    frame_rows = grad_in.shape[0]
    context_width = memory.shape[1]
    rest = depth - prenet_width

    def shard(step):
        return jnp.minimum(step, blocks - 1)

    def timed(step):
        return span - 1 - jnp.clip(step - blocks, 0, span - 1)

    def later(step):
        return timed(step) + lag

    def before(step):
        return jnp.maximum(timed(step) - 1, 0)

    shapes = [
        (groups, frame_rows, lanes),
        (1, columns),
        (frame_rows, prenet_width),
        (frame_rows, lanes),
        (rows, positions * lanes),
        (rows * positions, context_width),
        loc_map.shape,
        (pair, lanes),
    ]
    return pl.pallas_call(
        functools.partial(attention_backward_kernel, blocks, rows, positions, lag),
        grid=(blocks + span,),
        in_specs=[
            shard_spec(weight, shard),
            whole_spec(grad_in),
            whole_spec(grad_out),
            timed_spec(gates, timed),
            timed_spec(cells, before),
            timed_spec(bent, timed),
            timed_spec(weights, timed),
            timed_spec(window, timed),
            whole_spec(loc_map),
            whole_spec(memory),
            whole_spec(query_weight),
            whole_spec(energy_v),
            zone_spec(zone, timed, 0),
            zone_spec(zone, later, 0),
            timed_spec(resume, timed),
            timed_spec(valid, timed),
            whole_spec(next_resume),
        ]
        + [pl.BlockSpec(memory_space=pl.ANY)] * len(awaited),
        out_specs=[out_spec(shape) for shape in shapes],
        out_shape=[jax.ShapeDtypeStruct(shape, f32) for shape in shapes],
        scratch_shapes=[
            pltpu.VMEM((blocks, rest, width), bf16),
            pltpu.VMEM((blocks, rest, width), bf16),
            pltpu.VMEM((blocks, prenet_width, width), bf16),
            pltpu.VMEM((blocks, prenet_width, width), bf16),
            pltpu.VMEM((blocks, frame_rows, width), f32),
            pltpu.VMEM(loc_map.shape, bf16),
            pltpu.VMEM(loc_map.shape, bf16),
            pltpu.VMEM(memory.shape, bf16),
            pltpu.VMEM(memory.shape, bf16),
            pltpu.VMEM(query_weight.shape, bf16),
            pltpu.VMEM(query_weight.shape, bf16),
            pltpu.VMEM((span * pair, positions * lanes), f32),
            pltpu.VMEM((span * pair, context_width), f32),
            pltpu.VMEM((span * pair, rows * positions), f32),
            pltpu.VMEM((span * pair, lanes), f32),
            pltpu.VMEM((pair, units), f32),
            pltpu.VMEM((pair, units), f32),
            pltpu.VMEM((pair, context_width), f32),
            pltpu.VMEM((pair, lanes), f32),
        ],
        compiler_params=params(),
        cost_estimate=cost(lanes * lanes, 1),
        name="attention_backward",
    )(
        weight,
        grad_in,
        grad_out,
        gates,
        cells,
        bent,
        weights,
        window,
        loc_map,
        memory,
        query_weight,
        energy_v,
        zone,
        zone,
        resume,
        valid,
        next_resume,
        *awaited,
    )


def dot(left, right, left_dim=1, right_dim=0):
    return lax.dot_general(
        left, right, (((left_dim,), (right_dim,)), ((), ())), precision=high, preferred_element_type=f32
    )


def gather_columns(shard):
    depth, width = shard.shape
    if width % lanes:
        full = lax.all_gather(shard, both, axis=1, tiled=True)
        return full.reshape(depth, -1, lanes).swapaxes(0, 1)
    stacked = lax.all_gather(shard, both, axis=0)
    if width == lanes:
        return stacked
    return stacked.reshape(-1, depth, width // lanes, lanes).swapaxes(1, 2).reshape(-1, depth, lanes)


def along_core(values):
    return lax.ppermute(values, "section", [(place, place ^ 1) for place in range(4)])


def along_y(values):
    return lax.ppermute(values, "section", [(place, place ^ 2) for place in range(4)])


def gather_y(values):
    return jnp.stack([values, along_y(values)])


def gather_core(two):
    return jnp.concatenate([two, along_core(two)], axis=0)


def list_section(values):
    other = along_y(values)
    return [values, other, along_core(values), along_core(other)]


def gather_section(values):
    return gather_core(gather_y(values))


def section_order(four, own):
    entries = []
    for place in range(4):
        offset = own ^ place
        held = (offset % 2) * 2 + offset // 2
        entries.append(lax.dynamic_index_in_dim(four, held, 0, keepdims=False))
    return entries


def section_columns(pair, layers):
    own = lax.axis_index("section")
    four = gather_core(pair)
    depth = four.shape[1] // layers
    whole = []
    for layer in range(layers):
        blocks = section_order(four[:, layer * depth : (layer + 1) * depth], own)
        whole.append(jnp.concatenate(blocks, axis=1))
    return whole


def own_columns(values, columns):
    own = lax.axis_index("section")
    total = values[..., :columns]
    for place in range(1, values.shape[-1] // columns):
        total = jnp.where(own == place, values[..., place * columns : (place + 1) * columns], total)
    return total


def flat_join(arrays, devices):
    pieces = []
    for array in arrays:
        flat = array.reshape(-1)
        flat = jnp.pad(flat, (0, -flat.shape[0] % lanes))
        pieces.append(flat.reshape(-1, lanes))
    joined = jnp.concatenate(pieces, axis=0)
    joined = jnp.pad(joined, ((0, -joined.shape[0] % (8 * devices)), (0, 0)))
    return joined.reshape(devices, -1, lanes)


def part_sum(joined):
    return jnp.sum(lax.all_to_all(joined, both, 0, 0), axis=0)


def flat_whole(part, devices):
    return lax.all_to_all(jnp.broadcast_to(part[None], (devices,) + part.shape), both, 0, 0)


def flat_split(whole, arrays):
    whole = whole.reshape(-1, lanes)
    sums = []
    start = 0
    for array in arrays:
        count = -(-array.size // lanes)
        flat = whole[start : start + count].reshape(-1)
        sums.append(flat[: array.size].reshape(array.shape))
        start += count
    return sums


def exchange_ring(grads, extra=None):
    groups, frames, width = grads.shape
    size = lax.axis_size("dp")
    if extra is None:
        return lax.all_to_all(grads.reshape(size, groups // size, frames, width), "dp", 0, 0)
    joined = jnp.concatenate([grads.reshape(size, -1, width), extra], axis=1)
    received = lax.all_to_all(joined, "dp", 0, 0)
    count = groups // size * frames
    return received[:, :count].reshape(size, -1, frames, width), jnp.sum(received[:, count:], axis=0)


def sum_section(parts):
    own = lax.axis_index("section")
    core, place = own % 2, own // 2
    pairs = parts.reshape((2, 2) + parts.shape[1:])
    mine = jnp.where(core == 0, pairs[:, 0], pairs[:, 1])
    other = jnp.where(core == 0, pairs[:, 1], pairs[:, 0])
    pair = mine + along_core(other)
    mine = jnp.where(place == 0, pair[0], pair[1])
    other = jnp.where(place == 0, pair[1], pair[0])
    return mine + along_y(other)


def gathers_inputs(frame_rows, columns, devices):
    return frame_rows * devices <= columns


def column_gradients(inputs, pieces, received, grads):
    if received is not None:
        return sum_section(frame_product(inputs, received, pieces))
    groups, frames, width = grads.shape
    flat = grads.swapaxes(0, 1).reshape(frames, groups * width)
    parts = [
        lax.psum_scatter(dot(inputs[which][:, first:last], flat, 0, 0), both, scatter_dimension=1, tiled=True)
        for which, first, last in pieces
    ]
    return jnp.concatenate(parts, axis=0)


def gelu_slope(values):
    return jax.vjp(jax.nn.gelu, values)


def location_map(loc_filters, loc_dense, positions):
    filters, channels, taps = loc_filters.shape
    features = loc_dense.shape[1]
    joined = dot(loc_filters.reshape(filters, channels * taps), loc_dense, 0, 0)
    joined = joined.reshape(channels, taps, features)
    margin = taps // 2
    padded = jnp.pad(joined, ((0, 0), (positions, positions), (0, 0)))
    columns = [
        padded[:, positions + margin - place : 2 * positions + margin - place] for place in range(positions)
    ]
    spread_map = jnp.stack(columns, axis=2).reshape(channels * positions, positions * features)
    return jnp.pad(spread_map, ((0, lanes - channels * positions), (0, 0)))


def location_unmap(grad_map, channels, taps, positions, features):
    grads = grad_map[: channels * positions].reshape(channels, positions, positions, features)
    turned = jnp.flip(grads.swapaxes(1, 2), axis=1)
    padded = jnp.pad(turned, ((0, 0), (0, 0), (0, positions), (0, 0))).reshape(channels, -1, features)
    length = 2 * positions - 1
    skewed = padded[:, : positions * length].reshape(channels, positions, length, features)
    start = positions - 1 - taps // 2
    return jnp.sum(skewed[:, :, start : start + taps], axis=1)


def per_device(
    memory,
    enc_lengths,
    frame_segment,
    mel_target,
    prenet_keep,
    zone_keep,
    pre_first,
    pre_second,
    att_weight,
    att_bias,
    query_weight,
    memory_weight,
    loc_filters,
    loc_dense,
    energy_v,
    dec_weight,
    dec_bias,
    proj_weight,
    proj_bias,
    stop_weight,
    post_first,
    post_mid,
    post_last,
    norm_gain,
    norm_shift,
    last_gain,
    last_shift,
    grad_after,
    grad_stop,
):
    devices = lax.axis_size("dp") * lax.axis_size("section")
    rows, positions, context_width = memory.shape
    frames = frame_segment.shape[1]
    mel = mel_target.shape[2]
    units = att_bias.shape[0] // 4
    prenet_width = pre_first.shape[1]
    features = memory_weight.shape[1]
    lag = frames - span
    frame_rows = frames * rows

    att_all = gather_columns(att_weight)
    dec_all = gather_columns(dec_weight)
    mid_pair = gather_y(post_mid.reshape(-1, post_mid.shape[3]))
    mid_all = section_columns(mid_pair, 3)
    post_split = [split_matrix(weight.reshape(-1, weight.shape[-1])) for weight in [post_first] + mid_all + [post_last]]

    segment = frame_segment.T
    earlier = jnp.concatenate([segment[:1] - 1, segment[:-1]], axis=0)
    resume = (segment == earlier).astype(f32)
    shifted = jnp.concatenate([jnp.zeros_like(mel_target[:, :1]), mel_target[:, :-1]], axis=1)
    frames_in = (shifted.swapaxes(0, 1) * resume[:, :, None]).reshape(frame_rows, mel)
    keep = prenet_keep.transpose(1, 2, 0, 3).astype(f32) * 2.0
    keep_first = keep[:, 0].reshape(frame_rows, prenet_width)
    keep_second = keep[:, 1].reshape(frame_rows, prenet_width)
    gelu_first, first_back = gelu_slope(dot(frames_in, pre_first))
    pre_hidden = gelu_first * keep_first
    gelu_second, second_back = gelu_slope(dot(pre_hidden, pre_second))
    prenet_out = gelu_second * keep_second
    memory_flat = memory.reshape(rows * positions, context_width)
    processed = dot(memory_flat, memory_weight)
    loc_map = location_map(loc_filters, loc_dense, positions)
    zone = zone_keep.transpose(1, 2, 0, 3)

    first_part = segment == 0
    steps = jnp.arange(span)
    never = jnp.ones((span, rows), f32)
    resume_pair = jnp.concatenate([never, resume[lag:]], axis=1)[:, :, None]
    valid_pair = jnp.concatenate([first_part[:span], ~first_part[lag:]], axis=1).astype(f32)[:, :, None]
    encoder_first = jnp.arange(lanes)[None, :] < enc_lengths[:, :1]
    inside = jnp.arange(lanes)[None, :] < positions
    allowed = jnp.concatenate([encoder_first, inside & ~encoder_first], axis=0).astype(f32)
    next_resume = jnp.concatenate([resume[1:], jnp.zeros((1, rows), f32)], axis=0).reshape(frame_rows, 1)

    def to_frames(pairs):
        early = jnp.pad(pairs[:, :rows], ((0, lag), (0, 0), (0, 0)))
        late = jnp.pad(pairs[:, rows:], ((lag, 0), (0, 0), (0, 0)))
        return jnp.where(first_part[:, :, None], early, late).reshape(frame_rows, -1)

    energy_row = energy_v.reshape(1, features)
    processed_wide = processed.reshape(rows, positions * features)
    hidden, cells, contexts, gates, bent, weights, window = attention_forward(
        att_all,
        prenet_out,
        att_bias,
        loc_map,
        processed_wide,
        memory_flat,
        query_weight,
        energy_row,
        zone,
        resume_pair,
        allowed,
        lag,
        mid_pair,
    )
    att_frames = to_frames(hidden)
    context_frames = to_frames(contexts)
    dec_inputs = jnp.concatenate([att_frames, context_frames], axis=1)
    dec_hidden, dec_cells, dec_gates = decoder_forward(
        dec_all, dec_inputs, dec_bias, zone, resume_pair, rows, lag, [part for pair in post_split for part in pair]
    )
    dec_frames = to_frames(dec_hidden)

    prenet_later = jnp.concatenate([prenet_out[rows:], jnp.zeros((rows, prenet_width), f32)], axis=0)
    att_inputs_all = jnp.concatenate([prenet_later, context_frames, att_frames], axis=1)
    dec_earlier = jnp.concatenate([jnp.zeros((rows, units), f32), dec_frames[:-rows]], axis=0)
    dec_earlier = dec_earlier * resume.reshape(frame_rows, 1)
    dec_inputs_all = dec_earlier
    input_width = att_inputs_all.shape[1]
    input_pieces = []
    rings = gathers_inputs(frame_rows, 4 * units, devices)
    if rings:
        att_inputs_all = lax.all_gather(att_inputs_all, "dp", axis=0, tiled=True)
        dec_inputs_all = lax.all_gather(dec_inputs_all, "dp", axis=0, tiled=True)
        input_pieces = [att_inputs_all, dec_inputs_all]

    out_frames = jnp.concatenate([dec_frames, context_frames], axis=1)
    mel_before = dot(out_frames, proj_weight) + proj_bias
    stop_logit = jnp.sum(out_frames * stop_weight, axis=1).reshape(frames, rows).T

    section_size = lax.axis_size("section")
    kernel = post_first.shape[0]
    margin = kernel // 2
    padded = jnp.pad(segment, ((margin, margin), (0, 0)), constant_values=-1)
    same_segment = jnp.stack(
        [padded[offset : offset + frames] == segment for offset in range(kernel)], axis=2
    ).astype(f32)
    same = jnp.pad(same_segment, ((0, 0), (0, 0), (0, 8 - kernel))).reshape(frame_rows, 8)
    same_all = list_section(same)
    frame_count = frame_rows * devices
    gains = [norm_gain[layer : layer + 1] for layer in range(4)] + [last_gain.reshape(1, mel)]
    shifts = [norm_shift[layer : layer + 1] for layer in range(4)] + [last_shift.reshape(1, mel)]
    widths = [post_first.shape[2]] * 4 + [mel]
    grad_after_frames = grad_after.swapaxes(0, 1).reshape(frame_rows, mel)
    conv, copies = post_call(
        functools.partial(post_first_kernel, rows),
        [(frame_rows, widths[0]), (devices, 8, lanes)],
        "post_first",
        (mel_before, same, *post_split[0]),
    )
    scaled, inverse, active, inputs_all = [], [], [], []
    inputs_all.append(list_section(jnp.pad(mel_before, ((0, 0), (0, lanes - mel)))))
    for layer in range(4):
        scaled_now, active_now, inverse_now, conv, copies = post_call(
            functools.partial(post_next_kernel, rows, frame_count),
            [
                (frame_rows, widths[layer]),
                (frame_rows, widths[layer]),
                (1, widths[layer]),
                (frame_rows, widths[layer + 1]),
                (devices, 8, lanes),
            ],
            "post_next",
            (conv, share_sums(copies), gains[layer], shifts[layer], same, *post_split[layer + 1])
            + ((grad_after_frames,) if layer == 3 else ()),
        )
        scaled.append(scaled_now)
        active.append(active_now)
        inverse.append(inverse_now)
        inputs_all.append(list_section(active_now))
    mel_after, grad_conv, packed, upstream, copies = post_call(
        functools.partial(post_turn_kernel, rows, frame_count),
        [(frame_rows, mel), (frame_rows, lanes), (8, lanes), (frame_rows, widths[3]), (devices, 8, lanes)],
        "post_turn",
        (
            grad_after_frames,
            conv,
            share_sums(copies),
            mel_before,
            gains[4],
            shifts[4],
            same,
            *post_split[4],
            active[3],
            scaled[3],
        ),
    )
    weight_grads = [None] * 5
    gain_grads = [None] * 5
    shift_grads = [None] * 5
    shift_grads[4], gain_grads[4] = [row.reshape(-1) for row in unpack_sums(packed, mel)]
    weight_grads[4] = tap_gradient(
        inputs_all[4], list_section(grad_conv), same_all, kernel, rows, mel, split_inputs=True
    )
    for layer in reversed(range(4)):
        below = (active[layer - 1], scaled[layer - 1]) if layer else ()
        awaited = (weight_grads[layer + 2],) if layer < 3 else ()
        outs = [(frame_rows, widths[layer]), (8, lanes), (frame_rows, widths[layer - 1] if layer else mel)]
        if layer:
            outs.append((devices, 8, lanes))
        results = post_call(
            functools.partial(post_back_kernel, rows, frame_count, layer > 0, len(awaited)),
            outs,
            "post_back",
            (
                upstream,
                scaled[layer],
                share_sums(copies),
                inverse[layer],
                gains[layer],
                same,
                *post_split[layer],
                *below,
            ),
            awaited,
        )
        grad_conv, packed, upstream = results[:3]
        if layer:
            copies = results[3]
        shift_grads[layer], gain_grads[layer] = [row.reshape(-1) for row in unpack_sums(packed, widths[layer])]
        depth = widths[layer - 1] if layer else mel
        weight_grads[layer] = tap_gradient(inputs_all[layer], list_section(grad_conv), same_all, kernel, rows, depth)

    grad_mel = grad_after_frames + upstream
    grad_stop_frames = grad_stop.T.reshape(frame_rows, 1)
    grad_out = dot(grad_mel, proj_weight, 1, 1) + grad_stop_frames * stop_weight
    mel_grads = jnp.pad(
        jnp.concatenate([grad_mel, grad_stop_frames], axis=1), ((0, 0), (0, lanes - mel - 1))
    )
    mel_grads_all = jnp.concatenate(list_section(mel_grads), axis=0)
    outs_own = jnp.concatenate(
        [own_columns(outs, out_frames.shape[1] // section_size) for outs in list_section(out_frames)], axis=0
    )
    g_proj_part = dot(outs_own, mel_grads_all, 0, 0)
    group_grads, group_token = join_rows(
        [grad.reshape(-1, lanes) for grad in weight_grads + [g_proj_part]]
        + [jnp.pad(jnp.sum(mel_grads_all, axis=0, keepdims=True), ((0, 7), (0, 0)))],
        input_pieces,
    )
    group_sums = lax.psum(group_grads, "dp")
    dec_sums, grad_dec_inputs = decoder_backward(
        dec_all,
        grad_out,
        dec_gates,
        dec_cells,
        zone,
        resume_pair,
        valid_pair,
        rows,
        lag,
        [group_token],
    )
    g_dec_bias = jnp.sum(dec_sums, axis=1).reshape(-1)
    dec_columns = exchange_ring(dec_sums) if rings else None
    (
        att_sums,
        g_att_bias,
        grad_prenet,
        grad_query,
        grad_processed,
        grad_memory,
        grad_loc,
        grad_energy,
    ) = attention_backward(
        att_all,
        grad_dec_inputs,
        grad_out,
        gates,
        cells,
        bent,
        weights,
        window,
        loc_map,
        memory_flat,
        query_weight,
        energy_row,
        zone,
        resume_pair,
        valid_pair,
        next_resume,
        rows,
        positions,
        prenet_width,
        lag,
        (group_token,),
    )

    grad_processed = grad_processed.reshape(rows * positions, features)
    grad_memory = grad_memory + dot(grad_processed, memory_weight, 1, 1)
    g_memory_weight = dot(memory_flat, grad_processed, 0, 0)
    g_query_weight = dot(att_frames, grad_query, 0, 0)
    (grad_second,) = second_back(grad_prenet * keep_second)
    g_pre_second = dot(pre_hidden, grad_second, 0, 0)
    (grad_first,) = first_back(dot(grad_second, pre_second, 1, 1) * keep_first)
    g_pre_first = dot(frames_in, grad_first, 0, 0)
    filters, channels, taps = loc_filters.shape
    grad_joined = location_unmap(grad_loc, channels, taps, positions, features)
    late_grads = (
        g_pre_first,
        g_pre_second,
        g_att_bias,
        g_query_weight,
        g_memory_weight,
        grad_joined,
        jnp.sum(grad_energy, axis=0),
        g_dec_bias,
    )
    context_end = prenet_width + context_width
    dec_part = column_gradients(
        [att_inputs_all, dec_inputs_all],
        ((0, context_end, input_width), (0, prenet_width, context_end), (1, 0, units)),
        dec_columns,
        dec_sums,
    )
    late_joined = flat_join(late_grads, devices)
    if rings:
        late_ring = sum_section(late_joined.reshape((-1, 4) + late_joined.shape[1:]).swapaxes(0, 1))
        late_ring = late_ring + 0.0 * (dec_columns[0, 0, 0, 0] + group_sums[0, 0])
        att_columns, late_part = exchange_ring(att_sums, late_ring)
    else:
        att_columns = None
        late_part = part_sum(late_joined)
    att_part = column_gradients([att_inputs_all], ((0, 0, input_width),), att_columns, att_sums)

    late_sums = flat_split(flat_whole(late_part, devices), late_grads)
    grad_joined = late_sums[5].reshape(channels * taps, features)
    g_loc_filters = dot(loc_dense, grad_joined, 1, 1).reshape(loc_filters.shape)
    g_loc_dense = dot(loc_filters.reshape(filters, channels * taps), grad_joined)

    first_rows = kernel * mel
    mid_end = first_rows + post_mid.size // lanes
    proj_start = mid_end + first_rows
    proj_end = proj_start + out_frames.shape[1] // section_size
    mid_part = group_sums[first_rows:mid_end].reshape(post_mid.shape)
    own = lax.axis_index("section")
    shared = jnp.concatenate([group_sums[:first_rows], group_sums[mid_end:proj_end]], axis=0)
    shared_all = section_order(gather_section(shared), own)
    g_post_first = jnp.concatenate(
        [piece[:first_rows].reshape(kernel, mel, lanes) for piece in shared_all], axis=2
    )
    g_post_last = jnp.concatenate(
        [piece[first_rows : 2 * first_rows].reshape(kernel, mel, lanes) for piece in shared_all], axis=2
    ).swapaxes(1, 2)
    g_proj = jnp.concatenate([piece[2 * first_rows :] for piece in shared_all], axis=0)
    g_proj_bias = group_sums[proj_end, :mel]
    return (
        mel_after.reshape(frames, rows, mel).swapaxes(0, 1),
        stop_logit,
        grad_memory.reshape(memory.shape),
        late_sums[0],
        late_sums[1],
        att_part,
        late_sums[2].reshape(-1),
        late_sums[3],
        late_sums[4],
        g_loc_filters,
        g_loc_dense,
        late_sums[6],
        dec_part,
        late_sums[7],
        g_proj[:, :mel],
        g_proj_bias,
        g_proj[:, mel],
        g_post_first,
        mid_part,
        g_post_last,
        jnp.stack(gain_grads[:4]),
        jnp.stack(shift_grads[:4]),
        gain_grads[4],
        shift_grads[4],
    )


def solution(mesh):
    rows_only = P(both)
    columns_only = P(None, both)
    mid_spec = P(None, None, None, "section")
    placed = (
        (rows_only,) * 6
        + (P(), P(), columns_only)
        + (P(),) * 6
        + (columns_only,)
        + (P(),) * 5
        + (mid_spec,)
        + (P(),) * 5
        + (rows_only, rows_only)
    )
    given = (
        (rows_only,) * 3
        + (P(), P(), columns_only)
        + (P(),) * 6
        + (columns_only,)
        + (P(),) * 5
        + (mid_spec,)
        + (P(),) * 5
    )
    return jax.shard_map(per_device, mesh=mesh, in_specs=placed, out_specs=given, check_vma=False)
```

```python
import functools
import math

import jax
import jax.numpy as jnp
from jax import lax
from jax.experimental import pallas as pl
from jax.experimental.pallas import tpu as pltpu
from jax.sharding import PartitionSpec as P

high = lax.Precision.HIGH
norm_eps = 1e-05
f32 = jnp.float32
bf16 = jnp.bfloat16
both = ("dp", "section")
lanes = 128
vmem_limit = 62 * 1024 * 1024

span = 6
shard_block = 4


def split(values):
    upper = values.astype(bf16)
    lower = (values - upper.astype(f32)).astype(bf16)
    return upper, lower


def product(left, upper, lower, transposed=False):
    rows = left.shape[0]
    left_upper, left_lower = split(left)
    stacked = jnp.concatenate([left_upper, left_lower], axis=0)
    dims = (((1,), (1,)), ((), ())) if transposed else (((1,), (0,)), ((), ()))
    first = lax.dot_general(stacked, upper, dims, preferred_element_type=f32)
    second = lax.dot_general(left_upper, lower, dims, preferred_element_type=f32)
    return first[:rows] + first[rows:] + second


def sigmoid(values):
    return 0.5 * jnp.tanh(0.5 * values) + 0.5


def lane_index(shape):
    return lax.broadcasted_iota(jnp.int32, shape, 1)


def fold_lanes(values, positions):
    copies = values
    shift = positions
    while shift < lanes:
        copies = copies + pltpu.roll(copies, shift, 1)
        shift *= 2
    return copies


def diagonal_mask(rows, positions):
    shape = (2 * rows, rows * positions)
    row = lax.broadcasted_iota(jnp.int32, shape, 0)
    group = lax.broadcasted_iota(jnp.int32, shape, 1) // positions
    return group == jnp.where(row >= rows, row - rows, row)


def spread(weights, rows, positions):
    copies = fold_lanes(weights, positions)
    wide = jnp.concatenate([copies] * (rows * positions // lanes), axis=1)
    return jnp.where(diagonal_mask(rows, positions), wide, 0.0)


def collect(wide, rows, positions):
    kept = jnp.where(diagonal_mask(rows, positions), wide, 0.0)
    total = kept[:, :lanes]
    for start in range(lanes, rows * positions, lanes):
        total = total + kept[:, start : start + lanes]
    shift = positions
    while shift < lanes:
        total = total + pltpu.roll(total, shift, 1)
        shift *= 2
    return jnp.where(lane_index(total.shape) < positions, total, 0.0)


def store_parts(block_ref, first, last, upper_ref, lower_ref, index):
    for place in range(shard_block):
        upper, lower = split(block_ref[place, first:last, :])
        upper_ref[index, :, place * lanes : (place + 1) * lanes] = upper
        lower_ref[index, :, place * lanes : (place + 1) * lanes] = lower


def gate_forward(gate_sums, cell, hidden, zone_hidden, zone_cell):
    units = cell.shape[1]
    gate_in = sigmoid(gate_sums[:, :units])
    gate_keep = sigmoid(gate_sums[:, units : 2 * units])
    update = jnp.tanh(gate_sums[:, 2 * units : 3 * units])
    gate_out = sigmoid(gate_sums[:, 3 * units :])
    new_cell = gate_keep * cell + gate_in * update
    new_hidden = gate_out * jnp.tanh(new_cell)
    hidden = zone_hidden * hidden + (1.0 - zone_hidden) * new_hidden
    cell = zone_cell * cell + (1.0 - zone_cell) * new_cell
    return hidden, cell, (gate_in, gate_keep, update, gate_out)


def gate_backward(gates, cell, zone_hidden, zone_cell, grad_hidden, grad_cell):
    units = cell.shape[1]
    gate_in = gates[:, :units]
    gate_keep = gates[:, units : 2 * units]
    update = gates[:, 2 * units : 3 * units]
    gate_out = gates[:, 3 * units :]
    bent = jnp.tanh(gate_keep * cell + gate_in * update)
    grad_new = (1.0 - zone_hidden) * grad_hidden
    grad_new_cell = grad_new * gate_out * (1.0 - bent * bent) + (1.0 - zone_cell) * grad_cell
    grad_sums = (
        grad_new_cell * update * gate_in * (1.0 - gate_in),
        grad_new_cell * cell * gate_keep * (1.0 - gate_keep),
        grad_new_cell * gate_in * (1.0 - update * update),
        grad_new * bent * gate_out * (1.0 - gate_out),
    )
    return grad_sums, zone_hidden * grad_hidden, zone_cell * grad_cell + grad_new_cell * gate_keep


def zone_masks(early_ref, late_ref):
    masks = []
    for which in range(2):
        pair = jnp.concatenate([early_ref[0, which], late_ref[0, which]], axis=0)
        masks.append(pair.astype(f32))
    return masks


def attention_forward_kernel(
    blocks,
    rows,
    positions,
    lag,
    weight_ref,
    prenet_ref,
    bias_ref,
    loc_map_ref,
    processed_ref,
    memory_ref,
    query_ref,
    energy_ref,
    zone_early_ref,
    zone_late_ref,
    resume_ref,
    allowed_ref,
    awaited,
    hidden_out,
    cell_out,
    context_out,
    gates_out,
    bent_out,
    weights_out,
    window_out,
    upper,
    lower,
    inputs,
    loc_upper,
    loc_lower,
    memory_upper,
    memory_lower,
    query_upper,
    query_lower,
    sums,
    hidden,
    cell,
    context,
    window,
):
    step = pl.program_id(0)
    prenet_width = prenet_ref.shape[1]
    context_width = context.shape[1]
    units = hidden.shape[1]
    width = shard_block * lanes

    @pl.when(step == 0)
    def prepare():
        loc_upper[...], loc_lower[...] = split(loc_map_ref[...])
        memory_upper[...], memory_lower[...] = split(memory_ref[...])
        query_upper[...], query_lower[...] = split(query_ref[...])
        hidden[...] = jnp.zeros_like(hidden)
        cell[...] = jnp.zeros_like(cell)
        context[...] = jnp.zeros_like(context)
        window[...] = jnp.zeros_like(window)

    @pl.when(step < blocks)
    def load():
        store_parts(weight_ref, prenet_width, weight_ref.shape[1], upper, lower, step)
        first = jnp.concatenate([weight_ref[place, :prenet_width, :] for place in range(shard_block)], axis=1)
        first_upper, first_lower = split(first)
        inputs[step] = product(prenet_ref[...], first_upper, first_lower) + bias_ref[0]

    @pl.when(step >= blocks)
    def advance():
        frame = step - blocks
        resume = resume_ref[0]
        hidden_now = hidden[...] * resume
        cell_now = cell[...] * resume
        context_now = context[...] * resume
        window_now = window[...] * resume
        early = pl.multiple_of(frame * rows, rows)
        late = pl.multiple_of((frame + lag) * rows, rows)
        for block in range(blocks):
            taken = slice(block * width, (block + 1) * width)
            sums[:rows, taken] = inputs[block, pl.ds(early, rows), :]
            sums[rows:, taken] = inputs[block, pl.ds(late, rows), :]

        @pl.when(frame > 0)
        def recur():
            state = jnp.concatenate([context_now, hidden_now], axis=1)
            for block in range(blocks):
                taken = slice(block * width, (block + 1) * width)
                sums[:, taken] += product(state, upper[block], lower[block])

        zone_hidden, zone_cell = zone_masks(zone_early_ref, zone_late_ref)
        hidden_new, cell_new, gates = gate_forward(sums[...], cell_now, hidden_now, zone_hidden, zone_cell)
        for place, gate in enumerate(gates):
            gates_out[0, :, place * units : (place + 1) * units] = gate
        hidden[...] = hidden_new
        cell[...] = cell_new
        hidden_out[0] = hidden_new
        cell_out[0] = cell_new
        query = product(hidden_new, query_upper[...], query_lower[...])
        located = product(window_now, loc_upper[...], loc_lower[...])
        energy_v = energy_ref[...]
        lane = lane_index((2 * rows, lanes))
        energy = jnp.zeros((2 * rows, lanes), f32)
        for place in range(positions):
            taken = slice(place * lanes, (place + 1) * lanes)
            ready = processed_ref[:, taken]
            bent = jnp.tanh(query + jnp.concatenate([ready, ready], axis=0) + located[:, taken])
            bent_out[0, :, taken] = bent
            energy = jnp.where(lane == place, jnp.sum(bent * energy_v, axis=1, keepdims=True), energy)
        masked = jnp.where(allowed_ref[...] > 0.5, energy, -1000000000.0)
        exponent = jnp.exp(masked - jnp.max(masked, axis=1, keepdims=True))
        weights = exponent / jnp.sum(exponent, axis=1, keepdims=True)
        weights = jnp.where(lane < positions, weights, 0.0)
        weights_out[0] = weights
        window_out[0] = window_now
        second = (lane >= positions) & (lane < 2 * positions)
        window[...] = weights + pltpu.roll(weights, positions, 1) + jnp.where(second, window_now, 0.0)
        context_new = product(spread(weights, rows, positions), memory_upper[...], memory_lower[...])
        context[...] = context_new
        context_out[0] = context_new


def decoder_forward_kernel(
    blocks,
    rows,
    lag,
    awaited,
    weight_ref,
    frames_ref,
    bias_ref,
    zone_early_ref,
    zone_late_ref,
    resume_ref,
    *refs,
):
    hidden_out, cell_out, gates_out, upper, lower, inputs, sums, hidden, cell = refs[awaited:]
    step = pl.program_id(0)
    units = hidden.shape[1]
    width = shard_block * lanes

    @pl.when(step == 0)
    def prepare():
        hidden[...] = jnp.zeros_like(hidden)
        cell[...] = jnp.zeros_like(cell)

    @pl.when(step < blocks)
    def load():
        split_row = frames_ref.shape[1]
        store_parts(weight_ref, split_row, weight_ref.shape[1], upper, lower, step)
        first = jnp.concatenate([weight_ref[place, :split_row, :] for place in range(shard_block)], axis=1)
        first_upper, first_lower = split(first)
        inputs[step] = product(frames_ref[...], first_upper, first_lower) + bias_ref[0]

    @pl.when(step >= blocks)
    def advance():
        frame = step - blocks
        resume = resume_ref[0]
        hidden_now = hidden[...] * resume
        cell_now = cell[...] * resume
        early = pl.multiple_of(frame * rows, rows)
        late = pl.multiple_of((frame + lag) * rows, rows)
        for block in range(blocks):
            taken = slice(block * width, (block + 1) * width)
            sums[:rows, taken] = inputs[block, pl.ds(early, rows), :]
            sums[rows:, taken] = inputs[block, pl.ds(late, rows), :]

        @pl.when(frame > 0)
        def recur():
            for block in range(blocks):
                taken = slice(block * width, (block + 1) * width)
                sums[:, taken] += product(hidden_now, upper[block], lower[block])

        zone_hidden, zone_cell = zone_masks(zone_early_ref, zone_late_ref)
        hidden_new, cell_new, gates = gate_forward(sums[...], cell_now, hidden_now, zone_hidden, zone_cell)
        for place, gate in enumerate(gates):
            gates_out[0, :, place * units : (place + 1) * units] = gate
        hidden[...] = hidden_new
        cell[...] = cell_new
        hidden_out[0] = hidden_new
        cell_out[0] = cell_new


def add_frames(total_ref, grads, frame, rows, lag):
    early = pl.multiple_of(frame * rows, rows)
    late = pl.multiple_of((frame + lag) * rows, rows)
    total_ref[pl.ds(early, rows), :] += grads[:rows]
    total_ref[pl.ds(late, rows), :] += grads[rows:]


def decoder_backward_kernel(
    blocks,
    rows,
    lag,
    own_parts,
    in_parts,
    awaited,
    *refs,
):
    own_refs = refs[:own_parts]
    in_refs = refs[own_parts : own_parts + in_parts]
    (
        grad_ref,
        gates_ref,
        cell_ref,
        zone_early_ref,
        zone_late_ref,
        resume_ref,
        valid_ref,
    ) = refs[own_parts + in_parts : own_parts + in_parts + 7]
    grad_sums_out, grad_in_out, upper, lower, frame_sums, grad_hidden, grad_cell = refs[
        own_parts + in_parts + 7 + awaited :
    ]
    step = pl.program_id(0)
    units = grad_hidden.shape[1]
    width = shard_block * lanes

    @pl.when(step == 0)
    def prepare():
        grad_hidden[...] = jnp.zeros_like(grad_hidden)
        grad_cell[...] = jnp.zeros_like(grad_cell)
        frame_sums[...] = jnp.zeros_like(frame_sums)
        grad_in_out[...] = jnp.zeros_like(grad_in_out)

    @pl.when(step < blocks)
    def load():
        for which, own_ref in enumerate(own_refs):
            part = own_ref.shape[1]
            for place in range(shard_block):
                taken = slice(place * lanes, (place + 1) * lanes)
                own_upper, own_lower = split(own_ref[place])
                upper[step, which * part : (which + 1) * part, taken] = own_upper
                lower[step, which * part : (which + 1) * part, taken] = own_lower

    @pl.when((step >= blocks) & (step < blocks + span))
    def retreat():
        frame = span - 1 - (step - blocks)
        resume = resume_ref[0]
        early = pl.multiple_of(frame * rows, rows)
        late = pl.multiple_of((frame + lag) * rows, rows)
        arriving = jnp.concatenate(
            [grad_ref[pl.ds(early, rows), :units], grad_ref[pl.ds(late, rows), :units]], axis=0
        )
        total = grad_hidden[...] + arriving * valid_ref[0]
        cell_now = cell_ref[0] * jnp.where(frame > 0, resume, 0.0)
        zone_hidden, zone_cell = zone_masks(zone_early_ref, zone_late_ref)
        grad_sums, passed_hidden, passed_cell = gate_backward(
            gates_ref[0], cell_now, zone_hidden, zone_cell, total, grad_cell[...]
        )
        grad_cell[...] = passed_cell * resume
        grad_hidden[...] = passed_hidden
        for place, grads in enumerate(grad_sums):
            for part in range(units // width):
                block = place * (units // width) + part
                add_frames(frame_sums.at[block], grads[:, part * width : (part + 1) * width], frame, rows, lag)

        @pl.when(frame > 0)
        def recur():
            carried = grad_hidden[...]
            for place, grads in enumerate(grad_sums):
                for part in range(units // width):
                    block = place * (units // width) + part
                    taken = grads[:, part * width : (part + 1) * width]
                    carried = carried + product(taken, upper[block], lower[block], transposed=True)
            grad_hidden[...] = carried * resume

    @pl.when(step >= blocks + span)
    def pass_on():
        block = step - blocks - span
        grads = frame_sums[block]
        for place in range(shard_block):
            grad_sums_out[place] = grads[:, place * lanes : (place + 1) * lanes]
        for which, in_ref in enumerate(in_refs):
            part = in_ref.shape[1]
            taken = slice(which * part, (which + 1) * part)
            first = jnp.concatenate([in_ref[place] for place in range(shard_block)], axis=1)
            first_upper, first_lower = split(first)
            grad_in_out[:, taken] += product(grads, first_upper, first_lower, transposed=True)


def attention_backward_kernel(
    blocks,
    rows,
    positions,
    lag,
    weight_ref,
    grad_in_ref,
    grad_out_ref,
    gates_ref,
    cell_ref,
    bent_ref,
    weights_ref,
    window_ref,
    loc_map_ref,
    memory_ref,
    query_ref,
    energy_ref,
    zone_early_ref,
    zone_late_ref,
    resume_ref,
    valid_ref,
    next_resume_ref,
    awaited,
    grad_sums_out,
    grad_bias_out,
    grad_prenet_out,
    grad_query_out,
    grad_processed_out,
    grad_memory_out,
    grad_loc_out,
    grad_energy_out,
    upper,
    lower,
    first_upper,
    first_lower,
    frame_sums,
    loc_upper,
    loc_lower,
    memory_upper,
    memory_lower,
    query_upper,
    query_lower,
    grad_bent,
    grad_contexts,
    diagonals,
    windows,
    grad_hidden,
    grad_cell,
    grad_context,
    grad_window,
):
    step = pl.program_id(0)
    units = grad_hidden.shape[1]
    context_width = grad_context.shape[1]
    prenet_width = first_upper.shape[1]
    width = shard_block * lanes
    pair = 2 * rows

    @pl.when(step == 0)
    def prepare():
        loc_upper[...], loc_lower[...] = split(loc_map_ref[...])
        memory_upper[...], memory_lower[...] = split(memory_ref[...])
        query_upper[...], query_lower[...] = split(query_ref[...])
        grad_hidden[...] = jnp.zeros_like(grad_hidden)
        grad_cell[...] = jnp.zeros_like(grad_cell)
        grad_context[...] = jnp.zeros_like(grad_context)
        grad_window[...] = jnp.zeros_like(grad_window)
        frame_sums[...] = jnp.zeros_like(frame_sums)
        grad_query_out[...] = jnp.zeros_like(grad_query_out)
        grad_processed_out[...] = jnp.zeros_like(grad_processed_out)
        grad_energy_out[...] = jnp.zeros_like(grad_energy_out)

    @pl.when(step < blocks)
    def load():
        store_parts(weight_ref, prenet_width, weight_ref.shape[1], upper, lower, step)
        store_parts(weight_ref, 0, prenet_width, first_upper, first_lower, step)

    @pl.when(step >= blocks)
    def retreat():
        frame = span - 1 - (step - blocks)
        resume = resume_ref[0]
        valid = valid_ref[0]
        early = pl.multiple_of(frame * rows, rows)
        late = pl.multiple_of((frame + lag) * rows, rows)
        here = pl.multiple_of(frame * pair, pair)
        lane = lane_index((pair, lanes))
        arriving = jnp.concatenate(
            [
                grad_in_ref[pl.ds(start, rows), units:] + grad_out_ref[pl.ds(start, rows), units:]
                for start in (early, late)
            ],
            axis=0,
        )
        context_total = grad_context[...] + arriving * valid
        grad_contexts[pl.ds(here, pair), :] = context_total
        weights = weights_ref[0]
        diagonals[pl.ds(here, pair), :] = spread(weights, rows, positions)
        windows[pl.ds(here, pair), :] = window_ref[0]
        window_grad = grad_window[...]
        wide = product(context_total, memory_upper[...], memory_lower[...], transposed=True)
        grad_weights = collect(wide, rows, positions) + jnp.where(
            lane < positions, window_grad + pltpu.roll(window_grad, lanes - positions, 1), 0.0
        )
        inner = jnp.sum(weights * grad_weights, axis=1, keepdims=True)
        grad_energy = weights * (grad_weights - inner)
        energy_v = energy_ref[...]
        energy_total = jnp.zeros((pair, lanes), f32)
        query_total = jnp.zeros((pair, lanes), f32)
        for place in range(positions):
            taken = slice(place * lanes, (place + 1) * lanes)
            bent = bent_ref[0, :, taken]
            column = jnp.sum(jnp.where(lane == place, grad_energy, 0.0), axis=1, keepdims=True)
            energy_total = energy_total + column * bent
            slope = column * energy_v * (1.0 - bent * bent)
            query_total = query_total + slope
            grad_bent[pl.ds(here, pair), taken] = slope
            grad_processed_out[:, taken] += slope[:rows] + slope[rows:]
        grad_energy_out[...] += energy_total
        add_frames(grad_query_out, query_total, frame, rows, lag)
        slopes = grad_bent[pl.ds(here, pair), :]
        moved = product(slopes, loc_upper[...], loc_lower[...], transposed=True)
        second = (lane >= positions) & (lane < 2 * positions)
        grad_window[...] = resume * (moved + jnp.where(second, window_grad, 0.0))

        arriving = jnp.concatenate(
            [grad_in_ref[pl.ds(early, rows), :units], grad_in_ref[pl.ds(late, rows), :units]], axis=0
        )
        total = grad_hidden[...] + arriving * valid
        total = total + product(query_total, query_upper[...], query_lower[...], transposed=True)
        cell_now = cell_ref[0] * jnp.where(frame > 0, resume, 0.0)
        zone_hidden, zone_cell = zone_masks(zone_early_ref, zone_late_ref)
        grad_sums, passed_hidden, passed_cell = gate_backward(
            gates_ref[0], cell_now, zone_hidden, zone_cell, total, grad_cell[...]
        )
        grad_cell[...] = passed_cell * resume
        for place, grads in enumerate(grad_sums):
            for part in range(units // width):
                block = place * (units // width) + part
                add_frames(frame_sums.at[block], grads[:, part * width : (part + 1) * width], frame, rows, lag)

        @pl.when(frame > 0)
        def recur():
            carried = jnp.zeros((pair, context_width + units), f32)
            for place, grads in enumerate(grad_sums):
                for part in range(units // width):
                    block = place * (units // width) + part
                    taken = grads[:, part * width : (part + 1) * width]
                    carried = carried + product(taken, upper[block], lower[block], transposed=True)
            grad_context[...] = carried[:, :context_width] * resume
            grad_hidden[...] = (carried[:, context_width:] + passed_hidden) * resume

    @pl.when(step == blocks + span - 1)
    def finish():
        prenet_grad = jnp.zeros(grad_prenet_out.shape, f32)
        frame_rows = frame_sums.shape[1]
        for block in range(blocks):
            grads = frame_sums[block]
            prenet_grad = prenet_grad + product(grads, first_upper[block], first_lower[block], transposed=True)
            grad_bias_out[:, block * width : (block + 1) * width] = jnp.sum(grads, axis=0, keepdims=True)
            later = jnp.concatenate([grads[rows:], jnp.zeros((rows, width), f32)], axis=0) * next_resume_ref[...]
            for place in range(shard_block):
                grad_sums_out[block * shard_block + place] = later[:, place * lanes : (place + 1) * lanes]
        grad_prenet_out[...] = prenet_grad
        context_upper, context_lower = split(grad_contexts[...])
        grad_memory_out[...] = product(diagonals[...].T, context_upper, context_lower)
        window_turned = windows[...].T
        for block in range(blocks):
            taken = slice(block * width, (block + 1) * width)
            bent_upper, bent_lower = split(grad_bent[:, taken])
            grad_loc_out[:, taken] = product(window_turned, bent_upper, bent_lower)


def split_kernel(values_ref, upper_ref, lower_ref):
    upper_ref[...], lower_ref[...] = split(values_ref[...])


def split_matrix(values):
    shape = jax.ShapeDtypeStruct(values.shape, bf16)
    return pl.pallas_call(
        split_kernel,
        out_shape=[shape, shape],
        compiler_params=pltpu.CompilerParams(vmem_limit_bytes=vmem_limit),
        name="split_matrix",
    )(values)


def join_kernel(count, *refs):
    out_ref, token_ref = refs[-2:]
    start = 0
    for ref in refs[:count]:
        out_ref[start : start + ref.shape[0]] = ref[...]
        start += ref.shape[0]
    token_ref[...] = jnp.zeros_like(token_ref)


def join_rows(arrays, awaited):
    total = sum(array.shape[0] for array in arrays)
    return pl.pallas_call(
        functools.partial(join_kernel, len(arrays)),
        in_specs=[pl.BlockSpec(memory_space=pltpu.VMEM)] * len(arrays)
        + [pl.BlockSpec(memory_space=pl.ANY)] * len(awaited),
        out_shape=[jax.ShapeDtypeStruct((total, lanes), f32), jax.ShapeDtypeStruct((8, lanes), f32)],
        compiler_params=pltpu.CompilerParams(vmem_limit_bytes=vmem_limit),
        name="join_rows",
    )(*arrays, *awaited)


def pack_sums(*sums):
    rows = []
    for row in sums:
        channels = row.shape[1]
        if channels % lanes:
            row = jnp.concatenate([row, jnp.zeros((1, -channels % lanes), f32)], axis=1)
        rows += [row[:, start : start + lanes] for start in range(0, row.shape[1], lanes)]
    if len(rows) < 8:
        rows.append(jnp.zeros((8 - len(rows), lanes), f32))
    return jnp.concatenate(rows, axis=0)


def unpack_sums(packed, channels, number=2):
    count = -(-channels // lanes)
    rows = []
    for row in range(number):
        pieces = [packed[row * count + place : row * count + place + 1] for place in range(count)]
        rows.append(jnp.concatenate(pieces, axis=1)[:, :channels])
    return rows


def moved_rows(values, shift):
    if shift > 0:
        return jnp.concatenate([jnp.zeros((shift, values.shape[1]), f32), values[:-shift]], axis=0)
    if shift < 0:
        return jnp.concatenate([values[-shift:], jnp.zeros((-shift, values.shape[1]), f32)], axis=0)
    return values


def convolve(values, same, upper_ref, lower_ref, rows):
    kernel = upper_ref.shape[0] // values.shape[1]
    channels = values.shape[1]
    total = None
    for tap in range(kernel):
        taken = slice(tap * channels, (tap + 1) * channels)
        moved = moved_rows(values, (kernel // 2 - tap) * rows) * same[:, tap : tap + 1]
        piece = product(moved, upper_ref[taken, :], lower_ref[taken, :])
        total = piece if total is None else total + piece
    return total


def send_sums(copies_ref, *values):
    packed = pack_sums(*[jnp.sum(value, axis=0, keepdims=True) for value in values])
    for place in range(copies_ref.shape[0]):
        copies_ref[place] = packed


def post_first_kernel(rows, values_ref, same_ref, upper_ref, lower_ref, conv_out, copies_out):
    conv = convolve(values_ref[...], same_ref[...], upper_ref, lower_ref, rows)
    conv_out[...] = conv
    send_sums(copies_out, conv, conv * conv)


def post_next_kernel(
    rows,
    frame_count,
    conv_ref,
    sums_ref,
    gain_ref,
    shift_ref,
    same_ref,
    upper_ref,
    lower_ref,
    *refs,
):
    *grad_refs, scaled_out, active_out, inverse_out, conv_out, copies_out = refs
    conv = conv_ref[...]
    first, second = unpack_sums(jnp.sum(sums_ref[...], axis=0), conv.shape[1])
    average = first / frame_count
    inverse = lax.rsqrt(second / frame_count - average * average + norm_eps)
    scaled = (conv - average) * inverse
    active = jnp.tanh(scaled * gain_ref[...] + shift_ref[...])
    scaled_out[...] = scaled
    active_out[...] = active
    inverse_out[...] = inverse
    conv = convolve(active, same_ref[...], upper_ref, lower_ref, rows)
    conv_out[...] = conv
    grads = [piece for ref in grad_refs for piece in (ref[...], ref[...] * conv)]
    send_sums(copies_out, conv, conv * conv, *grads)


def conv_back(grad_conv, same, upper_ref, lower_ref, channels, rows):
    kernel = upper_ref.shape[0] // channels
    total = None
    for tap in range(kernel):
        taken = slice(tap * channels, (tap + 1) * channels)
        piece = product(grad_conv, upper_ref[taken, :], lower_ref[taken, :], transposed=True)
        piece = moved_rows(piece * same[:, tap : tap + 1], (tap - kernel // 2) * rows)
        total = piece if total is None else total + piece
    return total


def post_turn_kernel(
    rows,
    frame_count,
    grad_ref,
    conv_ref,
    sums_ref,
    before_ref,
    gain_ref,
    shift_ref,
    same_ref,
    upper_ref,
    lower_ref,
    active_ref,
    scaled_below_ref,
    after_out,
    conv_out,
    sums_out,
    grad_out,
    copies_out,
):
    conv = conv_ref[...]
    grad = grad_ref[...]
    gain = gain_ref[...]
    first, second, shift_grad, mixed = unpack_sums(jnp.sum(sums_ref[...], axis=0), conv.shape[1], 4)
    average = first / frame_count
    inverse = lax.rsqrt(second / frame_count - average * average + norm_eps)
    scaled = (conv - average) * inverse
    after_out[...] = before_ref[...] + scaled * gain + shift_ref[...]
    gain_grad = inverse * (mixed - average * shift_grad)
    sums_out[...] = pack_sums(shift_grad, gain_grad)
    grad_conv = inverse * gain * (grad - (shift_grad + scaled * gain_grad) / frame_count)
    conv_out[...] = jnp.concatenate([grad_conv, jnp.zeros((conv.shape[0], -conv.shape[1] % lanes), f32)], axis=1)
    active = active_ref[...]
    total = conv_back(grad_conv, same_ref[...], upper_ref, lower_ref, active.shape[1], rows)
    total = total * (1.0 - active * active)
    send_sums(copies_out, total, total * scaled_below_ref[...])
    grad_out[...] = total


def post_back_kernel(
    rows,
    frame_count,
    has_lower,
    awaited,
    grad_ref,
    scaled_ref,
    sums_ref,
    inverse_ref,
    gain_ref,
    same_ref,
    upper_ref,
    lower_ref,
    *refs,
):
    if has_lower:
        active_ref, scaled_below_ref = refs[:2]
        conv_out, sums_out, grad_out, copies_out = refs[2 + awaited :]
    else:
        conv_out, sums_out, grad_out = refs[awaited:]
    grad = grad_ref[...]
    scaled = scaled_ref[...]
    same = same_ref[...]
    packed = jnp.sum(sums_ref[...], axis=0)
    sums_out[...] = packed
    shift_grad, gain_grad = unpack_sums(packed, grad.shape[1])
    grad_conv = inverse_ref[...] * gain_ref[...] * (grad - (shift_grad + scaled * gain_grad) / frame_count)
    conv_out[...] = grad_conv
    total = conv_back(grad_conv, same, upper_ref, lower_ref, grad_out.shape[1], rows)
    if has_lower:
        active = active_ref[...]
        total = total * (1.0 - active * active)
        send_sums(copies_out, total, total * scaled_below_ref[...])
    grad_out[...] = total


def post_call(kernel, outs, name, operands, awaited=()):
    shapes = [jax.ShapeDtypeStruct(shape, f32) for shape in outs]
    in_specs = [pl.BlockSpec(memory_space=pltpu.VMEM)] * len(operands)
    in_specs += [pl.BlockSpec(memory_space=pl.ANY)] * len(awaited)
    return pl.pallas_call(
        kernel,
        in_specs=in_specs,
        out_specs=[pl.BlockSpec(memory_space=pltpu.VMEM)] * len(outs),
        out_shape=shapes,
        compiler_params=pltpu.CompilerParams(vmem_limit_bytes=vmem_limit),
        name=name,
    )(*operands, *awaited)


def share_sums(copies):
    return lax.all_to_all(copies, both, 0, 0)


def tap_gradient_kernel(rows, kernel, split_inputs, own_ref, *refs):
    count = (len(refs) - 1) // 3
    input_refs, grad_refs, same_refs = refs[:count], refs[count : 2 * count], refs[2 * count : 3 * count]
    out_ref = refs[-1]
    margin = kernel // 2
    place = pl.ds(pl.multiple_of(own_ref[0] * lanes, lanes), lanes)
    if split_inputs:
        inputs = [ref[:, place] for ref in input_refs]
        grads = [ref[...] for ref in grad_refs]
    else:
        inputs = [ref[...] for ref in input_refs]
        grads = [ref[:, place] for ref in grad_refs]
    moved = []
    for tap in range(kernel):
        pieces = [
            moved_rows(grad * same[:, tap : tap + 1], (tap - margin) * rows) for grad, same in zip(grads, same_refs)
        ]
        moved.append(jnp.concatenate(pieces, axis=0))
    upper, lower = split(jnp.concatenate(moved, axis=1))
    result = product(jnp.concatenate(inputs, axis=0).T, upper, lower)
    depth = out_ref.shape[1]
    for tap in range(kernel):
        block = result[:, tap * lanes : (tap + 1) * lanes]
        out_ref[tap] = block.T[:depth] if split_inputs else block[:depth]


def tap_gradient(inputs, grads, same, kernel, rows, depth, split_inputs=False):
    own = lax.axis_index("section").astype(jnp.int32).reshape(1)
    return pl.pallas_call(
        functools.partial(tap_gradient_kernel, rows, kernel, split_inputs),
        in_specs=[pl.BlockSpec(memory_space=pltpu.SMEM)]
        + [pl.BlockSpec(memory_space=pltpu.VMEM)] * (len(inputs) + len(grads) + len(same)),
        out_shape=jax.ShapeDtypeStruct((kernel, depth, lanes), f32),
        compiler_params=pltpu.CompilerParams(vmem_limit_bytes=vmem_limit),
        name="tap_gradient",
    )(own, *inputs, *grads, *same)


def frame_product_kernel(pieces, own_ref, *refs):
    inputs = refs[:-4]
    grads_ref, kept_ref, sent_ref, total = refs[-4:]
    step = pl.program_id(0)

    @pl.when(step == 0)
    def prepare():
        total[...] = jnp.zeros_like(total)

    blocks, groups = grads_ref.shape[:2]
    grads = jnp.concatenate(
        [jnp.concatenate([grads_ref[block, group] for group in range(groups)], axis=1) for block in range(blocks)],
        axis=0,
    )
    columns = grads.shape[1]
    turned_upper, turned_lower = split(grads.T)
    stacked = jnp.concatenate([turned_upper, turned_lower], axis=0)
    start = 0
    for which, first, last in pieces:
        upper, lower = split(inputs[which][:, first:last])
        one = jnp.dot(stacked, upper, preferred_element_type=f32)
        two = jnp.dot(turned_upper, lower, preferred_element_type=f32)
        total[:, start : start + last - first] += one[:columns] + one[columns:] + two
        start += last - first

    @pl.when(step == pl.num_programs(0) - 1)
    def finish():
        width = kept_ref.shape[2]
        core, place = own_ref[0] % 2, own_ref[0] // 2
        for part in range(4):
            turned = total[part * width : (part + 1) * width].T
            across = (place + part // 2) % 2

            @pl.when(core == part % 2)
            def keep():
                kept_ref[across] = turned

            @pl.when(core != part % 2)
            def send():
                sent_ref[across] = turned


def frame_product(inputs, grads, pieces):
    sources, groups, frames = grads.shape[:3]
    parts = lax.axis_size("section")
    block = 4 if sources % 4 == 0 else 1
    columns = groups // parts * lanes
    depth = sum(last - first for _, first, last in pieces)

    def block_spec(array):
        return pl.BlockSpec((block * frames, array.shape[1]), lambda step: (step, 0))

    return pl.pallas_call(
        functools.partial(frame_product_kernel, pieces),
        grid=(sources // block,),
        in_specs=[pl.BlockSpec(memory_space=pltpu.SMEM)]
        + [block_spec(array) for array in inputs]
        + [pl.BlockSpec((block, groups, frames, lanes), lambda step: (step, 0, 0, 0))],
        out_specs=[pl.BlockSpec((2, depth, columns), lambda step: (0, 0, 0))] * 2,
        out_shape=[jax.ShapeDtypeStruct((2, depth, columns), f32)] * 2,
        scratch_shapes=[pltpu.VMEM((parts * columns, depth), f32)],
        compiler_params=params(),
        name="frame_product",
    )(lax.axis_index("section").astype(jnp.int32).reshape(1), *inputs, grads)


def whole_spec(array):
    rank = len(array.shape)
    return pl.BlockSpec(array.shape, lambda step: (0,) * rank)


def timed_spec(array, place, depth=None):
    shape = (1,) + tuple(array.shape[1:])
    rank = len(array.shape)
    return pl.BlockSpec(shape, lambda step: (place(step),) + (0,) * (rank - 1))


def shard_spec(array, place):
    shape = (shard_block,) + tuple(array.shape[1:])
    return pl.BlockSpec(shape, lambda step: (place(step), 0, 0))


def zone_spec(zone, place, which):
    shape = (1, 2) + tuple(zone.shape[2:])
    return pl.BlockSpec(shape, lambda step: (place(step), which, 0, 0))


def out_spec(shape):
    rank = len(shape)
    return pl.BlockSpec(shape, lambda step: (0,) * rank)


def cost(weights, passes):
    return pl.CostEstimate(flops=2 * 256 * weights * 2 * passes, bytes_accessed=4 * weights, transcendentals=0)


def params():
    return pltpu.CompilerParams(vmem_limit_bytes=vmem_limit, dimension_semantics=("arbitrary",))


def attention_forward(
    weight, prenet_out, bias, loc_map, processed, memory, query_weight, energy_v, zone, resume, allowed, lag, awaited
):
    groups, depth = weight.shape[:2]
    blocks = groups // shard_block
    rows = memory.shape[0] // (processed.shape[1] // lanes)
    positions = processed.shape[1] // lanes
    columns = groups * lanes
    units = columns // 4
    context_width = memory.shape[1]
    frame_rows = prenet_out.shape[0]
    rest = depth - prenet_out.shape[1]
    width = shard_block * lanes
    pair = 2 * rows

    def shard(step):
        return jnp.minimum(step, blocks - 1)

    def timed(step):
        return jnp.clip(step - blocks, 0, span - 1)

    def later(step):
        return timed(step) + lag

    timed_shapes = [
        (span, pair, units),
        (span, pair, units),
        (span, pair, context_width),
        (span, pair, columns),
        (span, pair, positions * lanes),
        (span, pair, lanes),
        (span, pair, lanes),
    ]
    out_shape = [jax.ShapeDtypeStruct(shape, f32) for shape in timed_shapes]
    bias_blocks = bias.reshape(blocks, 1, width)
    return pl.pallas_call(
        functools.partial(attention_forward_kernel, blocks, rows, positions, lag),
        grid=(blocks + span,),
        in_specs=[
            shard_spec(weight, shard),
            whole_spec(prenet_out),
            timed_spec(bias_blocks, shard),
            whole_spec(loc_map),
            whole_spec(processed),
            whole_spec(memory),
            whole_spec(query_weight),
            whole_spec(energy_v),
            zone_spec(zone, timed, 0),
            zone_spec(zone, later, 0),
            timed_spec(resume, timed),
            whole_spec(allowed),
            pl.BlockSpec(memory_space=pl.ANY),
        ],
        out_specs=[timed_spec(shape, timed) for shape in out_shape],
        out_shape=out_shape,
        scratch_shapes=[
            pltpu.VMEM((blocks, rest, width), bf16),
            pltpu.VMEM((blocks, rest, width), bf16),
            pltpu.VMEM((blocks, frame_rows, width), f32),
            pltpu.VMEM(loc_map.shape, bf16),
            pltpu.VMEM(loc_map.shape, bf16),
            pltpu.VMEM(memory.shape, bf16),
            pltpu.VMEM(memory.shape, bf16),
            pltpu.VMEM(query_weight.shape, bf16),
            pltpu.VMEM(query_weight.shape, bf16),
            pltpu.VMEM((pair, columns), f32),
            pltpu.VMEM((pair, units), f32),
            pltpu.VMEM((pair, units), f32),
            pltpu.VMEM((pair, context_width), f32),
            pltpu.VMEM((pair, lanes), f32),
        ],
        compiler_params=params(),
        cost_estimate=cost(depth * columns, span),
        name="attention_forward",
    )(
        weight,
        prenet_out,
        bias_blocks,
        loc_map,
        processed,
        memory,
        query_weight,
        energy_v,
        zone,
        zone,
        resume,
        allowed,
        awaited,
    )


def decoder_forward(weight, frames, bias, zone, resume, rows, lag, awaited):
    groups = weight.shape[0]
    blocks = groups // shard_block
    columns = groups * lanes
    units = columns // 4
    width = shard_block * lanes
    pair = 2 * rows

    def shard(step):
        return jnp.minimum(step, blocks - 1)

    def timed(step):
        return jnp.clip(step - blocks, 0, span - 1)

    def later(step):
        return timed(step) + lag

    timed_shapes = [(span, pair, units), (span, pair, units), (span, pair, columns)]
    out_shape = [jax.ShapeDtypeStruct(shape, f32) for shape in timed_shapes]
    bias_blocks = bias.reshape(blocks, 1, width)
    return pl.pallas_call(
        functools.partial(decoder_forward_kernel, blocks, rows, lag, len(awaited)),
        grid=(blocks + span,),
        in_specs=[
            shard_spec(weight, shard),
            whole_spec(frames),
            timed_spec(bias_blocks, shard),
            zone_spec(zone, timed, 1),
            zone_spec(zone, later, 1),
            timed_spec(resume, timed),
        ]
        + [pl.BlockSpec(memory_space=pl.ANY)] * len(awaited),
        out_specs=[timed_spec(shape, timed) for shape in out_shape],
        out_shape=out_shape,
        scratch_shapes=[
            pltpu.VMEM((blocks, units, width), bf16),
            pltpu.VMEM((blocks, units, width), bf16),
            pltpu.VMEM((blocks, frames.shape[0], width), f32),
            pltpu.VMEM((pair, columns), f32),
            pltpu.VMEM((pair, units), f32),
            pltpu.VMEM((pair, units), f32),
        ],
        compiler_params=params(),
        cost_estimate=cost(weight.shape[1] * columns, span // 2),
        name="decoder_forward",
    )(weight, frames, bias_blocks, zone, zone, resume, *awaited)


def decoder_backward(weight, grad, gates, cells, zone, resume, valid, rows, lag, awaited):
    groups, depth = weight.shape[:2]
    blocks = groups // shard_block
    columns = groups * lanes
    units = columns // 4
    split_row = depth - units
    width = shard_block * lanes
    pair = 2 * rows
    frame_rows = grad.shape[0]
    part = math.gcd(units, split_row)
    own_parts = units // part
    in_parts = split_row // part

    def part_spec(index):
        return pl.BlockSpec((shard_block, part, lanes), index)

    def own_spec(which):
        return part_spec(lambda step: (shard(step), in_parts + which, 0))

    def in_spec(which):
        return part_spec(lambda step: (last_shard(step), which, 0))

    def shard(step):
        return jnp.minimum(step, blocks - 1)

    def last_shard(step):
        return jnp.clip(step - blocks - span, 0, blocks - 1)

    def timed(step):
        return span - 1 - jnp.clip(step - blocks, 0, span - 1)

    def later(step):
        return timed(step) + lag

    def before(step):
        return jnp.maximum(timed(step) - 1, 0)

    out_shape = [
        jax.ShapeDtypeStruct((groups, frame_rows, lanes), f32),
        jax.ShapeDtypeStruct((frame_rows, split_row), f32),
    ]
    return pl.pallas_call(
        functools.partial(decoder_backward_kernel, blocks, rows, lag, own_parts, in_parts, len(awaited)),
        grid=(2 * blocks + span,),
        in_specs=[own_spec(which) for which in range(own_parts)]
        + [in_spec(which) for which in range(in_parts)]
        + [
            whole_spec(grad),
            timed_spec(gates, timed),
            timed_spec(cells, before),
            zone_spec(zone, timed, 1),
            zone_spec(zone, later, 1),
            timed_spec(resume, timed),
            timed_spec(valid, timed),
        ]
        + [pl.BlockSpec(memory_space=pl.ANY)] * len(awaited),
        out_specs=[shard_spec(out_shape[0], last_shard), whole_spec(out_shape[1])],
        out_shape=out_shape,
        scratch_shapes=[
            pltpu.VMEM((blocks, units, width), bf16),
            pltpu.VMEM((blocks, units, width), bf16),
            pltpu.VMEM((blocks, frame_rows, width), f32),
            pltpu.VMEM((pair, units), f32),
            pltpu.VMEM((pair, units), f32),
        ],
        compiler_params=params(),
        cost_estimate=cost(depth * columns, 4 * span),
        name="decoder_backward",
    )(*[weight] * (own_parts + in_parts), grad, gates, cells, zone, zone, resume, valid, *awaited)


def attention_backward(
    weight,
    grad_in,
    grad_out,
    gates,
    cells,
    bent,
    weights,
    window,
    loc_map,
    memory,
    query_weight,
    energy_v,
    zone,
    resume,
    valid,
    next_resume,
    rows,
    positions,
    prenet_width,
    lag,
    awaited,
):
    groups, depth = weight.shape[:2]
    blocks = groups // shard_block
    columns = groups * lanes
    units = columns // 4
    width = shard_block * lanes
    pair = 2 * rows
    frame_rows = grad_in.shape[0]
    context_width = memory.shape[1]
    rest = depth - prenet_width

    def shard(step):
        return jnp.minimum(step, blocks - 1)

    def timed(step):
        return span - 1 - jnp.clip(step - blocks, 0, span - 1)

    def later(step):
        return timed(step) + lag

    def before(step):
        return jnp.maximum(timed(step) - 1, 0)

    shapes = [
        (groups, frame_rows, lanes),
        (1, columns),
        (frame_rows, prenet_width),
        (frame_rows, lanes),
        (rows, positions * lanes),
        (rows * positions, context_width),
        loc_map.shape,
        (pair, lanes),
    ]
    return pl.pallas_call(
        functools.partial(attention_backward_kernel, blocks, rows, positions, lag),
        grid=(blocks + span,),
        in_specs=[
            shard_spec(weight, shard),
            whole_spec(grad_in),
            whole_spec(grad_out),
            timed_spec(gates, timed),
            timed_spec(cells, before),
            timed_spec(bent, timed),
            timed_spec(weights, timed),
            timed_spec(window, timed),
            whole_spec(loc_map),
            whole_spec(memory),
            whole_spec(query_weight),
            whole_spec(energy_v),
            zone_spec(zone, timed, 0),
            zone_spec(zone, later, 0),
            timed_spec(resume, timed),
            timed_spec(valid, timed),
            whole_spec(next_resume),
        ]
        + [pl.BlockSpec(memory_space=pl.ANY)] * len(awaited),
        out_specs=[out_spec(shape) for shape in shapes],
        out_shape=[jax.ShapeDtypeStruct(shape, f32) for shape in shapes],
        scratch_shapes=[
            pltpu.VMEM((blocks, rest, width), bf16),
            pltpu.VMEM((blocks, rest, width), bf16),
            pltpu.VMEM((blocks, prenet_width, width), bf16),
            pltpu.VMEM((blocks, prenet_width, width), bf16),
            pltpu.VMEM((blocks, frame_rows, width), f32),
            pltpu.VMEM(loc_map.shape, bf16),
            pltpu.VMEM(loc_map.shape, bf16),
            pltpu.VMEM(memory.shape, bf16),
            pltpu.VMEM(memory.shape, bf16),
            pltpu.VMEM(query_weight.shape, bf16),
            pltpu.VMEM(query_weight.shape, bf16),
            pltpu.VMEM((span * pair, positions * lanes), f32),
            pltpu.VMEM((span * pair, context_width), f32),
            pltpu.VMEM((span * pair, rows * positions), f32),
            pltpu.VMEM((span * pair, lanes), f32),
            pltpu.VMEM((pair, units), f32),
            pltpu.VMEM((pair, units), f32),
            pltpu.VMEM((pair, context_width), f32),
            pltpu.VMEM((pair, lanes), f32),
        ],
        compiler_params=params(),
        cost_estimate=cost(lanes * lanes, 1),
        name="attention_backward",
    )(
        weight,
        grad_in,
        grad_out,
        gates,
        cells,
        bent,
        weights,
        window,
        loc_map,
        memory,
        query_weight,
        energy_v,
        zone,
        zone,
        resume,
        valid,
        next_resume,
        *awaited,
    )


def dot(left, right, left_dim=1, right_dim=0):
    return lax.dot_general(
        left, right, (((left_dim,), (right_dim,)), ((), ())), precision=high, preferred_element_type=f32
    )


def gather_columns(shard):
    depth, width = shard.shape
    if width % lanes:
        full = lax.all_gather(shard, both, axis=1, tiled=True)
        return full.reshape(depth, -1, lanes).swapaxes(0, 1)
    stacked = lax.all_gather(shard, both, axis=0)
    if width == lanes:
        return stacked
    return stacked.reshape(-1, depth, width // lanes, lanes).swapaxes(1, 2).reshape(-1, depth, lanes)


def along_core(values):
    return lax.ppermute(values, "section", [(place, place ^ 1) for place in range(4)])


def along_y(values):
    return lax.ppermute(values, "section", [(place, place ^ 2) for place in range(4)])


def gather_y(values):
    return jnp.stack([values, along_y(values)])


def gather_core(two):
    return jnp.concatenate([two, along_core(two)], axis=0)


def list_section(values):
    other = along_y(values)
    return [values, other, along_core(values), along_core(other)]


def gather_section(values):
    return gather_core(gather_y(values))


def section_order(four, own):
    entries = []
    for place in range(4):
        offset = own ^ place
        held = (offset % 2) * 2 + offset // 2
        entries.append(lax.dynamic_index_in_dim(four, held, 0, keepdims=False))
    return entries


def section_columns(pair, layers):
    own = lax.axis_index("section")
    four = gather_core(pair)
    depth = four.shape[1] // layers
    whole = []
    for layer in range(layers):
        blocks = section_order(four[:, layer * depth : (layer + 1) * depth], own)
        whole.append(jnp.concatenate(blocks, axis=1))
    return whole


def own_columns(values, columns):
    own = lax.axis_index("section")
    total = values[..., :columns]
    for place in range(1, values.shape[-1] // columns):
        total = jnp.where(own == place, values[..., place * columns : (place + 1) * columns], total)
    return total


def flat_join(arrays, devices):
    pieces = []
    for array in arrays:
        flat = array.reshape(-1)
        flat = jnp.pad(flat, (0, -flat.shape[0] % lanes))
        pieces.append(flat.reshape(-1, lanes))
    joined = jnp.concatenate(pieces, axis=0)
    joined = jnp.pad(joined, ((0, -joined.shape[0] % (8 * devices)), (0, 0)))
    return joined.reshape(devices, -1, lanes)


def part_sum(joined):
    return jnp.sum(lax.all_to_all(joined, both, 0, 0), axis=0)


def flat_whole(part, devices):
    return lax.all_to_all(jnp.broadcast_to(part[None], (devices,) + part.shape), both, 0, 0)


def flat_split(whole, arrays):
    whole = whole.reshape(-1, lanes)
    sums = []
    start = 0
    for array in arrays:
        count = -(-array.size // lanes)
        flat = whole[start : start + count].reshape(-1)
        sums.append(flat[: array.size].reshape(array.shape))
        start += count
    return sums


def exchange_ring(grads, extra=None):
    groups, frames, width = grads.shape
    size = lax.axis_size("dp")
    if extra is None:
        return lax.all_to_all(grads.reshape(size, groups // size, frames, width), "dp", 0, 0)
    joined = jnp.concatenate([grads.reshape(size, -1, width), extra], axis=1)
    received = lax.all_to_all(joined, "dp", 0, 0)
    count = groups // size * frames
    return received[:, :count].reshape(size, -1, frames, width), jnp.sum(received[:, count:], axis=0)


def sum_section(parts):
    own = lax.axis_index("section")
    core, place = own % 2, own // 2
    pairs = parts.reshape((2, 2) + parts.shape[1:])
    mine = jnp.where(core == 0, pairs[:, 0], pairs[:, 1])
    other = jnp.where(core == 0, pairs[:, 1], pairs[:, 0])
    pair = mine + along_core(other)
    mine = jnp.where(place == 0, pair[0], pair[1])
    other = jnp.where(place == 0, pair[1], pair[0])
    return mine + along_y(other)


def gathers_inputs(frame_rows, columns, devices):
    return frame_rows * devices <= columns


def column_gradients(inputs, pieces, received, grads):
    if received is not None:
        kept, sent = frame_product(inputs, received, pieces)
        pair = kept + along_core(sent)
        return pair[0] + along_y(pair[1])
    groups, frames, width = grads.shape
    flat = grads.swapaxes(0, 1).reshape(frames, groups * width)
    parts = [
        lax.psum_scatter(dot(inputs[which][:, first:last], flat, 0, 0), both, scatter_dimension=1, tiled=True)
        for which, first, last in pieces
    ]
    return jnp.concatenate(parts, axis=0)


def gelu_slope(values):
    return jax.vjp(jax.nn.gelu, values)


def location_map(loc_filters, loc_dense, positions):
    filters, channels, taps = loc_filters.shape
    features = loc_dense.shape[1]
    joined = dot(loc_filters.reshape(filters, channels * taps), loc_dense, 0, 0)
    joined = joined.reshape(channels, taps, features)
    margin = taps // 2
    padded = jnp.pad(joined, ((0, 0), (positions, positions), (0, 0)))
    columns = [
        padded[:, positions + margin - place : 2 * positions + margin - place] for place in range(positions)
    ]
    spread_map = jnp.stack(columns, axis=2).reshape(channels * positions, positions * features)
    return jnp.pad(spread_map, ((0, lanes - channels * positions), (0, 0)))


def location_unmap(grad_map, channels, taps, positions, features):
    grads = grad_map[: channels * positions].reshape(channels, positions, positions, features)
    turned = jnp.flip(grads.swapaxes(1, 2), axis=1)
    padded = jnp.pad(turned, ((0, 0), (0, 0), (0, positions), (0, 0))).reshape(channels, -1, features)
    length = 2 * positions - 1
    skewed = padded[:, : positions * length].reshape(channels, positions, length, features)
    start = positions - 1 - taps // 2
    return jnp.sum(skewed[:, :, start : start + taps], axis=1)


def per_device(
    memory,
    enc_lengths,
    frame_segment,
    mel_target,
    prenet_keep,
    zone_keep,
    pre_first,
    pre_second,
    att_weight,
    att_bias,
    query_weight,
    memory_weight,
    loc_filters,
    loc_dense,
    energy_v,
    dec_weight,
    dec_bias,
    proj_weight,
    proj_bias,
    stop_weight,
    post_first,
    post_mid,
    post_last,
    norm_gain,
    norm_shift,
    last_gain,
    last_shift,
    grad_after,
    grad_stop,
):
    devices = lax.axis_size("dp") * lax.axis_size("section")
    rows, positions, context_width = memory.shape
    frames = frame_segment.shape[1]
    mel = mel_target.shape[2]
    units = att_bias.shape[0] // 4
    prenet_width = pre_first.shape[1]
    features = memory_weight.shape[1]
    lag = frames - span
    frame_rows = frames * rows

    att_all = gather_columns(att_weight)
    dec_all = gather_columns(dec_weight)
    mid_pair = gather_y(post_mid.reshape(-1, post_mid.shape[3]))
    mid_all = section_columns(mid_pair, 3)
    post_split = [split_matrix(weight.reshape(-1, weight.shape[-1])) for weight in [post_first] + mid_all + [post_last]]

    segment = frame_segment.T
    earlier = jnp.concatenate([segment[:1] - 1, segment[:-1]], axis=0)
    resume = (segment == earlier).astype(f32)
    shifted = jnp.concatenate([jnp.zeros_like(mel_target[:, :1]), mel_target[:, :-1]], axis=1)
    frames_in = (shifted.swapaxes(0, 1) * resume[:, :, None]).reshape(frame_rows, mel)
    keep = prenet_keep.transpose(1, 2, 0, 3).astype(f32) * 2.0
    keep_first = keep[:, 0].reshape(frame_rows, prenet_width)
    keep_second = keep[:, 1].reshape(frame_rows, prenet_width)
    gelu_first, first_back = gelu_slope(dot(frames_in, pre_first))
    pre_hidden = gelu_first * keep_first
    gelu_second, second_back = gelu_slope(dot(pre_hidden, pre_second))
    prenet_out = gelu_second * keep_second
    memory_flat = memory.reshape(rows * positions, context_width)
    processed = dot(memory_flat, memory_weight)
    loc_map = location_map(loc_filters, loc_dense, positions)
    zone = zone_keep.transpose(1, 2, 0, 3)

    first_part = segment == 0
    steps = jnp.arange(span)
    never = jnp.ones((span, rows), f32)
    resume_pair = jnp.concatenate([never, resume[lag:]], axis=1)[:, :, None]
    valid_pair = jnp.concatenate([first_part[:span], ~first_part[lag:]], axis=1).astype(f32)[:, :, None]
    encoder_first = jnp.arange(lanes)[None, :] < enc_lengths[:, :1]
    inside = jnp.arange(lanes)[None, :] < positions
    allowed = jnp.concatenate([encoder_first, inside & ~encoder_first], axis=0).astype(f32)
    next_resume = jnp.concatenate([resume[1:], jnp.zeros((1, rows), f32)], axis=0).reshape(frame_rows, 1)

    def to_frames(pairs):
        early = jnp.pad(pairs[:, :rows], ((0, lag), (0, 0), (0, 0)))
        late = jnp.pad(pairs[:, rows:], ((lag, 0), (0, 0), (0, 0)))
        return jnp.where(first_part[:, :, None], early, late).reshape(frame_rows, -1)

    energy_row = energy_v.reshape(1, features)
    processed_wide = processed.reshape(rows, positions * features)
    hidden, cells, contexts, gates, bent, weights, window = attention_forward(
        att_all,
        prenet_out,
        att_bias,
        loc_map,
        processed_wide,
        memory_flat,
        query_weight,
        energy_row,
        zone,
        resume_pair,
        allowed,
        lag,
        mid_pair,
    )
    att_frames = to_frames(hidden)
    context_frames = to_frames(contexts)
    dec_inputs = jnp.concatenate([att_frames, context_frames], axis=1)
    dec_hidden, dec_cells, dec_gates = decoder_forward(
        dec_all, dec_inputs, dec_bias, zone, resume_pair, rows, lag, [part for pair in post_split for part in pair]
    )
    dec_frames = to_frames(dec_hidden)

    prenet_later = jnp.concatenate([prenet_out[rows:], jnp.zeros((rows, prenet_width), f32)], axis=0)
    att_inputs_all = jnp.concatenate([prenet_later, context_frames, att_frames], axis=1)
    dec_earlier = jnp.concatenate([jnp.zeros((rows, units), f32), dec_frames[:-rows]], axis=0)
    dec_earlier = dec_earlier * resume.reshape(frame_rows, 1)
    dec_inputs_all = dec_earlier
    input_width = att_inputs_all.shape[1]
    input_pieces = []
    rings = gathers_inputs(frame_rows, 4 * units, devices)
    if rings:
        att_inputs_all = lax.all_gather(att_inputs_all, "dp", axis=0, tiled=True)
        dec_inputs_all = lax.all_gather(dec_inputs_all, "dp", axis=0, tiled=True)
        input_pieces = [att_inputs_all, dec_inputs_all]

    out_frames = jnp.concatenate([dec_frames, context_frames], axis=1)
    mel_before = dot(out_frames, proj_weight) + proj_bias
    stop_logit = jnp.sum(out_frames * stop_weight, axis=1).reshape(frames, rows).T

    section_size = lax.axis_size("section")
    kernel = post_first.shape[0]
    margin = kernel // 2
    padded = jnp.pad(segment, ((margin, margin), (0, 0)), constant_values=-1)
    same_segment = jnp.stack(
        [padded[offset : offset + frames] == segment for offset in range(kernel)], axis=2
    ).astype(f32)
    same = jnp.pad(same_segment, ((0, 0), (0, 0), (0, 8 - kernel))).reshape(frame_rows, 8)
    same_all = list_section(same)
    frame_count = frame_rows * devices
    gains = [norm_gain[layer : layer + 1] for layer in range(4)] + [last_gain.reshape(1, mel)]
    shifts = [norm_shift[layer : layer + 1] for layer in range(4)] + [last_shift.reshape(1, mel)]
    widths = [post_first.shape[2]] * 4 + [mel]
    grad_after_frames = grad_after.swapaxes(0, 1).reshape(frame_rows, mel)
    conv, copies = post_call(
        functools.partial(post_first_kernel, rows),
        [(frame_rows, widths[0]), (devices, 8, lanes)],
        "post_first",
        (mel_before, same, *post_split[0]),
    )
    scaled, inverse, active, inputs_all = [], [], [], []
    inputs_all.append(list_section(jnp.pad(mel_before, ((0, 0), (0, lanes - mel)))))
    for layer in range(4):
        scaled_now, active_now, inverse_now, conv, copies = post_call(
            functools.partial(post_next_kernel, rows, frame_count),
            [
                (frame_rows, widths[layer]),
                (frame_rows, widths[layer]),
                (1, widths[layer]),
                (frame_rows, widths[layer + 1]),
                (devices, 8, lanes),
            ],
            "post_next",
            (conv, share_sums(copies), gains[layer], shifts[layer], same, *post_split[layer + 1])
            + ((grad_after_frames,) if layer == 3 else ()),
        )
        scaled.append(scaled_now)
        active.append(active_now)
        inverse.append(inverse_now)
        inputs_all.append(list_section(active_now))
    mel_after, grad_conv, packed, upstream, copies = post_call(
        functools.partial(post_turn_kernel, rows, frame_count),
        [(frame_rows, mel), (frame_rows, lanes), (8, lanes), (frame_rows, widths[3]), (devices, 8, lanes)],
        "post_turn",
        (
            grad_after_frames,
            conv,
            share_sums(copies),
            mel_before,
            gains[4],
            shifts[4],
            same,
            *post_split[4],
            active[3],
            scaled[3],
        ),
    )
    weight_grads = [None] * 5
    gain_grads = [None] * 5
    shift_grads = [None] * 5
    shift_grads[4], gain_grads[4] = [row.reshape(-1) for row in unpack_sums(packed, mel)]
    weight_grads[4] = tap_gradient(
        inputs_all[4], list_section(grad_conv), same_all, kernel, rows, mel, split_inputs=True
    )
    for layer in reversed(range(4)):
        below = (active[layer - 1], scaled[layer - 1]) if layer else ()
        awaited = (weight_grads[layer + 2],) if layer < 3 else ()
        outs = [(frame_rows, widths[layer]), (8, lanes), (frame_rows, widths[layer - 1] if layer else mel)]
        if layer:
            outs.append((devices, 8, lanes))
        results = post_call(
            functools.partial(post_back_kernel, rows, frame_count, layer > 0, len(awaited)),
            outs,
            "post_back",
            (
                upstream,
                scaled[layer],
                share_sums(copies),
                inverse[layer],
                gains[layer],
                same,
                *post_split[layer],
                *below,
            ),
            awaited,
        )
        grad_conv, packed, upstream = results[:3]
        if layer:
            copies = results[3]
        shift_grads[layer], gain_grads[layer] = [row.reshape(-1) for row in unpack_sums(packed, widths[layer])]
        depth = widths[layer - 1] if layer else mel
        weight_grads[layer] = tap_gradient(inputs_all[layer], list_section(grad_conv), same_all, kernel, rows, depth)

    grad_mel = grad_after_frames + upstream
    grad_stop_frames = grad_stop.T.reshape(frame_rows, 1)
    grad_out = dot(grad_mel, proj_weight, 1, 1) + grad_stop_frames * stop_weight
    mel_grads = jnp.pad(
        jnp.concatenate([grad_mel, grad_stop_frames], axis=1), ((0, 0), (0, lanes - mel - 1))
    )
    mel_grads_all = jnp.concatenate(list_section(mel_grads), axis=0)
    outs_own = jnp.concatenate(
        [own_columns(outs, out_frames.shape[1] // section_size) for outs in list_section(out_frames)], axis=0
    )
    g_proj_part = dot(outs_own, mel_grads_all, 0, 0)
    group_grads, group_token = join_rows(
        [grad.reshape(-1, lanes) for grad in weight_grads + [g_proj_part]]
        + [jnp.pad(jnp.sum(mel_grads_all, axis=0, keepdims=True), ((0, 7), (0, 0)))],
        input_pieces,
    )
    group_sums = lax.psum(group_grads, "dp")
    dec_sums, grad_dec_inputs = decoder_backward(
        dec_all,
        grad_out,
        dec_gates,
        dec_cells,
        zone,
        resume_pair,
        valid_pair,
        rows,
        lag,
        [group_token],
    )
    g_dec_bias = jnp.sum(dec_sums, axis=1).reshape(-1)
    dec_columns = exchange_ring(dec_sums) if rings else None
    (
        att_sums,
        g_att_bias,
        grad_prenet,
        grad_query,
        grad_processed,
        grad_memory,
        grad_loc,
        grad_energy,
    ) = attention_backward(
        att_all,
        grad_dec_inputs,
        grad_out,
        gates,
        cells,
        bent,
        weights,
        window,
        loc_map,
        memory_flat,
        query_weight,
        energy_row,
        zone,
        resume_pair,
        valid_pair,
        next_resume,
        rows,
        positions,
        prenet_width,
        lag,
        (group_token,),
    )

    grad_processed = grad_processed.reshape(rows * positions, features)
    grad_memory = grad_memory + dot(grad_processed, memory_weight, 1, 1)
    g_memory_weight = dot(memory_flat, grad_processed, 0, 0)
    g_query_weight = dot(att_frames, grad_query, 0, 0)
    (grad_second,) = second_back(grad_prenet * keep_second)
    g_pre_second = dot(pre_hidden, grad_second, 0, 0)
    (grad_first,) = first_back(dot(grad_second, pre_second, 1, 1) * keep_first)
    g_pre_first = dot(frames_in, grad_first, 0, 0)
    filters, channels, taps = loc_filters.shape
    grad_joined = location_unmap(grad_loc, channels, taps, positions, features)
    late_grads = (
        g_pre_first,
        g_pre_second,
        g_att_bias,
        g_query_weight,
        g_memory_weight,
        grad_joined,
        jnp.sum(grad_energy, axis=0),
        g_dec_bias,
    )
    context_end = prenet_width + context_width
    dec_part = column_gradients(
        [att_inputs_all, dec_inputs_all],
        ((0, context_end, input_width), (0, prenet_width, context_end), (1, 0, units)),
        dec_columns,
        dec_sums,
    )
    late_joined = flat_join(late_grads, devices)
    if rings:
        late_ring = sum_section(late_joined.reshape((-1, 4) + late_joined.shape[1:]).swapaxes(0, 1))
        late_ring = late_ring + 0.0 * (dec_columns[0, 0, 0, 0] + group_sums[0, 0])
        att_columns, late_part = exchange_ring(att_sums, late_ring)
    else:
        att_columns = None
        late_part = part_sum(late_joined)
    att_part = column_gradients([att_inputs_all], ((0, 0, input_width),), att_columns, att_sums)

    late_sums = flat_split(flat_whole(late_part, devices), late_grads)
    grad_joined = late_sums[5].reshape(channels * taps, features)
    g_loc_filters = dot(loc_dense, grad_joined, 1, 1).reshape(loc_filters.shape)
    g_loc_dense = dot(loc_filters.reshape(filters, channels * taps), grad_joined)

    first_rows = kernel * mel
    mid_end = first_rows + post_mid.size // lanes
    proj_start = mid_end + first_rows
    proj_end = proj_start + out_frames.shape[1] // section_size
    mid_part = group_sums[first_rows:mid_end].reshape(post_mid.shape)
    own = lax.axis_index("section")
    shared = jnp.concatenate([group_sums[:first_rows], group_sums[mid_end:proj_end]], axis=0)
    shared_all = section_order(gather_section(shared), own)
    g_post_first = jnp.concatenate(
        [piece[:first_rows].reshape(kernel, mel, lanes) for piece in shared_all], axis=2
    )
    g_post_last = jnp.concatenate(
        [piece[first_rows : 2 * first_rows].reshape(kernel, mel, lanes) for piece in shared_all], axis=2
    ).swapaxes(1, 2)
    g_proj = jnp.concatenate([piece[2 * first_rows :] for piece in shared_all], axis=0)
    g_proj_bias = group_sums[proj_end, :mel]
    return (
        mel_after.reshape(frames, rows, mel).swapaxes(0, 1),
        stop_logit,
        grad_memory.reshape(memory.shape),
        late_sums[0],
        late_sums[1],
        att_part,
        late_sums[2].reshape(-1),
        late_sums[3],
        late_sums[4],
        g_loc_filters,
        g_loc_dense,
        late_sums[6],
        dec_part,
        late_sums[7],
        g_proj[:, :mel],
        g_proj_bias,
        g_proj[:, mel],
        g_post_first,
        mid_part,
        g_post_last,
        jnp.stack(gain_grads[:4]),
        jnp.stack(shift_grads[:4]),
        gain_grads[4],
        shift_grads[4],
    )


def solution(mesh):
    rows_only = P(both)
    columns_only = P(None, both)
    mid_spec = P(None, None, None, "section")
    placed = (
        (rows_only,) * 6
        + (P(), P(), columns_only)
        + (P(),) * 6
        + (columns_only,)
        + (P(),) * 5
        + (mid_spec,)
        + (P(),) * 5
        + (rows_only, rows_only)
    )
    given = (
        (rows_only,) * 3
        + (P(), P(), columns_only)
        + (P(),) * 6
        + (columns_only,)
        + (P(),) * 5
        + (mid_spec,)
        + (P(),) * 5
    )
    return jax.shard_map(per_device, mesh=mesh, in_specs=placed, out_specs=given, check_vma=False)
```
